32 devices in a mesh: wide: 16 (over z, y, core), narrow: 2 (over x).
Axes of the slice: x: 2, y: 2, z: 4, core: 2. Of those that a mesh axis runs over, the one named last changes fastest.
Arguments:
- tokens: bfloat16 [128, 128, 768], P(('wide', 'narrow')), may hold values from -6 to 6
- land_mask: int32 [128, 128], P(('wide', 'narrow')), may hold values from 0 to 1, as said below
- cotangent: bfloat16 [128, 128, 768], P(('wide', 'narrow')), may hold values from -6 to 6
- qkv_weight: bfloat16 [768, 2304], replicated, may hold values from -0.21875 to 0.21875
- query_bias: float32 [768], replicated, may hold values from -3 to 3
- value_bias: float32 [768], replicated, may hold values from -3 to 3
- proj_weight: bfloat16 [768, 768], replicated, may hold values from -0.625 to 0.625
- proj_bias: float32 [768], replicated, may hold values from -3 to 3
- up_weight: bfloat16 [768, 3072], replicated, may hold values from -0.21875 to 0.21875
- up_bias: float32 [3072], replicated, may hold values from -3 to 3
- down_weight: bfloat16 [3072, 768], replicated, may hold values from -0.109375 to 0.109375
- down_bias: float32 [768], replicated, may hold values from -3 to 3
- norm1_gain: float32 [768], replicated, may hold values from 0.1 to 1.9
- norm1_shift: float32 [768], replicated, may hold values from -2 to 2
- norm2_gain: float32 [768], replicated, may hold values from 0.1 to 1.9
- norm2_shift: float32 [768], replicated, may hold values from -2 to 2
Outputs:
- output: bfloat16 [128, 128, 768], P(('wide', 'narrow'))
- tokens_grad: float32 [128, 128, 768], P(('wide', 'narrow'))
- qkv_grad: float32 [768, 2304], P('wide', 'narrow')
- query_bias_grad: float32 [768], replicated
- value_bias_grad: float32 [768], replicated
- proj_grad: float32 [768, 768], P('wide', 'narrow')
- proj_bias_grad: float32 [768], replicated
- up_grad: float32 [768, 3072], P('wide', 'narrow')
- up_bias_grad: float32 [3072], replicated
- down_grad: float32 [3072, 768], P('wide', 'narrow')
- down_bias_grad: float32 [768], replicated
- norm1_gain_grad: float32 [768], replicated
- norm1_shift_grad: float32 [768], replicated
- norm2_gain_grad: float32 [768], replicated
- norm2_shift_grad: float32 [768], replicated
The draws below stay inside these ranges and needn't reach their ends.
Inputs may be any that keep to these rules, and one draw needn't show every extreme that they name: `land_mask`: every field holds at least one land patch; in every draw one field is all land and another holds a single land patch; which slots are land is random.
All inputs are finite; a program needn't handle non-finite values.
Results may differ from the reference program's by a relative error of at most 0.012.
Values sent between devices are 32-bit elements; how exact they have to be, the bound alone decides.
A program may use at most 192 MiB of HBM per device.

```python
import math
import jax
import jax.numpy as jnp
from jax import lax

D = 768
HEADS = 12
FF = 3072
PATCHES = 128
FIELDS = 128


def draw_land_mask(key, part):
    key = jax.random.fold_in(key, 7)
    subkeys = jax.random.split(key, 5)
    former = jax.random.randint(subkeys[0], (FIELDS,), 1, PATCHES + 1)
    latter = jax.random.randint(subkeys[1], (FIELDS,), 1, PATCHES + 1)
    counts = jnp.minimum(former, latter)
    full_field = jax.random.randint(subkeys[2], (), 0, FIELDS)
    offset = jax.random.randint(subkeys[3], (), 1, FIELDS)
    single_field = (full_field + offset) % FIELDS
    places = jnp.arange(FIELDS)
    counts = jnp.where(places == full_field, PATCHES, counts)
    counts = jnp.where(places == single_field, 1, counts)

    def shuffled(subkey):
        return jax.random.permutation(subkey, PATCHES)
    orders = jax.vmap(shuffled)(jax.random.split(subkeys[4], FIELDS))
    return (orders < counts[:, None]).astype(jnp.int32)


def block_levels(own_key, shape, shards, smallest, largest):
    loudness = 1.0
    for dim, blocks in shards:
        heights = jax.random.uniform(jax.random.fold_in(jax.random.fold_in(own_key, 6), dim), (blocks,), jnp.float32, smallest / len(shards), largest / len(shards))
        loudness = loudness * jnp.repeat(jnp.exp(heights), shape[dim] // blocks).reshape((-1,) + (1,) * (len(shape) - 1 - dim))
    return loudness


def bell_draw(own_key, extent, deviation, most, cuts=(), held_as=jnp.bfloat16):
    loudness = block_levels(own_key, extent, cuts, -0.22, 0.18) if cuts else 1.0
    drawn = jax.random.normal(own_key, extent, jnp.float32) * deviation * loudness
    return jnp.minimum(jnp.maximum(drawn, -most), most).astype(held_as)


def setup_inputs(seed: int = 0) -> dict:
    key_of = jax.random.split(jax.random.key(seed), 17)
    return {
        "tokens": bell_draw(key_of[0], (FIELDS, PATCHES, D), 1.0, 6.0, ((0, 32),)),
        "land_mask": draw_land_mask(jax.random.fold_in(key_of[16], 71), 0),
        "cotangent": bell_draw(key_of[2], (FIELDS, PATCHES, D), 1.0, 6.0, ((0, 32),)),
        "qkv_weight": bell_draw(key_of[3], (D, 3 * D), D ** -0.5, 0.21875),
        "query_bias": bell_draw(key_of[4], (D,), 0.5, 3.0, (), jnp.float32),
        "value_bias": bell_draw(key_of[5], (D,), 0.5, 3.0, (), jnp.float32),
        "proj_weight": bell_draw(key_of[6], (D, D), (D // 8) ** -0.5, 0.625),
        "proj_bias": bell_draw(key_of[7], (D,), 0.5, 3.0, (), jnp.float32),
        "up_weight": bell_draw(key_of[8], (D, FF), D ** -0.5, 0.21875),
        "up_bias": bell_draw(key_of[9], (FF,), 0.5, 3.0, (), jnp.float32),
        "down_weight": bell_draw(key_of[10], (FF, D), FF ** -0.5, 0.109375),
        "down_bias": bell_draw(key_of[11], (D,), 0.5, 3.0, (), jnp.float32),
        "norm1_gain": jnp.clip(1.0 + 0.18 * jax.random.normal(key_of[12], (D,), jnp.float32), 0.1, 1.9),
        "norm1_shift": bell_draw(key_of[13], (D,), 0.3, 2.0, (), jnp.float32),
        "norm2_gain": jnp.clip(1.0 + 0.18 * jax.random.normal(key_of[14], (D,), jnp.float32), 0.1, 1.9),
        "norm2_shift": bell_draw(key_of[15], (D,), 0.3, 2.0, (), jnp.float32),
    }


@jax.custom_vjp
def low(v):
    return lax.optimization_barrier(v.astype(jnp.bfloat16)).astype(jnp.float32)

@jax.custom_vjp
def low_back(v):
    return v

def low_keep(v):
    return (low(v), None)

def low_pass(kept, grad):
    return (grad,)

def back_keep(v):
    return (v, None)

def back_low(kept, grad):
    return (low(grad),)
low.defvjp(low_keep, low_pass)
low_back.defvjp(back_keep, back_low)
HIGHEST = lax.Precision.HIGHEST

def round_both(values):
    return low_back(low(values))

def layer_norm(inputs, norm_gain, norm_shift):
    average = lax.optimization_barrier(jnp.mean(inputs, -1, keepdims=True))
    centred = inputs - average
    variance = lax.optimization_barrier(jnp.mean(centred * centred, -1, keepdims=True))
    return centred * lax.rsqrt(variance + 1e-06) * norm_gain + norm_shift

def field_block(inputs, visible, params):
    qkv_weight, query_bias, value_bias, proj_weight, proj_bias, up_weight, up_bias, down_weight, down_bias, norm1_gain, norm1_shift, norm2_gain, norm2_shift = params
    groups, length, model_width = inputs.shape
    head_width = model_width // HEADS
    scaling = head_width ** (-0.5)
    normed_one = low(layer_norm(inputs, norm1_gain, norm1_shift))
    joint = jnp.einsum('gpd,de->gpe', normed_one, qkv_weight, precision=HIGHEST)
    queries = round_both(joint[..., :model_width] + query_bias).reshape(groups, length, HEADS, head_width)
    key_rows = round_both(joint[..., model_width:2 * model_width]).reshape(groups, length, HEADS, head_width)
    values = round_both(joint[..., 2 * model_width:] + value_bias).reshape(groups, length, HEADS, head_width)
    scores = low_back(jnp.einsum('gqhe,gkhe->ghqk', queries, key_rows, precision=HIGHEST) * scaling)
    scores = jnp.where(visible[:, None, None, :], scores, -1e+30)
    highest = lax.optimization_barrier(jnp.max(scores, -1, keepdims=True))
    exponent = jnp.exp(scores - highest)
    attention = exponent / lax.optimization_barrier(jnp.sum(exponent, -1, keepdims=True))
    attended = jnp.einsum('ghqk,gkhe->gqhe', low(attention), values, precision=HIGHEST)
    attended = round_both(attended.reshape(groups, length, model_width))
    branch = low_back(jnp.einsum('gpd,de->gpe', attended, proj_weight, precision=HIGHEST) + proj_bias)
    middle = inputs + branch
    normed_two = low(layer_norm(middle, norm2_gain, norm2_shift))
    hidden = low_back(jnp.einsum('gpd,dn->gpn', normed_two, up_weight, precision=HIGHEST) + up_bias)
    activated = low(jax.nn.gelu(hidden))
    return middle + jnp.einsum('gpn,nd->gpd', activated, down_weight, precision=HIGHEST) + down_bias

def reference(tokens, land_mask, cotangent, qkv_weight, query_bias, value_bias, proj_weight, proj_bias, up_weight, up_bias, down_weight, down_bias, norm1_gain, norm1_shift, norm2_gain, norm2_shift):
    visible = land_mask > 0
    params = tuple((array_in.astype(jnp.float32) for array_in in (qkv_weight, query_bias, value_bias, proj_weight, proj_bias, up_weight, up_bias, down_weight, down_bias, norm1_gain, norm1_shift, norm2_gain, norm2_shift)))
    group_size = math.gcd(FIELDS, 32)
    batches = FIELDS // group_size

    def forward(inputs, weights_in):
        packed = inputs.reshape(batches, group_size, PATCHES, D)
        masks = visible.reshape(batches, group_size, PATCHES)

        def group_step(pair_in):
            return jax.checkpoint(field_block)(pair_in[0], pair_in[1], weights_in)
        return lax.map(group_step, (packed, masks)).reshape(FIELDS, PATCHES, D)
    output, pull_back = jax.vjp(forward, tokens.astype(jnp.float32), params)
    tokens_grad, grads = pull_back(cotangent.astype(jnp.float32))
    return (output.astype(jnp.bfloat16), tokens_grad, grads[0], grads[1], grads[2], grads[3], grads[4], grads[5], grads[6], grads[7], grads[8], grads[9], grads[10], grads[11], grads[12])
```

```python
import jax
import jax.numpy as jnp
from jax import lax
from jax.experimental import pallas as pl
from jax.experimental.pallas import tpu as pltpu
from jax.sharding import PartitionSpec as P

HEADS = 12
F32 = jnp.float32
BF16 = jnp.bfloat16
SLOTS = 6


def dot(a, b):
    return lax.dot_general(a, b, (((1,), (0,)), ((), ())), preferred_element_type=F32)


def dot_nt(a, b):
    return lax.dot_general(a, b, (((1,), (1,)), ((), ())), preferred_element_type=F32)


def dot_tn(a, b):
    return lax.dot_general(a, b, (((0,), (0,)), ((), ())), preferred_element_type=F32)


def standardise(rows):
    centred = rows - jnp.mean(rows, -1, keepdims=True)
    scale = lax.rsqrt(jnp.mean(centred * centred, -1, keepdims=True) + 1e-06)
    return centred * scale, scale


def norm_back(unit_rows, scale, pulled):
    return scale * (
        pulled
        - jnp.mean(pulled, -1, keepdims=True)
        - unit_rows * jnp.mean(pulled * unit_rows, -1, keepdims=True)
    )


def column_sums(rows):
    return jnp.sum(rows, axis=0, keepdims=True)


def layer_kernel(wide, narrow, fields, patches, *refs):
    (
        tokens_in, cotangent_in, qkv_in, proj_in, up_in, down_in,
        land, query_bias, value_bias, proj_bias, up_bias, down_bias,
        gain_one, shift_one, gain_two, shift_two,
        output_out, tokens_out, qkv_out, proj_out, up_out, down_out, vec_out,
        tok, cot, n1, qkv, att, mid, n2, act_t, act, hgr, acc, ngr, left, w_a, w_b, w_p, qkv_bias,
        keep, core_in, in_0, in_1, in_2, in_3, vec, vec_in,
        load_sem, core_send, core_recv, core_free, stage_send, stage_recv, final_sem,
        vec_send, vec_recv, store_sem,
    ) = refs
    model = tok.shape[1]
    hidden_width = w_a.shape[1]
    stage_in = (in_0, in_1, in_2, in_3)
    at_wide = lax.axis_index("wide")
    at_narrow = lax.axis_index("narrow")
    width = model // narrow
    block_rows = model // wide
    group_rows = block_rows // 3
    chunk = width

    def my_bit(axis, level):
        index = at_wide if axis == "wide" else at_narrow
        return lax.rem(lax.div(index, 1 << level), 2)

    def partner(axis, level):
        shift = (1 << level) * (1 - 2 * my_bit(axis, level))
        if axis == "wide":
            return (at_wide + shift, at_narrow)
        return (at_wide, at_narrow + shift)

    wide_bits = [("wide", i) for i in range(1, wide.bit_length() - 1)]
    narrow_bits = [("narrow", i) for i in range(narrow.bit_length() - 1)]
    all_bits = [("wide", 0)] + wide_bits + narrow_bits
    stages = len(wide_bits) + len(narrow_bits)
    blocks = 1 << stages
    core = my_bit("wide", 0)
    mine = {bit: my_bit(*bit) for bit in all_bits}
    to = {bit: partner(*bit) for bit in all_bits}

    def order(unit, group):
        if group == 0:
            return narrow_bits + wide_bits
        if group == 1:
            return wide_bits[:1] + narrow_bits + wide_bits[1:]
        if unit % 2 == 0:
            return wide_bits[1:2] + narrow_bits + wide_bits[:1] + wide_bits[2:]
        return wide_bits[1:2] + wide_bits[:1] + narrow_bits + wide_bits[2:]

    def place(unit, group, row_block, column_block):
        found = 0
        for axis, level in order(unit, group):
            index = row_block if axis == "wide" else column_block
            found = 2 * found + ((index >> level) & 1)
        return found

    barrier = pltpu.get_barrier_semaphore()
    for bit in all_bits:
        pl.semaphore_signal(
            barrier, inc=1, device_id=to[bit], device_id_type=pl.DeviceIdType.MESH
        )

    def remote(src, dst, send, recv, bit):
        return pltpu.make_async_remote_copy(
            src_ref=src, dst_ref=dst, send_sem=send, recv_sem=recv,
            device_id=to[bit], device_id_type=pl.DeviceIdType.MESH,
        )

    def core_copy(unit):
        slot = unit % 2
        return remote(
            keep.at[SLOTS + slot], core_in.at[slot],
            core_send.at[slot], core_recv.at[slot], ("wide", 0),
        )

    def core_start(unit):
        if unit >= 2:
            pl.semaphore_wait(core_free, 1)
        core_copy(unit).start()

    def span(unit, group, stage):
        half = blocks >> (stage + 1)
        sequence = order(unit, group)
        base = 0
        for earlier in range(stage):
            base = base + mine[sequence[earlier]] * (blocks >> (earlier + 1))
        bit = sequence[stage]
        return half, base + mine[bit] * half, base + (1 - mine[bit]) * half, bit

    def stage_copy(unit, group, stage):
        half, own, other, bit = span(unit, group, stage)
        return remote(
            keep.at[unit % SLOTS, group, pl.ds(other, half)],
            stage_in[stage].at[unit, group],
            stage_send.at[unit, stage, group],
            stage_recv.at[unit, stage, group],
            bit,
        )

    def core_end(unit):
        slot = unit % 2
        core_copy(unit).wait()

        def step(block, carry):
            for group in range(3):
                keep[unit % SLOTS, group, block] += core_in[slot, group, block]
            return carry

        lax.fori_loop(0, blocks, step, 0)
        if unit + 2 < 12:
            pl.semaphore_signal(
                core_free, inc=1, device_id=to[("wide", 0)],
                device_id_type=pl.DeviceIdType.MESH,
            )
        for group in range(3):
            stage_copy(unit, group, 0).start()

    def final_copy(unit, group):
        half, own, other, bit = span(unit, group, stages - 1)
        ref, row, column = (
            (up_out, 0, unit * width),
            (down_out, (unit - 4) * block_rows, 0),
            (proj_out, 0, 0),
            (qkv_out, 0, (unit - 9) * width),
        )[0 if unit < 4 else 1 if unit < 8 else 2 if unit == 8 else 3]
        return pltpu.make_async_copy(
            keep.at[unit % SLOTS, group, own],
            ref.at[pl.ds(row + group * group_rows, group_rows), pl.ds(column, width)],
            final_sem.at[unit % SLOTS, group],
        )

    def stage_end(unit, stage):
        for group in range(3):
            stage_copy(unit, group, stage).wait()
            half, own, other, bit = span(unit, group, stage)
            keep[unit % SLOTS, group, pl.ds(own, half)] += stage_in[stage][unit, group]
            if stage + 1 < stages:
                stage_copy(unit, group, stage + 1).start()
            else:
                final_copy(unit, group).start()

    def final_wait(unit):
        for group in range(3):
            final_copy(unit, group).wait()

    def tick(number):
        for stage in reversed(range(stages)):
            unit = number - stage
            if 0 <= unit < 12:
                stage_end(unit, stage)

    def make_unit(unit, lhs_half, rhs):
        if unit >= SLOTS:
            final_wait(unit - SLOTS)
        kept, sent = unit % SLOTS, SLOTS + unit % 2
        index = [kept + core * (sent - kept), sent + core * (kept - sent)]
        half_blocks = wide // 2
        for half in range(2):
            product = dot(lhs_half(half), rhs())
            for row_block in range(half_blocks):
                for group in range(3):
                    top = row_block * block_rows + group * group_rows
                    for column_block in range(narrow):
                        where = place(unit, group, half * half_blocks + row_block, column_block)
                        keep[index[row_block % 2], group, where] = product[
                            top : top + group_rows,
                            column_block * width : (column_block + 1) * width,
                        ]
        core_start(unit)

    def load(src, dst, number):
        copy = pltpu.make_async_copy(src, dst, load_sem.at[number])
        copy.start()
        return copy

    tok_load = load(tokens_in, tok, 0)
    qkv_load = load(qkv_in, w_a.at[:, pl.ds(0, 3 * model)], 1)
    proj_load = load(proj_in, w_p, 2)
    cot_load = load(cotangent_in, cot, 3)
    down_load = load(down_in, w_b, 4)
    vec[...] = jnp.zeros_like(vec)
    qkv_bias[:, 0:model] = query_bias[...]
    qkv_bias[:, model : 2 * model] = jnp.zeros((1, model), F32)
    qkv_bias[:, 2 * model :] = value_bias[...]

    def field_rows(field):
        return pl.ds(pl.multiple_of(field * patches, patches), patches)

    def each_field(step):
        def body(field, carry):
            step(field)
            return carry

        lax.fori_loop(0, fields, body, 0)

    tok_load.wait()

    def norm_one(field):
        rows = field_rows(field)
        unit_rows, scale = standardise(tok[rows, :].astype(F32))
        n1[rows, :] = (unit_rows * gain_one[...] + shift_one[...]).astype(BF16)

    each_field(norm_one)
    qkv_load.wait()

    def project(tile, carry):
        columns = pl.ds(pl.multiple_of(tile * 256, 256), 256)
        qkv[:, columns] = (dot(n1[...], w_a[:, columns]) + qkv_bias[:, columns]).astype(BF16)
        return carry

    lax.fori_loop(0, 3 * model // 256, project, 0)
    up_load = load(up_in, w_a, 5)

    lane = lax.broadcasted_iota(jnp.int32, (1, 128), 1)
    head_masks = [(lane < 64).astype(BF16), (lane >= 64).astype(BF16)]
    lane_full = lax.broadcasted_iota(jnp.int32, (patches, 128), 1)
    pairs = model // 128

    def stack_heads(rows, factor=1.0):
        return jnp.concatenate([rows * (mask * BF16(factor)) for mask in head_masks], 0)

    def pick_heads(rows):
        return jnp.where(lane_full < 64, rows[:patches], rows[patches:])

    def soften(stacked, key_rows, visible):
        scores = jnp.where(visible, dot_nt(stacked, key_rows), -1e30)
        exponent = jnp.exp(scores - jnp.max(scores, -1, keepdims=True))
        return exponent * (1.0 / jnp.sum(exponent, -1, keepdims=True))

    def pair_columns(pair):
        return [pl.ds(part * model + pair * 128, 128) for part in range(3)]

    def visible_of(field):
        return jnp.broadcast_to(land[pl.ds(field, 1), :], (2 * patches, patches)) > 0

    def attend(field):
        rows = field_rows(field)
        visible = visible_of(field)
        for pair in range(pairs):
            at_q, at_k, at_v = pair_columns(pair)
            attention = soften(stack_heads(qkv[rows, at_q], 0.125), qkv[rows, at_k], visible)
            both = dot(attention.astype(BF16), qkv[rows, at_v])
            att[rows, pl.ds(pair * 128, 128)] = pick_heads(both).astype(BF16)

    each_field(attend)
    proj_load.wait()

    def residual(tile, carry):
        columns = pl.ds(pl.multiple_of(tile * 256, 256), 256)
        mid[:, columns] = (
            tok[:, columns].astype(F32) + dot(att[...], w_p[:, columns]) + proj_bias[:, columns]
        )
        return carry

    lax.fori_loop(0, model // 256, residual, 0)

    def norm_two(field):
        rows = field_rows(field)
        unit_rows, scale = standardise(mid[rows, :])
        normed = (unit_rows * gain_two[...] + shift_two[...]).astype(BF16)
        n2[rows, :] = normed
        left[:, rows] = normed.T

    each_field(norm_two)

    root = 0.7978845608028654

    def hidden_columns(part, column_block):
        return column_block * (hidden_width // narrow) + part * chunk

    def feed(part):
        for column_block in range(narrow):
            first = hidden_columns(part, column_block)
            columns = pl.ds(first, chunk)
            here = pl.ds(column_block * chunk, chunk)
            hidden = dot(n2[...], w_a[:, columns]) + up_bias[:, columns]
            pulled = dot_nt(cot[...], w_b[columns, :])
            square = hidden * hidden
            bent = jnp.tanh(hidden * (root + (root * 0.044715) * square))
            cdf = 0.5 + 0.5 * bent
            activated = (hidden * cdf).astype(BF16)
            slope = cdf + (hidden * (0.5 - 0.5 * bent * bent)) * (
                root + (3 * root * 0.044715) * square
            )
            grad = (pulled * slope).astype(BF16)
            act[:, here] = activated
            hgr[:, here] = grad
            act_t[columns, :] = activated.T
            vec[pl.ds(3 + first // model, 1), pl.ds(first % model, chunk)] = column_sums(
                grad.astype(F32)
            )

    def feed_sums(part):
        for column_block in range(narrow):
            columns = pl.ds(hidden_columns(part, column_block), chunk)
            here = pl.ds(column_block * chunk, chunk)
            for target, term in (
                (acc, lambda: dot(act[:, here], w_b[columns, :])),
                (ngr, lambda: dot_nt(hgr[:, here], w_a[:, columns])),
            ):
                if part == 0 and column_block == 0:
                    target[...] = term()
                else:
                    target[...] += term()

    def left_half(half):
        return left[pl.ds(half * (model // 2), model // 2), :]

    def up_unit(part):
        make_unit(part, left_half, lambda: hgr[...])

    def down_unit(part):
        def rows(half):
            return jnp.concatenate(
                [
                    act_t[pl.ds(block * 4 * block_rows + part * block_rows, block_rows), :]
                    for block in range(half * wide // 2, (half + 1) * wide // 2)
                ],
                0,
            )

        make_unit(4 + part, rows, lambda: cot[...])

    def store_output(field):
        rows = field_rows(field)
        act[rows, :] = (mid[rows, :] + acc[rows, :] + down_bias[...]).astype(BF16)

    output_copy = pltpu.make_async_copy(act, output_out, store_sem.at[0])
    tokens_copy = pltpu.make_async_copy(acc, tokens_out, store_sem.at[1])

    def add_sums(row, columns, rows):
        vec[pl.ds(row, 1), columns] += column_sums(rows)

    everything = pl.ds(0, model)

    def middle_back(field):
        rows = field_rows(field)
        unit_rows, scale = standardise(mid[rows, :])
        grads = ngr[rows, :]
        top = cot[rows, :].astype(F32)
        add_sums(7, everything, top)
        add_sums(10, everything, grads * unit_rows)
        add_sums(11, everything, grads)
        total = top + norm_back(unit_rows, scale, grads * gain_two[...])
        acc[rows, :] = total
        low = total.astype(BF16)
        hgr[rows, :] = low
        add_sums(2, everything, low.astype(F32))

    def attend_back(field):
        rows = field_rows(field)
        visible = visible_of(field)
        for pair in range(pairs):
            at_q, at_k, at_v = pair_columns(pair)
            key_rows, values = qkv[rows, at_k], qkv[rows, at_v]
            stacked = stack_heads(qkv[rows, at_q], 0.125)
            attention = soften(stacked, key_rows, visible)
            pulled = stack_heads(act[rows, pl.ds(pair * 128, 128)])
            values_grad = dot_tn(attention.astype(BF16), pulled).astype(BF16)
            inner = dot_nt(pulled, values)
            inner = inner - jnp.sum(attention * inner, -1, keepdims=True)
            scores_grad = (attention * inner).astype(BF16)
            queries_grad = (pick_heads(dot(scores_grad, key_rows)) * 0.125).astype(BF16)
            keys_grad = dot_tn(scores_grad, stacked).astype(BF16)
            qkv[rows, at_q] = queries_grad
            qkv[rows, at_k] = keys_grad
            qkv[rows, at_v] = values_grad
            here = pl.ds(pair * 128, 128)
            add_sums(0, here, queries_grad.astype(F32))
            add_sums(1, here, values_grad.astype(F32))

    def proj_unit():
        for field in range(fields):
            left[:, field_rows(field)] = att[field_rows(field), :].T
        make_unit(8, left_half, lambda: hgr[...])

    def qkv_unit(part):
        if part == 0:
            for field in range(fields):
                left[:, field_rows(field)] = n1[field_rows(field), :].T
        stride = 3 * model // narrow
        make_unit(
            9 + part,
            left_half,
            lambda: jnp.concatenate(
                [
                    qkv[:, pl.ds(block * stride + part * width, width)]
                    for block in range(narrow)
                ],
                1,
            ),
        )

    def source_back(field):
        rows = field_rows(field)
        unit_rows, scale = standardise(tok[rows, :].astype(F32))
        grads = ngr[rows, :]
        add_sums(8, everything, grads * unit_rows)
        add_sums(9, everything, grads)
        acc[rows, :] += norm_back(unit_rows, scale, grads * gain_one[...])

    def vec_copy(number):
        return remote(
            vec, vec_in.at[number], vec_send.at[number], vec_recv.at[number], all_bits[number]
        )

    def vec_end(number):
        vec_copy(number).wait()
        vec[...] += vec_in[number]
        if number + 1 < len(all_bits):
            vec_copy(number + 1).start()

    up_load.wait()
    down_load.wait()
    cot_load.wait()
    feed(0)
    pl.semaphore_wait(barrier, len(all_bits))
    up_unit(0)
    feed_sums(0)
    core_end(0)
    feed(1)
    up_unit(1)
    feed_sums(1)
    core_end(1)

    feed(2)
    up_unit(2)
    feed_sums(2)
    tick(0)
    core_end(2)

    feed(3)
    up_unit(3)
    feed_sums(3)
    tick(1)
    core_end(3)

    qkv_again = load(qkv_in, w_a.at[:, pl.ds(0, 3 * model)], 1)
    down_unit(0)
    each_field(store_output)
    output_copy.start()
    each_field(middle_back)
    tick(2)
    core_end(4)

    down_unit(1)
    output_copy.wait()
    act[...] = dot_nt(hgr[...], w_p[...]).astype(BF16)
    attend_back(0)
    tick(3)
    core_end(5)

    down_unit(2)
    lax.fori_loop(1, fields - 1, lambda field, carry: (attend_back(field), carry)[1], 0)
    tick(4)
    core_end(6)

    down_unit(3)
    attend_back(fields - 1)
    tick(5)
    core_end(7)

    proj_unit()
    tick(6)
    core_end(8)

    qkv_unit(0)
    qkv_again.wait()
    ngr[...] = dot_nt(qkv[...], w_a[:, pl.ds(0, 3 * model)])
    tick(7)
    core_end(9)

    qkv_unit(1)
    each_field(source_back)
    tokens_copy.start()
    vec_copy(0).start()
    tick(8)
    core_end(10)

    qkv_unit(2)
    tick(9)
    core_end(11)

    left_over = list(range(len(all_bits)))
    for number in range(10, 12 + stages):
        if left_over:
            vec_end(left_over.pop(0))
        tick(number)
    while left_over:
        vec_end(left_over.pop(0))
    vec_store = pltpu.make_async_copy(vec, vec_out, store_sem.at[2])
    vec_store.start()
    tokens_copy.wait()
    for unit in range(12 - SLOTS, 12):
        final_wait(unit)
    vec_store.wait()


def local_fused(wide, narrow, *args):
    (
        tokens, land_mask, cotangent, qkv_weight, query_bias, value_bias, proj_weight, proj_bias,
        up_weight, up_bias, down_weight, down_bias, norm1_gain, norm1_shift, norm2_gain, norm2_shift,
    ) = args
    fields, patches, model = tokens.shape
    rows = fields * patches
    hidden_width = up_weight.shape[1]
    width, block_rows = model // narrow, model // wide
    bits = (wide * narrow).bit_length() - 1
    blocks = wide * narrow // 2
    group_rows = block_rows // 3
    anywhere = pl.BlockSpec(memory_space=pl.ANY)
    in_vmem = pl.BlockSpec(memory_space=pltpu.VMEM)

    def vmem(shape, dtype=F32):
        return pltpu.VMEM(shape, dtype)

    dma = pltpu.SemaphoreType.DMA
    results = pl.pallas_call(
        lambda *refs: layer_kernel(wide, narrow, fields, patches, *refs),
        out_shape=[
            jax.ShapeDtypeStruct((rows, model), BF16),
            jax.ShapeDtypeStruct((rows, model), F32),
            jax.ShapeDtypeStruct((block_rows, 3 * width), F32),
            jax.ShapeDtypeStruct((block_rows, width), F32),
            jax.ShapeDtypeStruct((block_rows, 4 * width), F32),
            jax.ShapeDtypeStruct((4 * block_rows, width), F32),
            jax.ShapeDtypeStruct((16, model), F32),
        ],
        in_specs=[anywhere] * 6 + [in_vmem] * 10,
        out_specs=[anywhere] * 7,
        scratch_shapes=[
            vmem((rows, model), BF16),
            vmem((rows, model), BF16),
            vmem((rows, model), BF16),
            vmem((rows, 3 * model), BF16),
            vmem((rows, model), BF16),
            vmem((rows, model)),
            vmem((rows, model), BF16),
            vmem((hidden_width, rows), BF16),
            vmem((rows, model), BF16),
            vmem((rows, model), BF16),
            vmem((rows, model)),
            vmem((rows, model)),
            vmem((model, rows), BF16),
            vmem((model, hidden_width), BF16),
            vmem((hidden_width, model), BF16),
            vmem((model, model), BF16),
            vmem((1, 3 * model)),
            vmem((SLOTS + 2, 3, blocks, group_rows, width)),
            vmem((2, 3, blocks, group_rows, width)),
            *[vmem((12, 3, blocks >> (s + 1), group_rows, width)) for s in range(4)],
            vmem((16, model)),
            vmem((bits, 16, model)),
            dma((6,)),
            dma((2,)),
            dma((2,)),
            pltpu.SemaphoreType.REGULAR,
            dma((12, bits - 1, 3)),
            dma((12, bits - 1, 3)),
            dma((SLOTS, 3)),
            dma((bits,)),
            dma((bits,)),
            dma((3,)),
        ],
        compiler_params=pltpu.CompilerParams(
            collective_id=0, has_side_effects=True, vmem_limit_bytes=63 << 20
        ),
        name="encoder_layer",
    )(
        tokens.reshape(rows, model),
        cotangent.reshape(rows, model),
        qkv_weight,
        proj_weight,
        up_weight,
        down_weight,
        land_mask,
        query_bias.reshape(1, -1),
        value_bias.reshape(1, -1),
        proj_bias.reshape(1, -1),
        up_bias.reshape(1, -1),
        down_bias.reshape(1, -1),
        norm1_gain.reshape(1, -1),
        norm1_shift.reshape(1, -1),
        norm2_gain.reshape(1, -1),
        norm2_shift.reshape(1, -1),
    )
    output, tokens_grad, qkv_grad, proj_grad, up_grad, down_grad, vectors = results
    return (
        output.reshape(tokens.shape),
        tokens_grad.reshape(tokens.shape),
        qkv_grad,
        vectors[0],
        vectors[1],
        proj_grad,
        vectors[2],
        up_grad,
        vectors[3:7].reshape(-1),
        down_grad,
        vectors[7],
        vectors[8],
        vectors[9],
        vectors[10],
        vectors[11],
    )


def layer_norm(inputs, norm_gain, norm_shift):
    average = jnp.mean(inputs, -1, keepdims=True)
    centred = inputs - average
    variance = jnp.mean(centred * centred, -1, keepdims=True)
    return centred * lax.rsqrt(variance + 1e-06) * norm_gain + norm_shift


def attend_scores(queries, key_rows, visible, scaling):
    scores = (
        jnp.einsum("fqhe,fkhe->fhqk", queries, key_rows, preferred_element_type=jnp.float32)
        * scaling
    )
    return jnp.where(visible[:, None, None, :], scores, -1e30)


def share_sums(former, latter):
    row_sums = (
        lax.psum_scatter(former, "wide", scatter_dimension=0, tiled=True),
        lax.psum_scatter(latter, "wide", scatter_dimension=0, tiled=True),
    )
    return (
        lax.psum_scatter(row_sums[0], "narrow", scatter_dimension=1, tiled=True),
        lax.psum_scatter(row_sums[1], "narrow", scatter_dimension=1, tiled=True),
    )


def local(
    tokens,
    land_mask,
    cotangent,
    qkv_weight,
    query_bias,
    value_bias,
    proj_weight,
    proj_bias,
    up_weight,
    up_bias,
    down_weight,
    down_bias,
    norm1_gain,
    norm1_shift,
    norm2_gain,
    norm2_shift,
):
    field_count, length, model_width = tokens.shape
    head_count = HEADS
    head_width = model_width // head_count
    scaling = head_width ** (-0.5)
    visible = land_mask > 0
    split_shape = (field_count, length, head_count, head_width)
    source = tokens.astype(jnp.float32)
    normed_one = layer_norm(source, norm1_gain, norm1_shift).astype(jnp.bfloat16)
    joint = jnp.einsum("fpd,de->fpe", normed_one, qkv_weight, preferred_element_type=jnp.float32)
    queries = (joint[..., :model_width] + query_bias).astype(jnp.bfloat16).reshape(split_shape)
    key_rows = joint[..., model_width : 2 * model_width].astype(jnp.bfloat16).reshape(split_shape)
    values = (joint[..., 2 * model_width :] + value_bias).astype(jnp.bfloat16).reshape(split_shape)
    scores = attend_scores(queries, key_rows, visible, scaling)
    highest = jnp.max(scores, -1, keepdims=True)
    exponent = jnp.exp(scores - highest)
    summed = jnp.sum(exponent, -1, keepdims=True)
    attention = exponent / summed
    log_total = highest + jnp.log(summed)
    attended = jnp.einsum(
        "fhqk,fkhe->fqhe",
        attention.astype(jnp.bfloat16),
        values,
        preferred_element_type=jnp.float32,
    )
    attended = attended.reshape(field_count, length, model_width).astype(jnp.bfloat16)
    middle = (
        source
        + jnp.einsum("fpd,de->fpe", attended, proj_weight, preferred_element_type=jnp.float32)
        + proj_bias
    )
    normed_two = layer_norm(middle, norm2_gain, norm2_shift).astype(jnp.bfloat16)
    hidden = (
        jnp.einsum("fpd,dn->fpn", normed_two, up_weight, preferred_element_type=jnp.float32)
        + up_bias
    )
    activated_full, gelu_pull = jax.vjp(jax.nn.gelu, hidden)
    activated = activated_full.astype(jnp.bfloat16)
    output = (
        middle
        + jnp.einsum("fpn,nd->fpd", activated, down_weight, preferred_element_type=jnp.float32)
        + down_bias
    )
    grad_out = cotangent.astype(jnp.float32)
    down_local = jnp.einsum("fpn,fpd->nd", activated, cotangent, preferred_element_type=jnp.float32)
    down_bias_local = jnp.sum(grad_out, axis=(0, 1))
    activated_grad = jnp.einsum(
        "fpd,nd->fpn", cotangent, down_weight, preferred_element_type=jnp.float32
    )
    hidden_grad = gelu_pull(activated_grad)[0].astype(jnp.bfloat16)
    up_local = jnp.einsum(
        "fpd,fpn->dn", normed_two, hidden_grad, preferred_element_type=jnp.float32
    )
    up_bias_local = jnp.sum(hidden_grad.astype(jnp.float32), axis=(0, 1))
    feed_sums = share_sums(up_local, down_local)
    normed_two_grad = jnp.einsum(
        "fpn,dn->fpd", hidden_grad, up_weight, preferred_element_type=jnp.float32
    )
    unused_two, norm_two_pull = jax.vjp(layer_norm, middle, norm2_gain, norm2_shift)
    middle_part, gain_two_local, shift_two_local = norm_two_pull(normed_two_grad)
    middle_grad = grad_out + middle_part
    middle_low = middle_grad.astype(jnp.bfloat16)
    proj_local = jnp.einsum("fpd,fpe->de", attended, middle_low, preferred_element_type=jnp.float32)
    proj_bias_local = jnp.sum(middle_low.astype(jnp.float32), axis=(0, 1))
    attended_grad = jnp.einsum(
        "fpe,de->fpd", middle_low, proj_weight, preferred_element_type=jnp.float32
    )
    attended_grad = attended_grad.astype(jnp.bfloat16).reshape(split_shape)
    scores = attend_scores(queries, key_rows, visible, scaling)
    attention = jnp.exp(scores - log_total)
    values_grad = jnp.einsum(
        "fhqk,fqhe->fkhe",
        attention.astype(jnp.bfloat16),
        attended_grad,
        preferred_element_type=jnp.float32,
    )
    attention_grad = jnp.einsum(
        "fqhe,fkhe->fhqk", attended_grad, values, preferred_element_type=jnp.float32
    )
    inner_sum = jnp.sum(attention * attention_grad, -1, keepdims=True)
    scores_grad = (attention * (attention_grad - inner_sum)).astype(jnp.bfloat16)
    queries_grad = (
        jnp.einsum("fhqk,fkhe->fqhe", scores_grad, key_rows, preferred_element_type=jnp.float32)
        * scaling
    )
    keys_grad = (
        jnp.einsum("fhqk,fqhe->fkhe", scores_grad, queries, preferred_element_type=jnp.float32)
        * scaling
    )
    flat_shape = (field_count, length, model_width)
    joint_grad = jnp.concatenate(
        [
            queries_grad.reshape(flat_shape),
            keys_grad.reshape(flat_shape),
            values_grad.reshape(flat_shape),
        ],
        -1,
    ).astype(jnp.bfloat16)
    qkv_local = jnp.einsum(
        "fpd,fpe->de", normed_one, joint_grad, preferred_element_type=jnp.float32
    )
    joint_sums = jnp.sum(joint_grad.astype(jnp.float32), axis=(0, 1))
    query_bias_local = joint_sums[:model_width]
    value_bias_local = joint_sums[2 * model_width :]
    attention_sums = share_sums(qkv_local, proj_local)
    normed_one_grad = jnp.einsum(
        "fpe,de->fpd", joint_grad, qkv_weight, preferred_element_type=jnp.float32
    )
    unused_one, norm_one_pull = jax.vjp(layer_norm, source, norm1_gain, norm1_shift)
    source_part, gain_one_local, shift_one_local = norm_one_pull(normed_one_grad)
    tokens_grad = middle_grad + source_part
    vectors = lax.psum(
        (
            query_bias_local,
            value_bias_local,
            proj_bias_local,
            up_bias_local,
            down_bias_local,
            gain_one_local,
            shift_one_local,
            gain_two_local,
            shift_two_local,
        ),
        ("wide", "narrow"),
    )
    return (
        output.astype(jnp.bfloat16),
        tokens_grad,
        attention_sums[0],
        vectors[0],
        vectors[1],
        attention_sums[1],
        vectors[2],
        feed_sums[0],
        vectors[3],
        feed_sums[1],
        vectors[4],
        vectors[5],
        vectors[6],
        vectors[7],
        vectors[8],
    )


def solution(mesh):
    wide, narrow = mesh.shape["wide"], mesh.shape["narrow"]
    placed = (
        P(("wide", "narrow"), None, None),
        P(("wide", "narrow"), None),
        P(("wide", "narrow"), None, None),
        P(),
        P(),
        P(),
        P(),
        P(),
        P(),
        P(),
        P(),
        P(),
        P(),
        P(),
        P(),
        P(),
    )
    fused = (wide, narrow) == (16, 2)

    def layer(*args):
        return local_fused(wide, narrow, *args) if fused else local(*args)

    return jax.shard_map(
        layer,
        mesh=mesh,
        in_specs=placed,
        out_specs=(
            P(("wide", "narrow"), None, None),
            P(("wide", "narrow"), None, None),
            P("wide", "narrow"),
            P(),
            P(),
            P("wide", "narrow"),
            P(),
            P("wide", "narrow"),
            P(),
            P("wide", "narrow"),
            P(),
            P(),
            P(),
            P(),
            P(),
        ),
        check_vma=False,
    )
```

```python
import jax
import jax.numpy as jnp
from jax import lax
from jax.experimental import pallas as pl
from jax.experimental.pallas import tpu as pltpu
from jax.sharding import PartitionSpec as P

HEADS = 12
F32 = jnp.float32
BF16 = jnp.bfloat16
SLOTS = 6
LAGS = (0, 2, 4, 6)
LEAD = 3


def dot(a, b):
    return lax.dot_general(a, b, (((1,), (0,)), ((), ())), preferred_element_type=F32)


def dot_nt(a, b):
    return lax.dot_general(a, b, (((1,), (1,)), ((), ())), preferred_element_type=F32)


def dot_tn(a, b):
    return lax.dot_general(a, b, (((0,), (0,)), ((), ())), preferred_element_type=F32)


def standardise(rows):
    centred = rows - jnp.mean(rows, -1, keepdims=True)
    scale = lax.rsqrt(jnp.mean(centred * centred, -1, keepdims=True) + 1e-06)
    return centred * scale, scale


def norm_back(unit_rows, scale, pulled):
    return scale * (
        pulled
        - jnp.mean(pulled, -1, keepdims=True)
        - unit_rows * jnp.mean(pulled * unit_rows, -1, keepdims=True)
    )


def column_sums(rows):
    return jnp.sum(rows, axis=0, keepdims=True)


def layer_kernel(wide, narrow, fields, patches, *refs):
    (
        tokens_in, cotangent_in, qkv_in, proj_in, up_in, down_in, land_in,
    ) = refs[:7]
    vectors_in, refs = refs[7:16], refs[16:]
    (
        output_out, tokens_out, qkv_out, proj_out, up_out, down_out, vec_out,
        tok, cot, n1, qkv, att, mid, n2, act_t, acts, hgrs, acc, ngr, left, w_a, w_b, w_p, qkv_bias, flat,
        keep, core_in, up_sum, down_sum, proj_sum, qkv_sum, in_0, in_1, in_2, in_3, vec, vec_in,
        load_sem, core_send, core_recv, core_free, stage_send, stage_recv, final_sem,
        vec_send, vec_recv, store_sem, land,
    ) = refs[:-9]
    vectors_held = refs[-9:]
    (
        query_bias, value_bias, proj_bias, up_bias, down_bias,
        gain_one, shift_one, gain_two, shift_two,
    ) = vectors_held
    model = tok.shape[1]
    hidden_width = w_a.shape[1]
    stage_in = (in_0, in_1, in_2, in_3)
    act, hgr = acts.at[0], hgrs.at[0]
    at_wide = lax.axis_index("wide")
    at_narrow = lax.axis_index("narrow")
    width = model // narrow
    block_rows = model // wide
    group_rows = block_rows // 3
    chunk = width
    parts = 36

    def my_bit(axis, level):
        index = at_wide if axis == "wide" else at_narrow
        return lax.rem(lax.div(index, 1 << level), 2)

    def partner(axis, level):
        shift = (1 << level) * (1 - 2 * my_bit(axis, level))
        if axis == "wide":
            return (at_wide + shift, at_narrow)
        return (at_wide, at_narrow + shift)

    wide_bits = [("wide", i) for i in range(1, wide.bit_length() - 1)]
    narrow_bits = [("narrow", i) for i in range(narrow.bit_length() - 1)]
    all_bits = [("wide", 0)] + wide_bits + narrow_bits
    stages = len(wide_bits) + len(narrow_bits)
    blocks = 1 << stages
    core = my_bit("wide", 0)
    mine = {bit: my_bit(*bit) for bit in all_bits}
    to = {bit: partner(*bit) for bit in all_bits}

    def order(part, group):
        if group == 0:
            return narrow_bits + wide_bits
        if group == 1:
            return wide_bits[:1] + narrow_bits + wide_bits[1:]
        if part % 2 == 0:
            return wide_bits[1:2] + narrow_bits + wide_bits[:1] + wide_bits[2:]
        return wide_bits[1:2] + wide_bits[:1] + narrow_bits + wide_bits[2:]

    def place(part, group, row_block, column_block):
        found = 0
        for axis, level in order(part, group):
            index = row_block if axis == "wide" else column_block
            found = 2 * found + ((index >> level) & 1)
        return found

    barrier = pltpu.get_barrier_semaphore()
    for bit in all_bits:
        pl.semaphore_signal(
            barrier, inc=1, device_id=to[bit], device_id_type=pl.DeviceIdType.MESH
        )

    def remote(src, dst, send, recv, bit):
        return pltpu.make_async_remote_copy(
            src_ref=src, dst_ref=dst, send_sem=send, recv_sem=recv,
            device_id=to[bit], device_id_type=pl.DeviceIdType.MESH,
        )

    def kept_slot(part):
        return part % (3 * SLOTS)

    def sent_slot(part):
        return 3 * SLOTS + part % 6

    def core_copy(part):
        slot = part % 6
        return remote(
            keep.at[sent_slot(part)], core_in.at[slot],
            core_send.at[slot], core_recv.at[slot], ("wide", 0),
        )

    def core_start(part):
        if part >= 6:
            pl.semaphore_wait(core_free, 1)
        core_copy(part).start()

    def span(part, group, stage):
        half = blocks >> (stage + 1)
        sequence = order(part, group)
        base = 0
        for earlier in range(stage):
            base = base + mine[sequence[earlier]] * (blocks >> (earlier + 1))
        bit = sequence[stage]
        return half, base + mine[bit] * half, base + (1 - mine[bit]) * half, bit

    gaps = [LEAD] + [LAGS[i] - LAGS[i - 1] for i in range(1, 4)]
    cycle = [2 * (gap + gap % 2) for gap in gaps]

    def stage_copy(part, group, stage):
        half, own, other, bit = span(part, group, stage)
        sent = sum(gaps[:stage]) + part % gaps[stage]
        held = sum(cycle[:stage]) + part % cycle[stage]
        return remote(
            keep.at[kept_slot(part), group, pl.ds(other, half)],
            stage_in[stage].at[part % cycle[stage], group],
            stage_send.at[sent, group],
            stage_recv.at[held, group],
            bit,
        )

    def core_end(part):
        slot = part % 6
        core_copy(part).wait()
        keep[kept_slot(part)] += core_in[slot]
        if part + 6 < parts:
            pl.semaphore_signal(
                core_free, inc=1, device_id=to[("wide", 0)],
                device_id_type=pl.DeviceIdType.MESH,
            )
        for group in range(3):
            stage_copy(part, group, 0).start()

    def result_place(part, group):
        unit, row = part // 3, (part % 3) * group_rows
        if unit < 4:
            return up_sum, row, unit * width + group * 128
        if unit < 8:
            return down_sum, (unit - 4) * block_rows + row, group * 128
        if unit == 8:
            return proj_sum, row, group * 128
        return qkv_sum, row, (unit - 9) * width + group * 128

    def stage_end(part, stage):
        for group in range(3):
            stage_copy(part, group, stage).wait()
            half, own, other, bit = span(part, group, stage)
            slot, came = kept_slot(part), stage_in[stage].at[part % cycle[stage], group]
            if stage + 1 < stages:
                keep[slot, group, pl.ds(own, half)] += came[...]
                stage_copy(part, group, stage + 1).start()
            else:
                ref, row, column = result_place(part, group)
                ref[row : row + group_rows, column : column + 128] = (
                    keep[slot, group, own] + came[0]
                )

    result_copies = [
        pltpu.make_async_copy(src, dst, final_sem.at[number])
        for number, (src, dst) in enumerate(
            ((up_sum, up_out), (down_sum, down_out), (proj_sum, proj_out), (qkv_sum, qkv_out))
        )
    ]
    last_part = {11: 0, 23: 1, 26: 2, 35: 3}

    def tick(number):
        for stage in reversed(range(stages)):
            part = number - LAGS[stage]
            if 0 <= part < parts:
                stage_end(part, stage)
                if stage + 1 == stages and part in last_part:
                    result_copies[last_part[part]].start()

    def make_unit(unit, lhs_half, rhs):
        half_blocks = wide // 2
        for half in range(2):
            product = dot(lhs_half(half), rhs())
            for third in range(3):
                part = 3 * unit + third
                kept, sent = kept_slot(part), sent_slot(part)
                index = [kept + core * (sent - kept), sent + core * (kept - sent)]
                for row_block in range(half_blocks):
                    top = row_block * block_rows + third * group_rows
                    for column_block in range(narrow):
                        for group in range(3):
                            where = place(
                                part, group, half * half_blocks + row_block, column_block
                            )
                            side = column_block * width + group * 128
                            keep[index[row_block % 2], group, where] = product[
                                top : top + group_rows, side : side + 128
                            ]
        for third in range(3):
            core_start(3 * unit + third)

    def row_of(vector):
        return vector[...].reshape(1, vector.shape[0])

    def load(src, dst, number):
        copy = pltpu.make_async_copy(src, dst, load_sem.at[number])
        copy.start()
        return copy

    tok_load = load(tokens_in, tok, 0)
    qkv_load = load(qkv_in, w_a.at[:, pl.ds(0, 3 * model)], 1)
    small_loads = [load(land_in, land, 6)] + [
        load(src, dst, 7 + number)
        for number, (src, dst) in enumerate(zip(vectors_in, vectors_held))
    ]
    vec[...] = jnp.zeros_like(vec)
    for small in small_loads:
        small.wait()
    qkv_bias[:, 0:model] = row_of(query_bias)
    qkv_bias[:, model : 2 * model] = jnp.zeros((1, model), F32)
    qkv_bias[:, 2 * model :] = row_of(value_bias)
    for number, vector in enumerate(
        (proj_bias, down_bias, gain_one, shift_one, gain_two, shift_two)
    ):
        flat[number : number + 1, 0:model] = row_of(vector)
    flat[6:7, :] = row_of(up_bias)

    def field_rows(field):
        return pl.ds(pl.multiple_of(field * patches, patches), patches)

    def each_field(step):
        def body(field, carry):
            step(field)
            return carry

        lax.fori_loop(0, fields, body, 0)

    tok_load.wait()
    at_model = pl.ds(0, model)
    proj_row, down_row, gain_one_row, shift_one_row, gain_two_row, shift_two_row = (
        flat.at[pl.ds(number, 1), at_model] for number in range(6)
    )
    up_row = flat.at[pl.ds(6, 1), :]

    def norm_one(field):
        rows = field_rows(field)
        unit_rows, scale = standardise(tok[rows, :].astype(F32))
        n1[rows, :] = (unit_rows * gain_one_row[...] + shift_one_row[...]).astype(BF16)

    each_field(norm_one)
    qkv_load.wait()
    proj_load = load(proj_in, w_p, 2)
    cot_load = load(cotangent_in, cot, 3)
    down_load = load(down_in, w_b, 4)

    def project(tile, carry):
        columns = pl.ds(pl.multiple_of(tile * 256, 256), 256)
        qkv[:, columns] = (dot(n1[...], w_a[:, columns]) + qkv_bias[:, columns]).astype(BF16)
        return carry

    lax.fori_loop(0, 3 * model // 256, project, 0)
    up_load = load(up_in, w_a, 5)

    lane = lax.broadcasted_iota(jnp.int32, (1, 128), 1)
    head_masks = [(lane < 64).astype(BF16), (lane >= 64).astype(BF16)]
    lane_full = lax.broadcasted_iota(jnp.int32, (patches, 128), 1)
    pairs = model // 128

    def stack_heads(rows, factor=1.0):
        return jnp.concatenate([rows * (mask * BF16(factor)) for mask in head_masks], 0)

    def pick_heads(rows):
        return jnp.where(lane_full < 64, rows[:patches], rows[patches:])

    def soften(stacked, key_rows, visible):
        scores = jnp.where(visible, dot_nt(stacked, key_rows), -1e30)
        exponent = jnp.exp(scores - jnp.max(scores, -1, keepdims=True))
        return exponent * (1.0 / jnp.sum(exponent, -1, keepdims=True))

    def pair_columns(pair):
        return [pl.ds(part * model + pair * 128, 128) for part in range(3)]

    def visible_of(field):
        return jnp.broadcast_to(land[pl.ds(field, 1), :], (2 * patches, patches)) > 0

    def attend(field):
        rows = field_rows(field)
        visible = visible_of(field)
        for pair in range(pairs):
            at_q, at_k, at_v = pair_columns(pair)
            attention = soften(stack_heads(qkv[rows, at_q], 0.125), qkv[rows, at_k], visible)
            both = dot(attention.astype(BF16), qkv[rows, at_v])
            att[rows, pl.ds(pair * 128, 128)] = pick_heads(both).astype(BF16)

    each_field(attend)
    proj_load.wait()

    def residual(tile, carry):
        columns = pl.ds(pl.multiple_of(tile * 256, 256), 256)
        mid[:, columns] = (
            tok[:, columns].astype(F32) + dot(att[...], w_p[:, columns]) + proj_row[:, columns]
        )
        return carry

    lax.fori_loop(0, model // 256, residual, 0)

    def norm_two(field):
        rows = field_rows(field)
        unit_rows, scale = standardise(mid[rows, :])
        normed = (unit_rows * gain_two_row[...] + shift_two_row[...]).astype(BF16)
        n2[rows, :] = normed
        left[:, rows] = normed.T

    each_field(norm_two)

    root = 0.7978845608028654

    def hidden_columns(part, column_block):
        return column_block * (hidden_width // narrow) + part * chunk

    def feed(part):
        for column_block in range(narrow):
            first = hidden_columns(part, column_block)
            columns = pl.ds(first, chunk)
            here = pl.ds(column_block * chunk, chunk)
            hidden = dot(n2[...], w_a[:, columns]) + up_row[:, columns]
            pulled = dot_nt(cot[...], w_b[columns, :])
            square = hidden * hidden
            bent = jnp.tanh(hidden * (root + (root * 0.044715) * square))
            cdf = 0.5 + 0.5 * bent
            activated = (hidden * cdf).astype(BF16)
            slope = cdf + (hidden * (0.5 - 0.5 * bent * bent)) * (
                root + (3 * root * 0.044715) * square
            )
            grad = (pulled * slope).astype(BF16)
            acts[part, :, here] = activated
            hgrs[part, :, here] = grad
            act_t[columns, :] = activated.T
            vec[pl.ds(3 + first // model, 1), pl.ds(first % model, chunk)] = column_sums(
                grad.astype(F32)
            )

    def feed_sums(part):
        for column_block in range(narrow):
            columns = pl.ds(hidden_columns(part, column_block), chunk)
            here = pl.ds(column_block * chunk, chunk)
            for target, term in (
                (acc, lambda: dot(acts[part, :, here], w_b[columns, :])),
                (ngr, lambda: dot_nt(hgrs[part, :, here], w_a[:, columns])),
            ):
                if part == 0 and column_block == 0:
                    target[...] = term()
                else:
                    target[...] += term()

    def left_half(half):
        return left[pl.ds(half * (model // 2), model // 2), :]

    def up_unit(part):
        make_unit(part, left_half, lambda: hgrs[part])

    def down_unit(part):
        def rows(half):
            return jnp.concatenate(
                [
                    act_t[pl.ds(block * 4 * block_rows + part * block_rows, block_rows), :]
                    for block in range(half * wide // 2, (half + 1) * wide // 2)
                ],
                0,
            )

        make_unit(4 + part, rows, lambda: cot[...])

    def store_output(field):
        rows = field_rows(field)
        act[rows, :] = (mid[rows, :] + acc[rows, :] + down_row[...]).astype(BF16)

    output_copy = pltpu.make_async_copy(act, output_out, store_sem.at[0])
    tokens_copy = pltpu.make_async_copy(acc, tokens_out, store_sem.at[1])

    def add_sums(row, columns, rows):
        vec[pl.ds(row, 1), columns] += column_sums(rows)

    everything = pl.ds(0, model)

    def middle_back(field):
        rows = field_rows(field)
        unit_rows, scale = standardise(mid[rows, :])
        grads = ngr[rows, :]
        top = cot[rows, :].astype(F32)
        add_sums(7, everything, top)
        add_sums(10, everything, grads * unit_rows)
        add_sums(11, everything, grads)
        total = top + norm_back(unit_rows, scale, grads * gain_two_row[...])
        acc[rows, :] = total
        low = total.astype(BF16)
        hgr[rows, :] = low
        add_sums(2, everything, low.astype(F32))

    def attend_back(field):
        rows = field_rows(field)
        visible = visible_of(field)
        for pair in range(pairs):
            at_q, at_k, at_v = pair_columns(pair)
            key_rows, values = qkv[rows, at_k], qkv[rows, at_v]
            stacked = stack_heads(qkv[rows, at_q], 0.125)
            attention = soften(stacked, key_rows, visible)
            pulled = stack_heads(act[rows, pl.ds(pair * 128, 128)])
            values_grad = dot_tn(attention.astype(BF16), pulled).astype(BF16)
            inner = dot_nt(pulled, values)
            inner = inner - jnp.sum(attention * inner, -1, keepdims=True)
            scores_grad = (attention * inner).astype(BF16)
            queries_grad = (pick_heads(dot(scores_grad, key_rows)) * 0.125).astype(BF16)
            keys_grad = dot_tn(scores_grad, stacked).astype(BF16)
            qkv[rows, at_q] = queries_grad
            qkv[rows, at_k] = keys_grad
            qkv[rows, at_v] = values_grad
            here = pl.ds(pair * 128, 128)
            add_sums(0, here, queries_grad.astype(F32))
            add_sums(1, here, values_grad.astype(F32))

    def proj_unit():
        for field in range(fields):
            left[:, field_rows(field)] = att[field_rows(field), :].T
        make_unit(8, left_half, lambda: hgr[...])

    def qkv_unit(part):
        if part == 0:
            for field in range(fields):
                left[:, field_rows(field)] = n1[field_rows(field), :].T
        stride = 3 * model // narrow
        make_unit(
            9 + part,
            left_half,
            lambda: jnp.concatenate(
                [
                    qkv[:, pl.ds(block * stride + part * width, width)]
                    for block in range(narrow)
                ],
                1,
            ),
        )

    def source_back(field):
        rows = field_rows(field)
        unit_rows, scale = standardise(tok[rows, :].astype(F32))
        grads = ngr[rows, :]
        add_sums(8, everything, grads * unit_rows)
        add_sums(9, everything, grads)
        acc[rows, :] += norm_back(unit_rows, scale, grads * gain_one_row[...])

    def vec_copy(number):
        return remote(
            vec, vec_in.at[number], vec_send.at[number], vec_recv.at[number], all_bits[number]
        )

    def vec_end(number):
        vec_copy(number).wait()
        vec[...] += vec_in[number]
        if number + 1 < len(all_bits):
            vec_copy(number + 1).start()

    def attend_backs(first, last):
        lax.fori_loop(first, last, lambda field, carry: (attend_back(field), carry)[1], 0)

    def make_attended_grad():
        output_copy.wait()
        act[...] = dot_nt(hgr[...], w_p[...]).astype(BF16)

    def finish_output():
        each_field(store_output)
        output_copy.start()

    def make_normed_grad():
        load(qkv_in, w_a.at[:, pl.ds(0, 3 * model)], 1).wait()
        ngr[...] = dot_nt(qkv[...], w_a[:, pl.ds(0, 3 * model)])

    def finish_tokens():
        each_field(source_back)
        tokens_copy.start()
        vec_copy(0).start()

    up_load.wait()
    down_load.wait()
    cot_load.wait()
    feed(0)
    pl.semaphore_wait(barrier, len(all_bits))
    up_unit(0)
    core_end(0)
    core_end(1)
    core_end(2)
    feed(1)
    up_unit(1)
    work = {
        0: lambda: feed(2),
        1: lambda: up_unit(2),
        2: lambda: feed_sums(0),
        3: lambda: feed(3),
        4: lambda: up_unit(3),
        5: lambda: feed_sums(1),
        6: lambda: feed_sums(2),
        7: lambda: down_unit(0),
        8: lambda: feed_sums(3),
        9: finish_output,
        10: lambda: down_unit(1),
        11: lambda: each_field(middle_back),
        12: make_attended_grad,
        13: lambda: down_unit(2),
        14: lambda: attend_back(0),
        15: lambda: attend_backs(1, fields - 2),
        16: lambda: down_unit(3),
        17: lambda: attend_back(fields - 2),
        18: lambda: attend_back(fields - 1),
        19: proj_unit,
        22: lambda: qkv_unit(0),
        23: make_normed_grad,
        25: lambda: qkv_unit(1),
        26: finish_tokens,
        28: lambda: qkv_unit(2),
        29: lambda: vec_end(0),
        31: lambda: vec_end(1),
        33: lambda: vec_end(2),
        35: lambda: vec_end(3),
        37: lambda: vec_end(4),
    }
    vec_store = pltpu.make_async_copy(vec, vec_out, store_sem.at[2])
    for number in range(parts + LAGS[-1]):
        if number in work:
            work[number]()
        tick(number)
        if 0 <= number + LEAD < parts:
            core_end(number + LEAD)
        if number == 37:
            vec_store.start()
    for copy in result_copies:
        copy.wait()
    tokens_copy.wait()
    vec_store.wait()


def place_results(*refs):
    arrays, vec, placed, vectors, (sem, *held) = refs[:6], refs[6], refs[7:13], refs[13:22], refs[22:]
    inward = [
        pltpu.make_async_copy(src, dst, sem.at[0, number])
        for number, (src, dst) in enumerate(zip(arrays, held))
    ]
    outward = [
        pltpu.make_async_copy(src, dst, sem.at[1, number])
        for number, (src, dst) in enumerate(zip(held, placed))
    ]
    for copy in inward:
        copy.start()
    row = 0
    for vector in vectors:
        model = vec.shape[1]
        for part in range(vector.shape[0] // model):
            vector[pl.ds(part * model, model)] = vec[row, :]
            row += 1
    for before, after in zip(inward, outward):
        before.wait()
        after.start()
    for copy in outward:
        copy.wait()


def local_fused(wide, narrow, *args):
    (
        tokens, land_mask, cotangent, qkv_weight, query_bias, value_bias, proj_weight, proj_bias,
        up_weight, up_bias, down_weight, down_bias, norm1_gain, norm1_shift, norm2_gain, norm2_shift,
    ) = args
    fields, patches, model = tokens.shape
    rows = fields * patches
    hidden_width = up_weight.shape[1]
    width, block_rows = model // narrow, model // wide
    bits = (wide * narrow).bit_length() - 1
    blocks = wide * narrow // 2
    group_rows = block_rows // 3
    gaps = [LEAD] + [LAGS[i] - LAGS[i - 1] for i in range(1, 4)]
    cycle = [2 * (gap + gap % 2) for gap in gaps]
    anywhere = pl.BlockSpec(memory_space=pl.ANY)
    in_vmem = pl.BlockSpec(memory_space=pltpu.VMEM)

    def vmem(shape, dtype=F32):
        return pltpu.VMEM(shape, dtype)

    dma = pltpu.SemaphoreType.DMA
    vectors = [model] * 3 + [hidden_width] + [model] * 5
    results = pl.pallas_call(
        lambda *refs: layer_kernel(wide, narrow, fields, patches, *refs),
        out_shape=[
            jax.ShapeDtypeStruct((rows, model), BF16),
            jax.ShapeDtypeStruct((rows, model), F32),
            jax.ShapeDtypeStruct((block_rows, 3 * width), F32),
            jax.ShapeDtypeStruct((block_rows, width), F32),
            jax.ShapeDtypeStruct((block_rows, 4 * width), F32),
            jax.ShapeDtypeStruct((4 * block_rows, width), F32),
            jax.ShapeDtypeStruct((16, model), F32),
        ],
        in_specs=[anywhere] * 16,
        out_specs=[anywhere] * 7,
        scratch_shapes=[
            vmem((rows, model), BF16),
            vmem((rows, model), BF16),
            vmem((rows, model), BF16),
            vmem((rows, 3 * model), BF16),
            vmem((rows, model), BF16),
            vmem((rows, model)),
            vmem((rows, model), BF16),
            vmem((hidden_width, rows), BF16),
            vmem((4, rows, model), BF16),
            vmem((4, rows, model), BF16),
            vmem((rows, model)),
            vmem((rows, model)),
            vmem((model, rows), BF16),
            vmem((model, hidden_width), BF16),
            vmem((hidden_width, model), BF16),
            vmem((model, model), BF16),
            vmem((1, 3 * model)),
            vmem((8, hidden_width)),
            vmem((3 * SLOTS + 6, 3, blocks, group_rows, 128)),
            vmem((6, 3, blocks, group_rows, 128)),
            vmem((block_rows, 4 * width)),
            vmem((4 * block_rows, width)),
            vmem((block_rows, width)),
            vmem((block_rows, 3 * width)),
            *[vmem((cycle[s], 3, blocks >> (s + 1), group_rows, 128)) for s in range(4)],
            vmem((16, model)),
            vmem((bits, 16, model)),
            dma((16,)),
            dma((6,)),
            dma((6,)),
            pltpu.SemaphoreType.REGULAR,
            dma((sum(gaps), 3)),
            dma((sum(cycle), 3)),
            dma((4,)),
            dma((bits,)),
            dma((bits,)),
            dma((3,)),
            vmem((fields, patches), jnp.int32),
            *[vmem((size,)) for size in vectors],
        ],
        compiler_params=pltpu.CompilerParams(
            collective_id=0, has_side_effects=True, vmem_limit_bytes=63 << 20
        ),
        name="encoder_layer",
    )(
        tokens.reshape(rows, model),
        cotangent.reshape(rows, model),
        qkv_weight,
        proj_weight,
        up_weight,
        down_weight,
        land_mask,
        query_bias,
        value_bias,
        proj_bias,
        up_bias,
        down_bias,
        norm1_gain,
        norm1_shift,
        norm2_gain,
        norm2_shift,
    )
    placed = pl.pallas_call(
        place_results,
        out_shape=[jax.ShapeDtypeStruct(array.shape, array.dtype) for array in results[:6]]
        + [jax.ShapeDtypeStruct((size,), F32) for size in vectors],
        in_specs=[anywhere] * 6 + [in_vmem],
        out_specs=[anywhere] * 6 + [in_vmem] * 9,
        scratch_shapes=[dma((2, 6))] + [vmem(array.shape, array.dtype) for array in results[:6]],
        name="place_results",
    )(*results)
    output, tokens_grad, qkv_grad, proj_grad, up_grad, down_grad = placed[:6]
    (
        query_grad, value_grad, proj_bias_grad, up_bias_grad, down_bias_grad,
        gain_one_grad, shift_one_grad, gain_two_grad, shift_two_grad,
    ) = placed[6:]
    return (
        output.reshape(tokens.shape),
        tokens_grad.reshape(tokens.shape),
        qkv_grad,
        query_grad,
        value_grad,
        proj_grad,
        proj_bias_grad,
        up_grad,
        up_bias_grad,
        down_grad,
        down_bias_grad,
        gain_one_grad,
        shift_one_grad,
        gain_two_grad,
        shift_two_grad,
    )


def layer_norm(inputs, norm_gain, norm_shift):
    average = jnp.mean(inputs, -1, keepdims=True)
    centred = inputs - average
    variance = jnp.mean(centred * centred, -1, keepdims=True)
    return centred * lax.rsqrt(variance + 1e-06) * norm_gain + norm_shift


def attend_scores(queries, key_rows, visible, scaling):
    scores = (
        jnp.einsum("fqhe,fkhe->fhqk", queries, key_rows, preferred_element_type=jnp.float32)
        * scaling
    )
    return jnp.where(visible[:, None, None, :], scores, -1e30)


def share_sums(former, latter):
    row_sums = (
        lax.psum_scatter(former, "wide", scatter_dimension=0, tiled=True),
        lax.psum_scatter(latter, "wide", scatter_dimension=0, tiled=True),
    )
    return (
        lax.psum_scatter(row_sums[0], "narrow", scatter_dimension=1, tiled=True),
        lax.psum_scatter(row_sums[1], "narrow", scatter_dimension=1, tiled=True),
    )


def local(
    tokens,
    land_mask,
    cotangent,
    qkv_weight,
    query_bias,
    value_bias,
    proj_weight,
    proj_bias,
    up_weight,
    up_bias,
    down_weight,
    down_bias,
    norm1_gain,
    norm1_shift,
    norm2_gain,
    norm2_shift,
):
    field_count, length, model_width = tokens.shape
    head_count = HEADS
    head_width = model_width // head_count
    scaling = head_width ** (-0.5)
    visible = land_mask > 0
    split_shape = (field_count, length, head_count, head_width)
    source = tokens.astype(jnp.float32)
    normed_one = layer_norm(source, norm1_gain, norm1_shift).astype(jnp.bfloat16)
    joint = jnp.einsum("fpd,de->fpe", normed_one, qkv_weight, preferred_element_type=jnp.float32)
    queries = (joint[..., :model_width] + query_bias).astype(jnp.bfloat16).reshape(split_shape)
    key_rows = joint[..., model_width : 2 * model_width].astype(jnp.bfloat16).reshape(split_shape)
    values = (joint[..., 2 * model_width :] + value_bias).astype(jnp.bfloat16).reshape(split_shape)
    scores = attend_scores(queries, key_rows, visible, scaling)
    highest = jnp.max(scores, -1, keepdims=True)
    exponent = jnp.exp(scores - highest)
    summed = jnp.sum(exponent, -1, keepdims=True)
    attention = exponent / summed
    log_total = highest + jnp.log(summed)
    attended = jnp.einsum(
        "fhqk,fkhe->fqhe",
        attention.astype(jnp.bfloat16),
        values,
        preferred_element_type=jnp.float32,
    )
    attended = attended.reshape(field_count, length, model_width).astype(jnp.bfloat16)
    middle = (
        source
        + jnp.einsum("fpd,de->fpe", attended, proj_weight, preferred_element_type=jnp.float32)
        + proj_bias
    )
    normed_two = layer_norm(middle, norm2_gain, norm2_shift).astype(jnp.bfloat16)
    hidden = (
        jnp.einsum("fpd,dn->fpn", normed_two, up_weight, preferred_element_type=jnp.float32)
        + up_bias
    )
    activated_full, gelu_pull = jax.vjp(jax.nn.gelu, hidden)
    activated = activated_full.astype(jnp.bfloat16)
    output = (
        middle
        + jnp.einsum("fpn,nd->fpd", activated, down_weight, preferred_element_type=jnp.float32)
        + down_bias
    )
    grad_out = cotangent.astype(jnp.float32)
    down_local = jnp.einsum("fpn,fpd->nd", activated, cotangent, preferred_element_type=jnp.float32)
    down_bias_local = jnp.sum(grad_out, axis=(0, 1))
    activated_grad = jnp.einsum(
        "fpd,nd->fpn", cotangent, down_weight, preferred_element_type=jnp.float32
    )
    hidden_grad = gelu_pull(activated_grad)[0].astype(jnp.bfloat16)
    up_local = jnp.einsum(
        "fpd,fpn->dn", normed_two, hidden_grad, preferred_element_type=jnp.float32
    )
    up_bias_local = jnp.sum(hidden_grad.astype(jnp.float32), axis=(0, 1))
    feed_sums = share_sums(up_local, down_local)
    normed_two_grad = jnp.einsum(
        "fpn,dn->fpd", hidden_grad, up_weight, preferred_element_type=jnp.float32
    )
    unused_two, norm_two_pull = jax.vjp(layer_norm, middle, norm2_gain, norm2_shift)
    middle_part, gain_two_local, shift_two_local = norm_two_pull(normed_two_grad)
    middle_grad = grad_out + middle_part
    middle_low = middle_grad.astype(jnp.bfloat16)
    proj_local = jnp.einsum("fpd,fpe->de", attended, middle_low, preferred_element_type=jnp.float32)
    proj_bias_local = jnp.sum(middle_low.astype(jnp.float32), axis=(0, 1))
    attended_grad = jnp.einsum(
        "fpe,de->fpd", middle_low, proj_weight, preferred_element_type=jnp.float32
    )
    attended_grad = attended_grad.astype(jnp.bfloat16).reshape(split_shape)
    scores = attend_scores(queries, key_rows, visible, scaling)
    attention = jnp.exp(scores - log_total)
    values_grad = jnp.einsum(
        "fhqk,fqhe->fkhe",
        attention.astype(jnp.bfloat16),
        attended_grad,
        preferred_element_type=jnp.float32,
    )
    attention_grad = jnp.einsum(
        "fqhe,fkhe->fhqk", attended_grad, values, preferred_element_type=jnp.float32
    )
    inner_sum = jnp.sum(attention * attention_grad, -1, keepdims=True)
    scores_grad = (attention * (attention_grad - inner_sum)).astype(jnp.bfloat16)
    queries_grad = (
        jnp.einsum("fhqk,fkhe->fqhe", scores_grad, key_rows, preferred_element_type=jnp.float32)
        * scaling
    )
    keys_grad = (
        jnp.einsum("fhqk,fqhe->fkhe", scores_grad, queries, preferred_element_type=jnp.float32)
        * scaling
    )
    flat_shape = (field_count, length, model_width)
    joint_grad = jnp.concatenate(
        [
            queries_grad.reshape(flat_shape),
            keys_grad.reshape(flat_shape),
            values_grad.reshape(flat_shape),
        ],
        -1,
    ).astype(jnp.bfloat16)
    qkv_local = jnp.einsum(
        "fpd,fpe->de", normed_one, joint_grad, preferred_element_type=jnp.float32
    )
    joint_sums = jnp.sum(joint_grad.astype(jnp.float32), axis=(0, 1))
    query_bias_local = joint_sums[:model_width]
    value_bias_local = joint_sums[2 * model_width :]
    attention_sums = share_sums(qkv_local, proj_local)
    normed_one_grad = jnp.einsum(
        "fpe,de->fpd", joint_grad, qkv_weight, preferred_element_type=jnp.float32
    )
    unused_one, norm_one_pull = jax.vjp(layer_norm, source, norm1_gain, norm1_shift)
    source_part, gain_one_local, shift_one_local = norm_one_pull(normed_one_grad)
    tokens_grad = middle_grad + source_part
    vectors = lax.psum(
        (
            query_bias_local,
            value_bias_local,
            proj_bias_local,
            up_bias_local,
            down_bias_local,
            gain_one_local,
            shift_one_local,
            gain_two_local,
            shift_two_local,
        ),
        ("wide", "narrow"),
    )
    return (
        output.astype(jnp.bfloat16),
        tokens_grad,
        attention_sums[0],
        vectors[0],
        vectors[1],
        attention_sums[1],
        vectors[2],
        feed_sums[0],
        vectors[3],
        feed_sums[1],
        vectors[4],
        vectors[5],
        vectors[6],
        vectors[7],
        vectors[8],
    )


def solution(mesh):
    wide, narrow = mesh.shape["wide"], mesh.shape["narrow"]
    placed = (
        P(("wide", "narrow"), None, None),
        P(("wide", "narrow"), None),
        P(("wide", "narrow"), None, None),
        P(),
        P(),
        P(),
        P(),
        P(),
        P(),
        P(),
        P(),
        P(),
        P(),
        P(),
        P(),
        P(),
    )
    fused = (wide, narrow) == (16, 2)

    def layer(*args):
        return local_fused(wide, narrow, *args) if fused else local(*args)

    return jax.shard_map(
        layer,
        mesh=mesh,
        in_specs=placed,
        out_specs=(
            P(("wide", "narrow"), None, None),
            P(("wide", "narrow"), None, None),
            P("wide", "narrow"),
            P(),
            P(),
            P("wide", "narrow"),
            P(),
            P("wide", "narrow"),
            P(),
            P("wide", "narrow"),
            P(),
            P(),
            P(),
            P(),
            P(),
        ),
        check_vma=False,
    )
```

```python
import jax
import jax.numpy as jnp
from jax import lax
from jax.experimental import pallas as pl
from jax.experimental.pallas import tpu as pltpu
from jax.sharding import PartitionSpec as P

HEADS = 12
F32 = jnp.float32
BF16 = jnp.bfloat16
SLOTS = 6
LAGS = (0, 2, 4, 6)
LEAD = 3
UNROLL = 3


def dot(a, b):
    return lax.dot_general(a, b, (((1,), (0,)), ((), ())), preferred_element_type=F32)


def dot_nt(a, b):
    return lax.dot_general(a, b, (((1,), (1,)), ((), ())), preferred_element_type=F32)


def dot_tn(a, b):
    return lax.dot_general(a, b, (((0,), (0,)), ((), ())), preferred_element_type=F32)


def standardise(rows):
    centred = rows - jnp.mean(rows, -1, keepdims=True)
    scale = lax.rsqrt(jnp.mean(centred * centred, -1, keepdims=True) + 1e-06)
    return centred * scale, scale


def norm_back(unit_rows, scale, pulled):
    return scale * (
        pulled
        - jnp.mean(pulled, -1, keepdims=True)
        - unit_rows * jnp.mean(pulled * unit_rows, -1, keepdims=True)
    )


def column_sums(rows):
    return jnp.sum(rows, axis=0, keepdims=True)


def layer_kernel(wide, narrow, fields, patches, *refs):
    (
        tokens_in, cotangent_in, qkv_in, proj_in, up_in, down_in, land_in,
    ) = refs[:7]
    vectors_in, refs = refs[7:16], refs[16:]
    (
        output_out, tokens_out, qkv_out, proj_out, up_out, down_out, vec_out,
        tok, cot, n1, qkv, att, mid, n2, act_t, acts, hgrs, acc, ngr, left, w_a, w_b, w_p, qkv_bias, flat,
        keep, core_in, up_sums, up_sum, down_sum, proj_sum, qkv_sum, in_0, in_1, in_2, in_3, vec, vec_in,
        load_sem, core_send, core_recv, core_free, stage_send, stage_recv, final_sem,
        vec_send, vec_recv, store_sem, land,
    ) = refs[:-9]
    vectors_held = refs[-9:]
    (
        query_bias, value_bias, proj_bias, up_bias, down_bias,
        gain_one, shift_one, gain_two, shift_two,
    ) = vectors_held
    model = tok.shape[1]
    hidden_width = w_a.shape[1]
    stage_in = (in_0, in_1, in_2, in_3)
    act, hgr = acts.at[0], hgrs.at[0]
    at_wide = lax.axis_index("wide")
    at_narrow = lax.axis_index("narrow")
    width = model // narrow
    block_rows = model // wide
    group_rows = block_rows // 3
    chunk = width
    parts = 36

    def my_bit(axis, level):
        index = at_wide if axis == "wide" else at_narrow
        return lax.rem(lax.div(index, 1 << level), 2)

    def partner(axis, level):
        shift = (1 << level) * (1 - 2 * my_bit(axis, level))
        if axis == "wide":
            return (at_wide + shift, at_narrow)
        return (at_wide, at_narrow + shift)

    wide_bits = [("wide", i) for i in range(1, wide.bit_length() - 1)]
    narrow_bits = [("narrow", i) for i in range(narrow.bit_length() - 1)]
    all_bits = [("wide", 0)] + wide_bits + narrow_bits
    stages = len(wide_bits) + len(narrow_bits)
    blocks = 1 << stages
    core = my_bit("wide", 0)
    mine = {bit: my_bit(*bit) for bit in all_bits}
    to = {bit: partner(*bit) for bit in all_bits}

    def order(part, group):
        if group == 0:
            return narrow_bits + wide_bits
        if group == 1:
            return wide_bits[:1] + narrow_bits + wide_bits[1:]
        if part % 2 == 0:
            return wide_bits[1:2] + narrow_bits + wide_bits[:1] + wide_bits[2:]
        return wide_bits[1:2] + wide_bits[:1] + narrow_bits + wide_bits[2:]

    def place(part, group, row_block, column_block):
        found = 0
        for axis, level in order(part, group):
            index = row_block if axis == "wide" else column_block
            found = 2 * found + ((index >> level) & 1)
        return found

    barrier = pltpu.get_barrier_semaphore()
    for bit in all_bits:
        pl.semaphore_signal(
            barrier, inc=1, device_id=to[bit], device_id_type=pl.DeviceIdType.MESH
        )

    def remote(src, dst, send, recv, bit):
        return pltpu.make_async_remote_copy(
            src_ref=src, dst_ref=dst, send_sem=send, recv_sem=recv,
            device_id=to[bit], device_id_type=pl.DeviceIdType.MESH,
        )

    def kept_slot(part):
        return part % (3 * SLOTS)

    def sent_slot(part):
        return 3 * SLOTS + part % 6

    def core_copy(part):
        slot = part % 6
        return remote(
            keep.at[sent_slot(part)], core_in.at[slot],
            core_send.at[slot], core_recv.at[slot], ("wide", 0),
        )

    def core_start(part):
        if part >= 6:
            pl.semaphore_wait(core_free, 1)
        core_copy(part).start()

    def span(part, group, stage):
        half = blocks >> (stage + 1)
        sequence = order(part, group)
        base = 0
        for earlier in range(stage):
            base = base + mine[sequence[earlier]] * (blocks >> (earlier + 1))
        bit = sequence[stage]
        return half, base + mine[bit] * half, base + (1 - mine[bit]) * half, bit

    gaps = [LEAD] + [LAGS[i] - LAGS[i - 1] for i in range(1, 4)]
    cycle = [2 * (gap + gap % 2) for gap in gaps]

    def stage_copy(part, group, stage):
        half, own, other, bit = span(part, group, stage)
        sent = sum(gaps[:stage]) + part % gaps[stage]
        held = sum(cycle[:stage]) + part % cycle[stage]
        return remote(
            keep.at[kept_slot(part), group, pl.ds(other, half)],
            stage_in[stage].at[part % cycle[stage], group],
            stage_send.at[sent, group],
            stage_recv.at[held, group],
            bit,
        )

    def core_end(part):
        slot = part % 6
        core_copy(part).wait()
        keep[kept_slot(part)] += core_in[slot]
        if part + 6 < parts:
            pl.semaphore_signal(
                core_free, inc=1, device_id=to[("wide", 0)],
                device_id_type=pl.DeviceIdType.MESH,
            )
        for group in range(3):
            stage_copy(part, group, 0).start()

    def result_place(part, group):
        unit, row = part // 3, (part % 3) * group_rows
        if unit < 4:
            return up_sum, row, unit * width + group * 128
        if unit < 8:
            return down_sum, (unit - 4) * block_rows + row, group * 128
        if unit == 8:
            return proj_sum, row, group * 128
        return qkv_sum, row, (unit - 9) * width + group * 128

    def stage_end(part, stage):
        for group in range(3):
            stage_copy(part, group, stage).wait()
            half, own, other, bit = span(part, group, stage)
            slot, came = kept_slot(part), stage_in[stage].at[part % cycle[stage], group]
            if stage + 1 < stages:
                keep[slot, group, pl.ds(own, half)] += came[...]
                stage_copy(part, group, stage + 1).start()
            else:
                ref, row, column = result_place(part, group)
                ref[row : row + group_rows, column : column + 128] = (
                    keep[slot, group, own] + came[0]
                )

    result_copies = [
        pltpu.make_async_copy(src, dst, final_sem.at[number])
        for number, (src, dst) in enumerate(
            ((up_sum, up_out), (down_sum, down_out), (proj_sum, proj_out), (qkv_sum, qkv_out))
        )
    ]
    last_part = {11: 0, 23: 1, 26: 2, 35: 3}

    def tick(number):
        for stage in reversed(range(stages)):
            part = number - LAGS[stage]
            if 0 <= part < parts:
                stage_end(part, stage)
                if stage + 1 == stages and part in last_part:
                    result_copies[last_part[part]].start()

    def make_unit(unit, lhs_half, rhs):
        half_blocks = wide // 2

        def one(half, carry):
            product = dot(lhs_half(half), rhs())
            for third in range(3):
                part = 3 * unit + third
                kept, sent = kept_slot(part), sent_slot(part)
                index = [kept + core * (sent - kept), sent + core * (kept - sent)]
                for row_block in range(half_blocks):
                    top = row_block * block_rows + third * group_rows
                    for column_block in range(narrow):
                        for group in range(3):
                            first = place(part, group, row_block, column_block)
                            step = place(part, group, half_blocks, 0)
                            side = column_block * width + group * 128
                            keep[index[row_block % 2], group, first + half * step] = product[
                                top : top + group_rows, side : side + 128
                            ]
            return carry

        lax.fori_loop(0, 2, one, 0)
        for third in range(3):
            core_start(3 * unit + third)

    def row_of(vector):
        return vector[...].reshape(1, vector.shape[0])

    def load(src, dst, number):
        copy = pltpu.make_async_copy(src, dst, load_sem.at[number])
        copy.start()
        return copy

    tok_load = load(tokens_in, tok, 0)
    qkv_load = load(qkv_in, w_a.at[:, pl.ds(0, 3 * model)], 1)
    small_loads = [load(land_in, land, 6)] + [
        load(src, dst, 7 + number)
        for number, (src, dst) in enumerate(zip(vectors_in, vectors_held))
    ]
    vec[...] = jnp.zeros_like(vec)
    acc[...] = jnp.zeros_like(acc)
    ngr[...] = jnp.zeros_like(ngr)
    for small in small_loads:
        small.wait()
    qkv_bias[:, 0:model] = row_of(query_bias)
    qkv_bias[:, model : 2 * model] = jnp.zeros((1, model), F32)
    qkv_bias[:, 2 * model :] = row_of(value_bias)
    for number, vector in enumerate(
        (proj_bias, down_bias, gain_one, shift_one, gain_two, shift_two)
    ):
        flat[number : number + 1, 0:model] = row_of(vector)
    flat[6:7, :] = row_of(up_bias)

    def field_rows(field):
        return pl.ds(pl.multiple_of(field * patches, patches), patches)

    def each_field(step):
        def body(field, carry):
            step(field)
            return carry

        lax.fori_loop(0, fields, body, 0)

    tok_load.wait()
    at_model = pl.ds(0, model)
    proj_row, down_row, gain_one_row, shift_one_row, gain_two_row, shift_two_row = (
        flat.at[pl.ds(number, 1), at_model] for number in range(6)
    )
    up_row = flat.at[pl.ds(6, 1), :]

    def norm_one(field):
        rows = field_rows(field)
        unit_rows, scale = standardise(tok[rows, :].astype(F32))
        n1[rows, :] = (unit_rows * gain_one_row[...] + shift_one_row[...]).astype(BF16)

    each_field(norm_one)
    qkv_load.wait()
    proj_load = load(proj_in, w_p, 2)
    cot_load = load(cotangent_in, cot, 3)
    down_load = load(down_in, w_b, 4)

    def project(tile, carry):
        columns = pl.ds(pl.multiple_of(tile * 256, 256), 256)
        qkv[:, columns] = (dot(n1[...], w_a[:, columns]) + qkv_bias[:, columns]).astype(BF16)
        return carry

    lax.fori_loop(0, 3 * model // 256, project, 0)
    up_load = load(up_in, w_a, 5)

    lane = lax.broadcasted_iota(jnp.int32, (1, 128), 1)
    head_masks = [(lane < 64).astype(BF16), (lane >= 64).astype(BF16)]
    lane_full = lax.broadcasted_iota(jnp.int32, (patches, 128), 1)
    pairs = model // 128

    def stack_heads(rows, factor=1.0):
        return jnp.concatenate([rows * (mask * BF16(factor)) for mask in head_masks], 0)

    def pick_heads(rows):
        return jnp.where(lane_full < 64, rows[:patches], rows[patches:])

    def soften(stacked, key_rows, visible):
        scores = jnp.where(visible, dot_nt(stacked, key_rows), -1e30)
        exponent = jnp.exp(scores - jnp.max(scores, -1, keepdims=True))
        return exponent * (1.0 / jnp.sum(exponent, -1, keepdims=True))

    def pair_columns(pair):
        return [pl.ds(part * model + pair * 128, 128) for part in range(3)]

    def visible_of(field):
        return jnp.broadcast_to(land[pl.ds(field, 1), :], (2 * patches, patches)) > 0

    def attend(field):
        rows = field_rows(field)
        visible = visible_of(field)
        for pair in range(pairs):
            at_q, at_k, at_v = pair_columns(pair)
            attention = soften(stack_heads(qkv[rows, at_q], 0.125), qkv[rows, at_k], visible)
            both = dot(attention.astype(BF16), qkv[rows, at_v])
            att[rows, pl.ds(pair * 128, 128)] = pick_heads(both).astype(BF16)

    each_field(attend)
    proj_load.wait()

    def residual(tile, carry):
        columns = pl.ds(pl.multiple_of(tile * 256, 256), 256)
        mid[:, columns] = (
            tok[:, columns].astype(F32) + dot(att[...], w_p[:, columns]) + proj_row[:, columns]
        )
        return carry

    lax.fori_loop(0, model // 256, residual, 0)

    def norm_two(field):
        rows = field_rows(field)
        unit_rows, scale = standardise(mid[rows, :])
        normed = (unit_rows * gain_two_row[...] + shift_two_row[...]).astype(BF16)
        n2[rows, :] = normed
        left[:, rows] = normed.T

    each_field(norm_two)

    root = 0.7978845608028654

    def hidden_columns(part, column_block):
        return pl.multiple_of(column_block * (hidden_width // narrow) + part * chunk, chunk)

    def each_block(step):
        def body(column_block, carry):
            step(column_block)
            return carry

        lax.fori_loop(0, narrow, body, 0)

    def feed(part):
        def one(column_block):
            first = hidden_columns(part, column_block)
            columns = pl.ds(first, chunk)
            here = pl.ds(pl.multiple_of(column_block * chunk, chunk), chunk)
            hidden = dot(n2[...], w_a[:, columns]) + up_row[:, columns]
            pulled = dot_nt(cot[...], w_b[columns, :])
            square = hidden * hidden
            bent = jnp.tanh(hidden * (root + (root * 0.044715) * square))
            cdf = 0.5 + 0.5 * bent
            activated = (hidden * cdf).astype(BF16)
            slope = cdf + (hidden * (0.5 - 0.5 * bent * bent)) * (
                root + (3 * root * 0.044715) * square
            )
            grad = (pulled * slope).astype(BF16)
            acts[part, :, here] = activated
            hgrs[part, :, here] = grad
            act_t[columns, :] = activated.T
            up_sums[:, columns] = column_sums(grad.astype(F32))

        each_block(one)

    def feed_sums(part):
        def one(column_block):
            columns = pl.ds(hidden_columns(part, column_block), chunk)
            here = pl.ds(pl.multiple_of(column_block * chunk, chunk), chunk)
            acc[...] += dot(acts[part, :, here], w_b[columns, :])
            ngr[...] += dot_nt(hgrs[part, :, here], w_a[:, columns])

        each_block(one)

    def left_half(half):
        return left[pl.ds(pl.multiple_of(half * (model // 2), model // 2), model // 2), :]

    def up_unit(part):
        make_unit(part, left_half, lambda: hgrs[part])

    def down_unit(part):
        def rows(half):
            first = half * (hidden_width // 2) + part * block_rows
            return jnp.concatenate(
                [
                    act_t[
                        pl.ds(pl.multiple_of(first + block * 4 * block_rows, 16), block_rows), :
                    ]
                    for block in range(wide // 2)
                ],
                0,
            )

        make_unit(4 + part, rows, lambda: cot[...])

    def store_output(field):
        rows = field_rows(field)
        act[rows, :] = (mid[rows, :] + acc[rows, :] + down_row[...]).astype(BF16)

    output_copy = pltpu.make_async_copy(act, output_out, store_sem.at[0])
    tokens_copy = pltpu.make_async_copy(acc, tokens_out, store_sem.at[1])

    def add_sums(row, columns, rows):
        vec[pl.ds(row, 1), columns] += column_sums(rows)

    everything = pl.ds(0, model)

    def middle_back(field):
        rows = field_rows(field)
        unit_rows, scale = standardise(mid[rows, :])
        grads = ngr[rows, :]
        top = cot[rows, :].astype(F32)
        add_sums(7, everything, top)
        add_sums(10, everything, grads * unit_rows)
        add_sums(11, everything, grads)
        total = top + norm_back(unit_rows, scale, grads * gain_two_row[...])
        acc[rows, :] = total
        low = total.astype(BF16)
        hgr[rows, :] = low
        add_sums(2, everything, low.astype(F32))

    def attend_back(field, first_pair, last_pair):
        rows = field_rows(field)
        visible = visible_of(field)

        def one(pair, carry):
            here = pl.multiple_of(pair * 128, 128)
            at_q, at_k, at_v = (pl.ds(step * model + here, 128) for step in range(3))
            key_rows, values = qkv[rows, at_k], qkv[rows, at_v]
            stacked = stack_heads(qkv[rows, at_q], 0.125)
            attention = soften(stacked, key_rows, visible)
            pulled = stack_heads(act[rows, pl.ds(here, 128)])
            values_grad = dot_tn(attention.astype(BF16), pulled).astype(BF16)
            inner = dot_nt(pulled, values)
            inner = inner - jnp.sum(attention * inner, -1, keepdims=True)
            scores_grad = (attention * inner).astype(BF16)
            queries_grad = (pick_heads(dot(scores_grad, key_rows)) * 0.125).astype(BF16)
            keys_grad = dot_tn(scores_grad, stacked).astype(BF16)
            qkv[rows, at_q] = queries_grad
            qkv[rows, at_k] = keys_grad
            qkv[rows, at_v] = values_grad
            add_sums(0, pl.ds(here, 128), queries_grad.astype(F32))
            add_sums(1, pl.ds(here, 128), values_grad.astype(F32))
            return carry

        lax.fori_loop(first_pair, last_pair, one, 0, unroll=UNROLL)

    def turn(source):
        for field in range(fields):
            left[:, field_rows(field)] = source[field_rows(field), :].T

    def proj_unit():
        turn(att)
        make_unit(8, left_half, lambda: hgr[...])

    def qkv_unit(part):
        stride = 3 * model // narrow
        make_unit(
            9 + part,
            left_half,
            lambda: jnp.concatenate(
                [
                    qkv[:, pl.ds(block * stride + part * width, width)]
                    for block in range(narrow)
                ],
                1,
            ),
        )

    def source_back(field):
        rows = field_rows(field)
        unit_rows, scale = standardise(tok[rows, :].astype(F32))
        grads = ngr[rows, :]
        add_sums(8, everything, grads * unit_rows)
        add_sums(9, everything, grads)
        acc[rows, :] += norm_back(unit_rows, scale, grads * gain_one_row[...])

    def vec_copy(number):
        return remote(
            vec, vec_in.at[number], vec_send.at[number], vec_recv.at[number], all_bits[number]
        )

    def vec_end(number):
        vec_copy(number).wait()
        vec[...] += vec_in[number]
        if number + 1 < len(all_bits):
            vec_copy(number + 1).start()

    def make_attended_grad():
        output_copy.wait()
        act[...] = dot_nt(hgr[...], w_p[...]).astype(BF16)

    def finish_output():
        for number in range(hidden_width // model):
            vec[3 + number : 4 + number, :] = up_sums[:, number * model : (number + 1) * model]
        each_field(store_output)
        output_copy.start()

    qkv_again = pltpu.make_async_copy(qkv_in, w_a.at[:, pl.ds(0, 3 * model)], load_sem.at[1])

    def make_normed_grad(half):
        columns = pl.ds(half * (model // 2), model // 2)
        if half == 0:
            qkv_again.wait()
        ngr[:, columns] = dot_nt(qkv[...], w_a[columns, pl.ds(0, 3 * model)])

    def finish_tokens():
        each_field(source_back)
        tokens_copy.start()
        vec_copy(0).start()

    def some(step, *values):
        return lambda: step(*values)

    halves = [(0, pairs // 2), (pairs // 2, pairs)]
    backs = [
        some(attend_back, field, *half) for field in range(fields) for half in halves
    ]
    backs_at = {13: 1, 15: 1, 16: 1, 18: 1, 19: 1, 21: 1, 22: 2}
    work = {
        0: [some(feed, 2)],
        1: [some(feed_sums, 0)],
        2: [some(up_unit, 2)],
        3: [some(feed, 3)],
        5: [some(up_unit, 3)],
        6: [some(feed_sums, 1)],
        7: [some(feed_sums, 2)],
        8: [some(down_unit, 0)],
        9: [some(feed_sums, 3), qkv_again.start],
        10: [finish_output],
        11: [some(down_unit, 1)],
        12: [some(each_field, middle_back), make_attended_grad],
        14: [some(down_unit, 2)],
        17: [some(down_unit, 3)],
        20: [proj_unit],
        23: [some(turn, n1), some(qkv_unit, 0)],
        24: [some(make_normed_grad, 0)],
        25: [some(make_normed_grad, 1)],
        26: [some(qkv_unit, 1)],
        27: [finish_tokens],
        29: [some(qkv_unit, 2)],
    }
    for number, count in backs_at.items():
        work[number] = [backs.pop(0) for _ in range(count)]
    for number in range(len(all_bits)):
        work.setdefault(30 + 2 * number, []).append(some(vec_end, number))

    up_load.wait()
    down_load.wait()
    cot_load.wait()
    feed(0)
    pl.semaphore_wait(barrier, len(all_bits))
    up_unit(0)
    core_end(0)
    core_end(1)
    core_end(2)
    feed(1)
    up_unit(1)
    vec_store = pltpu.make_async_copy(vec, vec_out, store_sem.at[2])
    for number in range(parts + LAGS[-1]):
        for step in work.get(number, []):
            step()
        tick(number)
        if 0 <= number + LEAD < parts:
            core_end(number + LEAD)
        if number == 30 + 2 * (len(all_bits) - 1):
            vec_store.start()
    for copy in result_copies:
        copy.wait()
    tokens_copy.wait()
    vec_store.wait()


def place_results(*refs):
    arrays, vec, placed, vectors, (sem, *held) = refs[:6], refs[6], refs[7:13], refs[13:22], refs[22:]
    inward = [
        pltpu.make_async_copy(src, dst, sem.at[0, number])
        for number, (src, dst) in enumerate(zip(arrays, held))
    ]
    outward = [
        pltpu.make_async_copy(src, dst, sem.at[1, number])
        for number, (src, dst) in enumerate(zip(held, placed))
    ]
    for copy in inward:
        copy.start()
    row = 0
    for vector in vectors:
        model = vec.shape[1]
        for part in range(vector.shape[0] // model):
            vector[pl.ds(part * model, model)] = vec[row, :]
            row += 1
    for before, after in zip(inward, outward):
        before.wait()
        after.start()
    for copy in outward:
        copy.wait()


def local_fused(wide, narrow, *args):
    (
        tokens, land_mask, cotangent, qkv_weight, query_bias, value_bias, proj_weight, proj_bias,
        up_weight, up_bias, down_weight, down_bias, norm1_gain, norm1_shift, norm2_gain, norm2_shift,
    ) = args
    fields, patches, model = tokens.shape
    rows = fields * patches
    hidden_width = up_weight.shape[1]
    width, block_rows = model // narrow, model // wide
    bits = (wide * narrow).bit_length() - 1
    blocks = wide * narrow // 2
    group_rows = block_rows // 3
    gaps = [LEAD] + [LAGS[i] - LAGS[i - 1] for i in range(1, 4)]
    cycle = [2 * (gap + gap % 2) for gap in gaps]
    anywhere = pl.BlockSpec(memory_space=pl.ANY)
    in_vmem = pl.BlockSpec(memory_space=pltpu.VMEM)

    def vmem(shape, dtype=F32):
        return pltpu.VMEM(shape, dtype)

    dma = pltpu.SemaphoreType.DMA
    vectors = [model] * 3 + [hidden_width] + [model] * 5
    results = pl.pallas_call(
        lambda *refs: layer_kernel(wide, narrow, fields, patches, *refs),
        out_shape=[
            jax.ShapeDtypeStruct((rows, model), BF16),
            jax.ShapeDtypeStruct((rows, model), F32),
            jax.ShapeDtypeStruct((block_rows, 3 * width), F32),
            jax.ShapeDtypeStruct((block_rows, width), F32),
            jax.ShapeDtypeStruct((block_rows, 4 * width), F32),
            jax.ShapeDtypeStruct((4 * block_rows, width), F32),
            jax.ShapeDtypeStruct((16, model), F32),
        ],
        in_specs=[anywhere] * 16,
        out_specs=[anywhere] * 7,
        scratch_shapes=[
            vmem((rows, model), BF16),
            vmem((rows, model), BF16),
            vmem((rows, model), BF16),
            vmem((rows, 3 * model), BF16),
            vmem((rows, model), BF16),
            vmem((rows, model)),
            vmem((rows, model), BF16),
            vmem((hidden_width, rows), BF16),
            vmem((4, rows, model), BF16),
            vmem((4, rows, model), BF16),
            vmem((rows, model)),
            vmem((rows, model)),
            vmem((model, rows), BF16),
            vmem((model, hidden_width), BF16),
            vmem((hidden_width, model), BF16),
            vmem((model, model), BF16),
            vmem((1, 3 * model)),
            vmem((8, hidden_width)),
            vmem((3 * SLOTS + 6, 3, blocks, group_rows, 128)),
            vmem((6, 3, blocks, group_rows, 128)),
            vmem((1, hidden_width)),
            vmem((block_rows, 4 * width)),
            vmem((4 * block_rows, width)),
            vmem((block_rows, width)),
            vmem((block_rows, 3 * width)),
            *[vmem((cycle[s], 3, blocks >> (s + 1), group_rows, 128)) for s in range(4)],
            vmem((16, model)),
            vmem((bits, 16, model)),
            dma((16,)),
            dma((6,)),
            dma((6,)),
            pltpu.SemaphoreType.REGULAR,
            dma((sum(gaps), 3)),
            dma((sum(cycle), 3)),
            dma((4,)),
            dma((bits,)),
            dma((bits,)),
            dma((3,)),
            vmem((fields, patches), jnp.int32),
            *[vmem((size,)) for size in vectors],
        ],
        compiler_params=pltpu.CompilerParams(
            collective_id=0, has_side_effects=True, vmem_limit_bytes=63 << 20
        ),
        name="encoder_layer",
    )(
        tokens.reshape(rows, model),
        cotangent.reshape(rows, model),
        qkv_weight,
        proj_weight,
        up_weight,
        down_weight,
        land_mask,
        query_bias,
        value_bias,
        proj_bias,
        up_bias,
        down_bias,
        norm1_gain,
        norm1_shift,
        norm2_gain,
        norm2_shift,
    )
    placed = pl.pallas_call(
        place_results,
        out_shape=[jax.ShapeDtypeStruct(array.shape, array.dtype) for array in results[:6]]
        + [jax.ShapeDtypeStruct((size,), F32) for size in vectors],
        in_specs=[anywhere] * 6 + [in_vmem],
        out_specs=[anywhere] * 6 + [in_vmem] * 9,
        scratch_shapes=[dma((2, 6))] + [vmem(array.shape, array.dtype) for array in results[:6]],
        name="place_results",
    )(*results)
    output, tokens_grad, qkv_grad, proj_grad, up_grad, down_grad = placed[:6]
    (
        query_grad, value_grad, proj_bias_grad, up_bias_grad, down_bias_grad,
        gain_one_grad, shift_one_grad, gain_two_grad, shift_two_grad,
    ) = placed[6:]
    return (
        output.reshape(tokens.shape),
        tokens_grad.reshape(tokens.shape),
        qkv_grad,
        query_grad,
        value_grad,
        proj_grad,
        proj_bias_grad,
        up_grad,
        up_bias_grad,
        down_grad,
        down_bias_grad,
        gain_one_grad,
        shift_one_grad,
        gain_two_grad,
        shift_two_grad,
    )


def layer_norm(inputs, norm_gain, norm_shift):
    average = jnp.mean(inputs, -1, keepdims=True)
    centred = inputs - average
    variance = jnp.mean(centred * centred, -1, keepdims=True)
    return centred * lax.rsqrt(variance + 1e-06) * norm_gain + norm_shift


def attend_scores(queries, key_rows, visible, scaling):
    scores = (
        jnp.einsum("fqhe,fkhe->fhqk", queries, key_rows, preferred_element_type=jnp.float32)
        * scaling
    )
    return jnp.where(visible[:, None, None, :], scores, -1e30)


def share_sums(former, latter):
    row_sums = (
        lax.psum_scatter(former, "wide", scatter_dimension=0, tiled=True),
        lax.psum_scatter(latter, "wide", scatter_dimension=0, tiled=True),
    )
    return (
        lax.psum_scatter(row_sums[0], "narrow", scatter_dimension=1, tiled=True),
        lax.psum_scatter(row_sums[1], "narrow", scatter_dimension=1, tiled=True),
    )


def local(
    tokens,
    land_mask,
    cotangent,
    qkv_weight,
    query_bias,
    value_bias,
    proj_weight,
    proj_bias,
    up_weight,
    up_bias,
    down_weight,
    down_bias,
    norm1_gain,
    norm1_shift,
    norm2_gain,
    norm2_shift,
):
    field_count, length, model_width = tokens.shape
    head_count = HEADS
    head_width = model_width // head_count
    scaling = head_width ** (-0.5)
    visible = land_mask > 0
    split_shape = (field_count, length, head_count, head_width)
    source = tokens.astype(jnp.float32)
    normed_one = layer_norm(source, norm1_gain, norm1_shift).astype(jnp.bfloat16)
    joint = jnp.einsum("fpd,de->fpe", normed_one, qkv_weight, preferred_element_type=jnp.float32)
    queries = (joint[..., :model_width] + query_bias).astype(jnp.bfloat16).reshape(split_shape)
    key_rows = joint[..., model_width : 2 * model_width].astype(jnp.bfloat16).reshape(split_shape)
    values = (joint[..., 2 * model_width :] + value_bias).astype(jnp.bfloat16).reshape(split_shape)
    scores = attend_scores(queries, key_rows, visible, scaling)
    highest = jnp.max(scores, -1, keepdims=True)
    exponent = jnp.exp(scores - highest)
    summed = jnp.sum(exponent, -1, keepdims=True)
    attention = exponent / summed
    log_total = highest + jnp.log(summed)
    attended = jnp.einsum(
        "fhqk,fkhe->fqhe",
        attention.astype(jnp.bfloat16),
        values,
        preferred_element_type=jnp.float32,
    )
    attended = attended.reshape(field_count, length, model_width).astype(jnp.bfloat16)
    middle = (
        source
        + jnp.einsum("fpd,de->fpe", attended, proj_weight, preferred_element_type=jnp.float32)
        + proj_bias
    )
    normed_two = layer_norm(middle, norm2_gain, norm2_shift).astype(jnp.bfloat16)
    hidden = (
        jnp.einsum("fpd,dn->fpn", normed_two, up_weight, preferred_element_type=jnp.float32)
        + up_bias
    )
    activated_full, gelu_pull = jax.vjp(jax.nn.gelu, hidden)
    activated = activated_full.astype(jnp.bfloat16)
    output = (
        middle
        + jnp.einsum("fpn,nd->fpd", activated, down_weight, preferred_element_type=jnp.float32)
        + down_bias
    )
    grad_out = cotangent.astype(jnp.float32)
    down_local = jnp.einsum("fpn,fpd->nd", activated, cotangent, preferred_element_type=jnp.float32)
    down_bias_local = jnp.sum(grad_out, axis=(0, 1))
    activated_grad = jnp.einsum(
        "fpd,nd->fpn", cotangent, down_weight, preferred_element_type=jnp.float32
    )
    hidden_grad = gelu_pull(activated_grad)[0].astype(jnp.bfloat16)
    up_local = jnp.einsum(
        "fpd,fpn->dn", normed_two, hidden_grad, preferred_element_type=jnp.float32
    )
    up_bias_local = jnp.sum(hidden_grad.astype(jnp.float32), axis=(0, 1))
    feed_sums = share_sums(up_local, down_local)
    normed_two_grad = jnp.einsum(
        "fpn,dn->fpd", hidden_grad, up_weight, preferred_element_type=jnp.float32
    )
    unused_two, norm_two_pull = jax.vjp(layer_norm, middle, norm2_gain, norm2_shift)
    middle_part, gain_two_local, shift_two_local = norm_two_pull(normed_two_grad)
    middle_grad = grad_out + middle_part
    middle_low = middle_grad.astype(jnp.bfloat16)
    proj_local = jnp.einsum("fpd,fpe->de", attended, middle_low, preferred_element_type=jnp.float32)
    proj_bias_local = jnp.sum(middle_low.astype(jnp.float32), axis=(0, 1))
    attended_grad = jnp.einsum(
        "fpe,de->fpd", middle_low, proj_weight, preferred_element_type=jnp.float32
    )
    attended_grad = attended_grad.astype(jnp.bfloat16).reshape(split_shape)
    scores = attend_scores(queries, key_rows, visible, scaling)
    attention = jnp.exp(scores - log_total)
    values_grad = jnp.einsum(
        "fhqk,fqhe->fkhe",
        attention.astype(jnp.bfloat16),
        attended_grad,
        preferred_element_type=jnp.float32,
    )
    attention_grad = jnp.einsum(
        "fqhe,fkhe->fhqk", attended_grad, values, preferred_element_type=jnp.float32
    )
    inner_sum = jnp.sum(attention * attention_grad, -1, keepdims=True)
    scores_grad = (attention * (attention_grad - inner_sum)).astype(jnp.bfloat16)
    queries_grad = (
        jnp.einsum("fhqk,fkhe->fqhe", scores_grad, key_rows, preferred_element_type=jnp.float32)
        * scaling
    )
    keys_grad = (
        jnp.einsum("fhqk,fqhe->fkhe", scores_grad, queries, preferred_element_type=jnp.float32)
        * scaling
    )
    flat_shape = (field_count, length, model_width)
    joint_grad = jnp.concatenate(
        [
            queries_grad.reshape(flat_shape),
            keys_grad.reshape(flat_shape),
            values_grad.reshape(flat_shape),
        ],
        -1,
    ).astype(jnp.bfloat16)
    qkv_local = jnp.einsum(
        "fpd,fpe->de", normed_one, joint_grad, preferred_element_type=jnp.float32
    )
    joint_sums = jnp.sum(joint_grad.astype(jnp.float32), axis=(0, 1))
    query_bias_local = joint_sums[:model_width]
    value_bias_local = joint_sums[2 * model_width :]
    attention_sums = share_sums(qkv_local, proj_local)
    normed_one_grad = jnp.einsum(
        "fpe,de->fpd", joint_grad, qkv_weight, preferred_element_type=jnp.float32
    )
    unused_one, norm_one_pull = jax.vjp(layer_norm, source, norm1_gain, norm1_shift)
    source_part, gain_one_local, shift_one_local = norm_one_pull(normed_one_grad)
    tokens_grad = middle_grad + source_part
    vectors = lax.psum(
        (
            query_bias_local,
            value_bias_local,
            proj_bias_local,
            up_bias_local,
            down_bias_local,
            gain_one_local,
            shift_one_local,
            gain_two_local,
            shift_two_local,
        ),
        ("wide", "narrow"),
    )
    return (
        output.astype(jnp.bfloat16),
        tokens_grad,
        attention_sums[0],
        vectors[0],
        vectors[1],
        attention_sums[1],
        vectors[2],
        feed_sums[0],
        vectors[3],
        feed_sums[1],
        vectors[4],
        vectors[5],
        vectors[6],
        vectors[7],
        vectors[8],
    )


def solution(mesh):
    wide, narrow = mesh.shape["wide"], mesh.shape["narrow"]
    placed = (
        P(("wide", "narrow"), None, None),
        P(("wide", "narrow"), None),
        P(("wide", "narrow"), None, None),
        P(),
        P(),
        P(),
        P(),
        P(),
        P(),
        P(),
        P(),
        P(),
        P(),
        P(),
        P(),
        P(),
    )
    fused = (wide, narrow) == (16, 2)

    def layer(*args):
        return local_fused(wide, narrow, *args) if fused else local(*args)

    return jax.shard_map(
        layer,
        mesh=mesh,
        in_specs=placed,
        out_specs=(
            P(("wide", "narrow"), None, None),
            P(("wide", "narrow"), None, None),
            P("wide", "narrow"),
            P(),
            P(),
            P("wide", "narrow"),
            P(),
            P("wide", "narrow"),
            P(),
            P("wide", "narrow"),
            P(),
            P(),
            P(),
            P(),
            P(),
        ),
        check_vma=False,
    )
```

```python
import jax
import jax.numpy as jnp
from jax import lax
from jax.experimental import pallas as pl
from jax.experimental.pallas import tpu as pltpu
from jax.sharding import PartitionSpec as P

HEADS = 12
F32 = jnp.float32
BF16 = jnp.bfloat16
SLOTS = 6
LAGS = (0, 2, 4, 6)
LEAD = 3
TILE = 768
FIRST = 9


def dot(a, b):
    return lax.dot_general(a, b, (((1,), (0,)), ((), ())), preferred_element_type=F32)


def dot_nt(a, b):
    return lax.dot_general(a, b, (((1,), (1,)), ((), ())), preferred_element_type=F32)


def dot_tn(a, b):
    return lax.dot_general(a, b, (((0,), (0,)), ((), ())), preferred_element_type=F32)


def standardise(rows):
    centred = rows - jnp.mean(rows, -1, keepdims=True)
    scale = lax.rsqrt(jnp.mean(centred * centred, -1, keepdims=True) + 1e-06)
    return centred * scale, scale


def norm_back(unit_rows, scale, pulled):
    return scale * (
        pulled
        - jnp.mean(pulled, -1, keepdims=True)
        - unit_rows * jnp.mean(pulled * unit_rows, -1, keepdims=True)
    )


def column_sums(rows):
    return jnp.sum(rows, axis=0, keepdims=True)


def layer_kernel(wide, narrow, fields, patches, *refs):
    (
        tokens_in, cotangent_in, qkv_in, proj_in, up_in, down_in, land_in,
    ) = refs[:7]
    vectors_in, refs = refs[7:16], refs[16:]
    (
        output_out, tokens_out, qkv_out, proj_out, up_out, down_out, vec_out,
        tok, cot, n1, qkv, att, mid, n2, act_t, acts, hgrs, acc, ngr, left, w_a, w_b, w_p, qkv_bias, flat,
        keep, core_in, up_sums, up_sum, down_sum, proj_sum, qkv_sum, in_0, in_1, in_2, in_3, vec, vec_in,
        load_sem, core_send, core_recv, core_free, stage_send, stage_recv, final_sem,
        vec_send, vec_recv, store_sem, land,
    ) = refs[:-9]
    vectors_held = refs[-9:]
    (
        query_bias, value_bias, proj_bias, up_bias, down_bias,
        gain_one, shift_one, gain_two, shift_two,
    ) = vectors_held
    model = tok.shape[1]
    hidden_width = w_a.shape[1]
    stage_in = (in_0, in_1, in_2, in_3)
    act, hgr = acts.at[0], hgrs.at[0]
    at_wide = lax.axis_index("wide")
    at_narrow = lax.axis_index("narrow")
    width = model // narrow
    block_rows = model // wide
    group_rows = block_rows // 3
    chunk = width
    parts = 36

    def my_bit(axis, level):
        index = at_wide if axis == "wide" else at_narrow
        return lax.rem(lax.div(index, 1 << level), 2)

    def partner(axis, level):
        shift = (1 << level) * (1 - 2 * my_bit(axis, level))
        if axis == "wide":
            return (at_wide + shift, at_narrow)
        return (at_wide, at_narrow + shift)

    wide_bits = [("wide", i) for i in range(1, wide.bit_length() - 1)]
    narrow_bits = [("narrow", i) for i in range(narrow.bit_length() - 1)]
    all_bits = [("wide", 0)] + wide_bits + narrow_bits
    stages = len(wide_bits) + len(narrow_bits)
    blocks = 1 << stages
    core = my_bit("wide", 0)
    mine = {bit: my_bit(*bit) for bit in all_bits}
    to = {bit: partner(*bit) for bit in all_bits}

    def order(part, group):
        if group == 0:
            return narrow_bits + wide_bits
        if group == 1:
            return wide_bits[:1] + narrow_bits + wide_bits[1:]
        if part % 2 == 0:
            return wide_bits[1:2] + narrow_bits + wide_bits[:1] + wide_bits[2:]
        return wide_bits[1:2] + wide_bits[:1] + narrow_bits + wide_bits[2:]

    def place(part, group, row_block, column_block):
        found = 0
        for axis, level in order(part, group):
            index = row_block if axis == "wide" else column_block
            found = 2 * found + ((index >> level) & 1)
        return found

    barrier = pltpu.get_barrier_semaphore()
    for bit in all_bits:
        pl.semaphore_signal(
            barrier, inc=1, device_id=to[bit], device_id_type=pl.DeviceIdType.MESH
        )

    def remote(src, dst, send, recv, bit):
        return pltpu.make_async_remote_copy(
            src_ref=src, dst_ref=dst, send_sem=send, recv_sem=recv,
            device_id=to[bit], device_id_type=pl.DeviceIdType.MESH,
        )

    def kept_slot(part):
        return part % (3 * SLOTS)

    def sent_slot(part):
        return 3 * SLOTS + part % 6

    def core_copy(part):
        slot = part % 6
        return remote(
            keep.at[sent_slot(part)], core_in.at[slot],
            core_send.at[slot], core_recv.at[slot], ("wide", 0),
        )

    def core_start(part):
        if part >= 6:
            pl.semaphore_wait(core_free, 1)
        core_copy(part).start()

    def span(part, group, stage):
        half = blocks >> (stage + 1)
        sequence = order(part, group)
        base = 0
        for earlier in range(stage):
            base = base + mine[sequence[earlier]] * (blocks >> (earlier + 1))
        bit = sequence[stage]
        return half, base + mine[bit] * half, base + (1 - mine[bit]) * half, bit

    gaps = [LEAD] + [LAGS[i] - LAGS[i - 1] for i in range(1, 4)]
    cycle = [2 * (gap + gap % 2) for gap in gaps]

    def stage_copy(part, group, stage):
        half, own, other, bit = span(part, group, stage)
        sent = sum(gaps[:stage]) + part % gaps[stage]
        held = sum(cycle[:stage]) + part % cycle[stage]
        return remote(
            keep.at[kept_slot(part), group, pl.ds(other, half)],
            stage_in[stage].at[part % cycle[stage], group],
            stage_send.at[sent, group],
            stage_recv.at[held, group],
            bit,
        )

    def core_end(part):
        slot = part % 6
        core_copy(part).wait()
        keep[kept_slot(part)] += core_in[slot]
        if part + 6 < parts:
            pl.semaphore_signal(
                core_free, inc=1, device_id=to[("wide", 0)],
                device_id_type=pl.DeviceIdType.MESH,
            )
        for group in range(3):
            stage_copy(part, group, 0).start()

    def result_place(part, group):
        unit, row = part // 3, (part % 3) * group_rows
        if unit < 4:
            return up_sum, row, unit * width + group * 128
        if unit < 8:
            return down_sum, (unit - 4) * block_rows + row, group * 128
        if unit == 8:
            return proj_sum, row, group * 128
        return qkv_sum, row, (unit - 9) * width + group * 128

    def stage_end(part, stage):
        for group in range(3):
            stage_copy(part, group, stage).wait()
            half, own, other, bit = span(part, group, stage)
            slot, came = kept_slot(part), stage_in[stage].at[part % cycle[stage], group]
            if stage + 1 < stages:
                keep[slot, group, pl.ds(own, half)] += came[...]
                stage_copy(part, group, stage + 1).start()
            else:
                ref, row, column = result_place(part, group)
                ref[row : row + group_rows, column : column + 128] = (
                    keep[slot, group, own] + came[0]
                )

    result_copies = [
        pltpu.make_async_copy(src, dst, final_sem.at[number])
        for number, (src, dst) in enumerate(
            ((up_sum, up_out), (down_sum, down_out), (proj_sum, proj_out), (qkv_sum, qkv_out))
        )
    ]
    last_part = {11: 0, 23: 1, 26: 2, 35: 3}

    def tick(number, between=()):
        for stage in reversed(range(stages)):
            if stage == 1:
                for step in between:
                    step()
            part = number - LAGS[stage]
            if 0 <= part < parts:
                stage_end(part, stage)
                if stage + 1 == stages and part in last_part:
                    result_copies[last_part[part]].start()

    def make_unit(unit, lhs_half, rhs):
        half_blocks = wide // 2

        def one(half, carry):
            product = dot(lhs_half(half), rhs())
            for third in range(3):
                part = 3 * unit + third
                kept, sent = kept_slot(part), sent_slot(part)
                index = [kept + core * (sent - kept), sent + core * (kept - sent)]
                for row_block in range(half_blocks):
                    top = row_block * block_rows + third * group_rows
                    for column_block in range(narrow):
                        for group in range(3):
                            first = place(part, group, row_block, column_block)
                            step = place(part, group, half_blocks, 0)
                            side = column_block * width + group * 128
                            keep[index[row_block % 2], group, first + half * step] = product[
                                top : top + group_rows, side : side + 128
                            ]
            return carry

        lax.fori_loop(0, 2, one, 0)
        for third in range(3):
            core_start(3 * unit + third)

    def row_of(vector):
        return vector[...].reshape(1, vector.shape[0])

    def load(src, dst, number):
        copy = pltpu.make_async_copy(src, dst, load_sem.at[number])
        copy.start()
        return copy

    tok_load = load(tokens_in, tok, 0)
    qkv_load = load(qkv_in, w_a.at[:, pl.ds(0, 3 * model)], 1)
    small_loads = [load(land_in, land, 6)] + [
        load(src, dst, 7 + number)
        for number, (src, dst) in enumerate(zip(vectors_in, vectors_held))
    ]
    vec[...] = jnp.zeros_like(vec)
    acc[...] = jnp.zeros_like(acc)
    ngr[...] = jnp.zeros_like(ngr)
    for small in small_loads:
        small.wait()
    qkv_bias[:, 0:model] = row_of(query_bias)
    qkv_bias[:, model : 2 * model] = jnp.zeros((1, model), F32)
    qkv_bias[:, 2 * model :] = row_of(value_bias)
    for number, vector in enumerate(
        (proj_bias, down_bias, gain_one, shift_one, gain_two, shift_two)
    ):
        flat[number : number + 1, 0:model] = row_of(vector)
    flat[6:7, :] = row_of(up_bias)

    def field_rows(field):
        return pl.ds(pl.multiple_of(field * patches, patches), patches)

    def each_field(step):
        def body(field, carry):
            step(field)
            return carry

        lax.fori_loop(0, fields, body, 0)

    tok_load.wait()
    at_model = pl.ds(0, model)
    proj_row, down_row, gain_one_row, shift_one_row, gain_two_row, shift_two_row = (
        flat.at[pl.ds(number, 1), at_model] for number in range(6)
    )
    up_row = flat.at[pl.ds(6, 1), :]

    def norm_one(field):
        rows = field_rows(field)
        unit_rows, scale = standardise(tok[rows, :].astype(F32))
        n1[rows, :] = (unit_rows * gain_one_row[...] + shift_one_row[...]).astype(BF16)

    each_field(norm_one)
    qkv_load.wait()
    proj_load = load(proj_in, w_p, 2)
    cot_load = load(cotangent_in, cot, 3)
    down_load = load(down_in, w_b, 4)

    def project(tile, carry):
        columns = pl.ds(pl.multiple_of(tile * TILE, TILE), TILE)
        qkv[:, columns] = (dot(n1[...], w_a[:, columns]) + qkv_bias[:, columns]).astype(BF16)
        return carry

    lax.fori_loop(0, 3 * model // TILE, project, 0)
    up_load = load(up_in, w_a, 5)

    lane = lax.broadcasted_iota(jnp.int32, (1, 128), 1)
    head_masks = [(lane < 64).astype(BF16), (lane >= 64).astype(BF16)]
    lane_full = lax.broadcasted_iota(jnp.int32, (patches, 128), 1)
    pairs = model // 128

    def stack_heads(rows, factor=1.0):
        return jnp.concatenate([rows * (mask * BF16(factor)) for mask in head_masks], 0)

    def pick_heads(rows):
        return jnp.where(lane_full < 64, rows[:patches], rows[patches:])

    def soften(stacked, key_rows, visible):
        scores = [dot_nt(one, keys) for one, keys in zip(stacked, key_rows)]
        scores = [jnp.where(visible, one, -1e30) for one in scores]
        tops = [jnp.max(one, -1, keepdims=True) for one in scores]
        exponents = [jnp.exp(one - top) for one, top in zip(scores, tops)]
        shares = [1.0 / jnp.sum(one, -1, keepdims=True) for one in exponents]
        return [one * share for one, share in zip(exponents, shares)]

    def pair_columns(pair):
        return [pl.ds(part * model + pair * 128, 128) for part in range(3)]

    def visible_of(field):
        return jnp.broadcast_to(land[pl.ds(field, 1), :], (2 * patches, patches)) > 0

    def attend(field):
        rows = field_rows(field)
        visible = visible_of(field)
        at = [pair_columns(pair) for pair in range(pairs)]
        stacked = [stack_heads(qkv[rows, at_q], 0.125) for at_q, at_k, at_v in at]
        attention = soften(stacked, [qkv[rows, at_k] for at_q, at_k, at_v in at], visible)
        both = [
            dot(one.astype(BF16), qkv[rows, at_v])
            for one, (at_q, at_k, at_v) in zip(attention, at)
        ]
        for pair in range(pairs):
            att[rows, pl.ds(pair * 128, 128)] = pick_heads(both[pair]).astype(BF16)

    each_field(attend)
    proj_load.wait()

    def residual(tile, carry):
        columns = pl.ds(pl.multiple_of(tile * 256, 256), 256)
        mid[:, columns] = (
            tok[:, columns].astype(F32) + dot(att[...], w_p[:, columns]) + proj_row[:, columns]
        )
        return carry

    lax.fori_loop(0, model // 256, residual, 0)

    def norm_two(field):
        rows = field_rows(field)
        unit_rows, scale = standardise(mid[rows, :])
        normed = (unit_rows * gain_two_row[...] + shift_two_row[...]).astype(BF16)
        n2[rows, :] = normed
        left[:, rows] = normed.T

    each_field(norm_two)

    root = 0.7978845608028654

    def hidden_columns(part, column_block):
        return pl.multiple_of(column_block * (hidden_width // narrow) + part * chunk, chunk)

    def each_block(step):
        def body(column_block, carry):
            step(column_block)
            return carry

        lax.fori_loop(0, narrow, body, 0)

    def feed(part):
        def one(column_block):
            first = hidden_columns(part, column_block)
            columns = pl.ds(first, chunk)
            here = pl.ds(pl.multiple_of(column_block * chunk, chunk), chunk)
            hidden = dot(n2[...], w_a[:, columns]) + up_row[:, columns]
            pulled = dot_nt(cot[...], w_b[columns, :])
            square = hidden * hidden
            bent = jnp.tanh(hidden * (root + (root * 0.044715) * square))
            cdf = 0.5 + 0.5 * bent
            activated = (hidden * cdf).astype(BF16)
            slope = cdf + (hidden * (0.5 - 0.5 * bent * bent)) * (
                root + (3 * root * 0.044715) * square
            )
            grad = (pulled * slope).astype(BF16)
            acts[part, :, here] = activated
            hgrs[part, :, here] = grad
            act_t[columns, :] = activated.T
            up_sums[:, columns] = column_sums(grad.astype(F32))

        each_block(one)

    def feed_sums(part):
        def one(column_block):
            columns = pl.ds(hidden_columns(part, column_block), chunk)
            here = pl.ds(pl.multiple_of(column_block * chunk, chunk), chunk)
            acc[...] += dot(acts[part, :, here], w_b[columns, :])
            ngr[...] += dot_nt(hgrs[part, :, here], w_a[:, columns])

        each_block(one)

    def left_half(half):
        return left[pl.ds(pl.multiple_of(half * (model // 2), model // 2), model // 2), :]

    def up_unit(part):
        make_unit(part, left_half, lambda: hgrs[part])

    def down_unit(part):
        def rows(half):
            first = half * (hidden_width // 2) + part * block_rows
            return jnp.concatenate(
                [
                    act_t[
                        pl.ds(pl.multiple_of(first + block * 4 * block_rows, 16), block_rows), :
                    ]
                    for block in range(wide // 2)
                ],
                0,
            )

        make_unit(4 + part, rows, lambda: cot[...])

    def store_output(field):
        rows = field_rows(field)
        act[rows, :] = (mid[rows, :] + acc[rows, :] + down_row[...]).astype(BF16)

    output_copy = pltpu.make_async_copy(act, output_out, store_sem.at[0])
    tokens_copy = pltpu.make_async_copy(acc, tokens_out, store_sem.at[1])

    def add_sums(row, columns, rows):
        vec[pl.ds(row, 1), columns] += column_sums(rows)

    everything = pl.ds(0, model)

    def middle_back(field):
        rows = field_rows(field)
        unit_rows, scale = standardise(mid[rows, :])
        grads = ngr[rows, :]
        top = cot[rows, :].astype(F32)
        add_sums(7, everything, top)
        add_sums(10, everything, grads * unit_rows)
        add_sums(11, everything, grads)
        total = top + norm_back(unit_rows, scale, grads * gain_two_row[...])
        acc[rows, :] = total
        low = total.astype(BF16)
        hgr[rows, :] = low
        add_sums(2, everything, low.astype(F32))

    def attend_back(field, first_pair, last_pair):
        rows = field_rows(field)
        visible = visible_of(field)

        some = range(first_pair, last_pair)
        at = [pair_columns(pair) for pair in some]
        here = [pl.ds(pair * 128, 128) for pair in some]
        stacked = [stack_heads(qkv[rows, at_q], 0.125) for at_q, at_k, at_v in at]
        pulled = [stack_heads(act[rows, columns]) for columns in here]
        attention = soften(stacked, [qkv[rows, at_k] for at_q, at_k, at_v in at], visible)
        inner = [dot_nt(one, qkv[rows, at_v]) for one, (at_q, at_k, at_v) in zip(pulled, at)]
        inner = [
            one - jnp.sum(share * one, -1, keepdims=True) for share, one in zip(attention, inner)
        ]
        scores_grad = [(share * one).astype(BF16) for share, one in zip(attention, inner)]
        queries_grad = [
            (pick_heads(dot(one, qkv[rows, at_k])) * 0.125).astype(BF16)
            for one, (at_q, at_k, at_v) in zip(scores_grad, at)
        ]
        keys_grad = [dot_tn(one, rest).astype(BF16) for one, rest in zip(scores_grad, stacked)]
        values_grad = [
            dot_tn(one.astype(BF16), rest).astype(BF16) for one, rest in zip(attention, pulled)
        ]
        for number, (at_q, at_k, at_v) in enumerate(at):
            qkv[rows, at_q] = queries_grad[number]
            qkv[rows, at_k] = keys_grad[number]
            qkv[rows, at_v] = values_grad[number]
            add_sums(0, here[number], queries_grad[number].astype(F32))
            add_sums(1, here[number], values_grad[number].astype(F32))

    def turn(source):
        for field in range(fields):
            left[:, field_rows(field)] = source[field_rows(field), :].T

    def proj_unit():
        turn(att)
        make_unit(8, left_half, lambda: hgr[...])

    def qkv_unit(part):
        stride = 3 * model // narrow
        make_unit(
            9 + part,
            left_half,
            lambda: jnp.concatenate(
                [
                    qkv[:, pl.ds(block * stride + part * width, width)]
                    for block in range(narrow)
                ],
                1,
            ),
        )

    def source_back(field):
        rows = field_rows(field)
        unit_rows, scale = standardise(tok[rows, :].astype(F32))
        grads = ngr[rows, :]
        add_sums(8, everything, grads * unit_rows)
        add_sums(9, everything, grads)
        acc[rows, :] += norm_back(unit_rows, scale, grads * gain_one_row[...])

    def vec_copy(number):
        return remote(
            vec, vec_in.at[number], vec_send.at[number], vec_recv.at[number], all_bits[number]
        )

    def vec_end(number):
        vec_copy(number).wait()
        vec[...] += vec_in[number]
        if number + 1 < len(all_bits):
            vec_copy(number + 1).start()

    def make_attended_grad():
        output_copy.wait()
        act[...] = dot_nt(hgr[...], w_p[...]).astype(BF16)

    def finish_output():
        for number in range(hidden_width // model):
            vec[3 + number : 4 + number, :] = up_sums[:, number * model : (number + 1) * model]
        each_field(store_output)
        output_copy.start()

    qkv_again = pltpu.make_async_copy(qkv_in, w_a.at[:, pl.ds(0, 3 * model)], load_sem.at[1])

    def make_normed_grad(half):
        columns = pl.ds(half * (model // 2), model // 2)
        if half == 0:
            qkv_again.wait()
        ngr[:, columns] = dot_nt(qkv[...], w_a[columns, pl.ds(0, 3 * model)])

    def finish_tokens():
        each_field(source_back)
        tokens_copy.start()
        vec_copy(0).start()

    def some(step, *values):
        return lambda: step(*values)

    halves = [(0, pairs // 2), (pairs // 2, pairs)]
    backs = [
        some(attend_back, field, *half) for field in range(fields) for half in halves
    ]
    backs_at = {13: 1, 15: 1, 16: 1, 18: 1, 19: 1, 21: 1, 22: 2}
    work = {
        0: [some(feed, 2)],
        1: [some(feed_sums, 0)],
        2: [some(up_unit, 2)],
        3: [some(feed, 3)],
        5: [some(up_unit, 3)],
        6: [some(feed_sums, 1)],
        7: [some(feed_sums, 2)],
        8: [some(down_unit, 0)],
        9: [some(feed_sums, 3), qkv_again.start],
        10: [finish_output],
        11: [some(down_unit, 1)],
        12: [some(each_field, middle_back), make_attended_grad],
        14: [some(down_unit, 2)],
        17: [some(down_unit, 3)],
        20: [proj_unit],
        23: [some(turn, n1), some(qkv_unit, 0)],
        24: [some(make_normed_grad, 0)],
        25: [some(make_normed_grad, 1)],
        26: [some(qkv_unit, 1)],
        27: [finish_tokens],
        29: [some(qkv_unit, 2)],
    }
    for number, count in backs_at.items():
        work[number] = [backs.pop(0) for _ in range(count)]
    for number in range(len(all_bits)):
        work.setdefault(30 + 2 * number, []).append(some(vec_end, number))

    up_load.wait()
    down_load.wait()
    cot_load.wait()
    feed(0)
    pl.semaphore_wait(barrier, len(all_bits))
    up_unit(0)
    core_end(0)
    core_end(1)
    core_end(2)
    feed(1)
    up_unit(1)
    vec_store = pltpu.make_async_copy(vec, vec_out, store_sem.at[2])
    for number in range(parts + LAGS[-1]):
        steps = work.get(number, [])
        for step in steps[:FIRST]:
            step()
        tick(number, steps[FIRST:])
        if 0 <= number + LEAD < parts:
            core_end(number + LEAD)
        if number == 30 + 2 * (len(all_bits) - 1):
            vec_store.start()
    for copy in result_copies:
        copy.wait()
    tokens_copy.wait()
    vec_store.wait()


def place_results(*refs):
    arrays, vec_in, placed, vectors_out = refs[:6], refs[6], refs[7:13], refs[13:22]
    in_sem, out_sem, vec_sem, vec, *held = refs[22:]
    vectors, held = held[:9], held[9:]

    def pieces(ref):
        count = 4 if ref.shape[0] % 64 == 0 and ref.shape[0] >= 512 else 1
        size = ref.shape[0] // count
        return [pl.ds(number * size, size) for number in range(count)]

    moves = [
        (src.at[rows], mid.at[rows], dst.at[rows])
        for src, mid, dst in zip(arrays, held, placed)
        for rows in pieces(src)
    ]
    vec_copy = pltpu.make_async_copy(vec_in, vec, vec_sem.at[9])
    vec_copy.start()
    inward, outward = [], []
    for number, (src, mid, dst) in enumerate(moves):
        inward.append(pltpu.make_async_copy(src, mid, in_sem.at[number]))
        outward.append(pltpu.make_async_copy(mid, dst, out_sem.at[number]))
        inward[-1].start()
    vec_copy.wait()
    row = 0
    vec_outward = []
    for number, (vector, vector_out) in enumerate(zip(vectors, vectors_out)):
        model = vec.shape[1]
        for part in range(vector.shape[0] // model):
            vector[pl.ds(part * model, model)] = vec[row, :]
            row += 1
        vec_outward.append(pltpu.make_async_copy(vector, vector_out, vec_sem.at[number]))
        vec_outward[-1].start()
    for before, after in zip(inward, outward):
        before.wait()
        after.start()
    for copy in outward + vec_outward:
        copy.wait()


def local_fused(wide, narrow, *args):
    (
        tokens, land_mask, cotangent, qkv_weight, query_bias, value_bias, proj_weight, proj_bias,
        up_weight, up_bias, down_weight, down_bias, norm1_gain, norm1_shift, norm2_gain, norm2_shift,
    ) = args
    fields, patches, model = tokens.shape
    rows = fields * patches
    hidden_width = up_weight.shape[1]
    width, block_rows = model // narrow, model // wide
    bits = (wide * narrow).bit_length() - 1
    blocks = wide * narrow // 2
    group_rows = block_rows // 3
    gaps = [LEAD] + [LAGS[i] - LAGS[i - 1] for i in range(1, 4)]
    cycle = [2 * (gap + gap % 2) for gap in gaps]
    anywhere = pl.BlockSpec(memory_space=pl.ANY)

    def vmem(shape, dtype=F32):
        return pltpu.VMEM(shape, dtype)

    dma = pltpu.SemaphoreType.DMA
    vectors = [model] * 3 + [hidden_width] + [model] * 5
    results = pl.pallas_call(
        lambda *refs: layer_kernel(wide, narrow, fields, patches, *refs),
        out_shape=[
            jax.ShapeDtypeStruct((rows, model), BF16),
            jax.ShapeDtypeStruct((rows, model), F32),
            jax.ShapeDtypeStruct((block_rows, 3 * width), F32),
            jax.ShapeDtypeStruct((block_rows, width), F32),
            jax.ShapeDtypeStruct((block_rows, 4 * width), F32),
            jax.ShapeDtypeStruct((4 * block_rows, width), F32),
            jax.ShapeDtypeStruct((16, model), F32),
        ],
        in_specs=[anywhere] * 16,
        out_specs=[anywhere] * 7,
        scratch_shapes=[
            vmem((rows, model), BF16),
            vmem((rows, model), BF16),
            vmem((rows, model), BF16),
            vmem((rows, 3 * model), BF16),
            vmem((rows, model), BF16),
            vmem((rows, model)),
            vmem((rows, model), BF16),
            vmem((hidden_width, rows), BF16),
            vmem((4, rows, model), BF16),
            vmem((4, rows, model), BF16),
            vmem((rows, model)),
            vmem((rows, model)),
            vmem((model, rows), BF16),
            vmem((model, hidden_width), BF16),
            vmem((hidden_width, model), BF16),
            vmem((model, model), BF16),
            vmem((1, 3 * model)),
            vmem((8, hidden_width)),
            vmem((3 * SLOTS + 6, 3, blocks, group_rows, 128)),
            vmem((6, 3, blocks, group_rows, 128)),
            vmem((1, hidden_width)),
            vmem((block_rows, 4 * width)),
            vmem((4 * block_rows, width)),
            vmem((block_rows, width)),
            vmem((block_rows, 3 * width)),
            *[vmem((cycle[s], 3, blocks >> (s + 1), group_rows, 128)) for s in range(4)],
            vmem((16, model)),
            vmem((bits, 16, model)),
            dma((16,)),
            dma((6,)),
            dma((6,)),
            pltpu.SemaphoreType.REGULAR,
            dma((sum(gaps), 3)),
            dma((sum(cycle), 3)),
            dma((4,)),
            dma((bits,)),
            dma((bits,)),
            dma((3,)),
            vmem((fields, patches), jnp.int32),
            *[vmem((size,)) for size in vectors],
        ],
        compiler_params=pltpu.CompilerParams(
            collective_id=0, has_side_effects=True, vmem_limit_bytes=63 << 20
        ),
        name="encoder_layer",
    )(
        tokens.reshape(rows, model),
        cotangent.reshape(rows, model),
        qkv_weight,
        proj_weight,
        up_weight,
        down_weight,
        land_mask,
        query_bias,
        value_bias,
        proj_bias,
        up_bias,
        down_bias,
        norm1_gain,
        norm1_shift,
        norm2_gain,
        norm2_shift,
    )
    placed = pl.pallas_call(
        place_results,
        out_shape=[jax.ShapeDtypeStruct(array.shape, array.dtype) for array in results[:6]]
        + [jax.ShapeDtypeStruct((size,), F32) for size in vectors],
        in_specs=[anywhere] * 7,
        out_specs=[anywhere] * 15,
        scratch_shapes=[dma((12,)), dma((12,)), dma((10,)), vmem((16, model))]
        + [vmem((size,)) for size in vectors]
        + [vmem(array.shape, array.dtype) for array in results[:6]],
        name="place_results",
    )(*results)
    output, tokens_grad, qkv_grad, proj_grad, up_grad, down_grad = placed[:6]
    (
        query_grad, value_grad, proj_bias_grad, up_bias_grad, down_bias_grad,
        gain_one_grad, shift_one_grad, gain_two_grad, shift_two_grad,
    ) = placed[6:]
    return (
        output.reshape(tokens.shape),
        tokens_grad.reshape(tokens.shape),
        qkv_grad,
        query_grad,
        value_grad,
        proj_grad,
        proj_bias_grad,
        up_grad,
        up_bias_grad,
        down_grad,
        down_bias_grad,
        gain_one_grad,
        shift_one_grad,
        gain_two_grad,
        shift_two_grad,
    )


def layer_norm(inputs, norm_gain, norm_shift):
    average = jnp.mean(inputs, -1, keepdims=True)
    centred = inputs - average
    variance = jnp.mean(centred * centred, -1, keepdims=True)
    return centred * lax.rsqrt(variance + 1e-06) * norm_gain + norm_shift


def attend_scores(queries, key_rows, visible, scaling):
    scores = (
        jnp.einsum("fqhe,fkhe->fhqk", queries, key_rows, preferred_element_type=jnp.float32)
        * scaling
    )
    return jnp.where(visible[:, None, None, :], scores, -1e30)


def share_sums(former, latter):
    row_sums = (
        lax.psum_scatter(former, "wide", scatter_dimension=0, tiled=True),
        lax.psum_scatter(latter, "wide", scatter_dimension=0, tiled=True),
    )
    return (
        lax.psum_scatter(row_sums[0], "narrow", scatter_dimension=1, tiled=True),
        lax.psum_scatter(row_sums[1], "narrow", scatter_dimension=1, tiled=True),
    )


def local(
    tokens,
    land_mask,
    cotangent,
    qkv_weight,
    query_bias,
    value_bias,
    proj_weight,
    proj_bias,
    up_weight,
    up_bias,
    down_weight,
    down_bias,
    norm1_gain,
    norm1_shift,
    norm2_gain,
    norm2_shift,
):
    field_count, length, model_width = tokens.shape
    head_count = HEADS
    head_width = model_width // head_count
    scaling = head_width ** (-0.5)
    visible = land_mask > 0
    split_shape = (field_count, length, head_count, head_width)
    source = tokens.astype(jnp.float32)
    normed_one = layer_norm(source, norm1_gain, norm1_shift).astype(jnp.bfloat16)
    joint = jnp.einsum("fpd,de->fpe", normed_one, qkv_weight, preferred_element_type=jnp.float32)
    queries = (joint[..., :model_width] + query_bias).astype(jnp.bfloat16).reshape(split_shape)
    key_rows = joint[..., model_width : 2 * model_width].astype(jnp.bfloat16).reshape(split_shape)
    values = (joint[..., 2 * model_width :] + value_bias).astype(jnp.bfloat16).reshape(split_shape)
    scores = attend_scores(queries, key_rows, visible, scaling)
    highest = jnp.max(scores, -1, keepdims=True)
    exponent = jnp.exp(scores - highest)
    summed = jnp.sum(exponent, -1, keepdims=True)
    attention = exponent / summed
    log_total = highest + jnp.log(summed)
    attended = jnp.einsum(
        "fhqk,fkhe->fqhe",
        attention.astype(jnp.bfloat16),
        values,
        preferred_element_type=jnp.float32,
    )
    attended = attended.reshape(field_count, length, model_width).astype(jnp.bfloat16)
    middle = (
        source
        + jnp.einsum("fpd,de->fpe", attended, proj_weight, preferred_element_type=jnp.float32)
        + proj_bias
    )
    normed_two = layer_norm(middle, norm2_gain, norm2_shift).astype(jnp.bfloat16)
    hidden = (
        jnp.einsum("fpd,dn->fpn", normed_two, up_weight, preferred_element_type=jnp.float32)
        + up_bias
    )
    activated_full, gelu_pull = jax.vjp(jax.nn.gelu, hidden)
    activated = activated_full.astype(jnp.bfloat16)
    output = (
        middle
        + jnp.einsum("fpn,nd->fpd", activated, down_weight, preferred_element_type=jnp.float32)
        + down_bias
    )
    grad_out = cotangent.astype(jnp.float32)
    down_local = jnp.einsum("fpn,fpd->nd", activated, cotangent, preferred_element_type=jnp.float32)
    down_bias_local = jnp.sum(grad_out, axis=(0, 1))
    activated_grad = jnp.einsum(
        "fpd,nd->fpn", cotangent, down_weight, preferred_element_type=jnp.float32
    )
    hidden_grad = gelu_pull(activated_grad)[0].astype(jnp.bfloat16)
    up_local = jnp.einsum(
        "fpd,fpn->dn", normed_two, hidden_grad, preferred_element_type=jnp.float32
    )
    up_bias_local = jnp.sum(hidden_grad.astype(jnp.float32), axis=(0, 1))
    feed_sums = share_sums(up_local, down_local)
    normed_two_grad = jnp.einsum(
        "fpn,dn->fpd", hidden_grad, up_weight, preferred_element_type=jnp.float32
    )
    unused_two, norm_two_pull = jax.vjp(layer_norm, middle, norm2_gain, norm2_shift)
    middle_part, gain_two_local, shift_two_local = norm_two_pull(normed_two_grad)
    middle_grad = grad_out + middle_part
    middle_low = middle_grad.astype(jnp.bfloat16)
    proj_local = jnp.einsum("fpd,fpe->de", attended, middle_low, preferred_element_type=jnp.float32)
    proj_bias_local = jnp.sum(middle_low.astype(jnp.float32), axis=(0, 1))
    attended_grad = jnp.einsum(
        "fpe,de->fpd", middle_low, proj_weight, preferred_element_type=jnp.float32
    )
    attended_grad = attended_grad.astype(jnp.bfloat16).reshape(split_shape)
    scores = attend_scores(queries, key_rows, visible, scaling)
    attention = jnp.exp(scores - log_total)
    values_grad = jnp.einsum(
        "fhqk,fqhe->fkhe",
        attention.astype(jnp.bfloat16),
        attended_grad,
        preferred_element_type=jnp.float32,
    )
    attention_grad = jnp.einsum(
        "fqhe,fkhe->fhqk", attended_grad, values, preferred_element_type=jnp.float32
    )
    inner_sum = jnp.sum(attention * attention_grad, -1, keepdims=True)
    scores_grad = (attention * (attention_grad - inner_sum)).astype(jnp.bfloat16)
    queries_grad = (
        jnp.einsum("fhqk,fkhe->fqhe", scores_grad, key_rows, preferred_element_type=jnp.float32)
        * scaling
    )
    keys_grad = (
        jnp.einsum("fhqk,fqhe->fkhe", scores_grad, queries, preferred_element_type=jnp.float32)
        * scaling
    )
    flat_shape = (field_count, length, model_width)
    joint_grad = jnp.concatenate(
        [
            queries_grad.reshape(flat_shape),
            keys_grad.reshape(flat_shape),
            values_grad.reshape(flat_shape),
        ],
        -1,
    ).astype(jnp.bfloat16)
    qkv_local = jnp.einsum(
        "fpd,fpe->de", normed_one, joint_grad, preferred_element_type=jnp.float32
    )
    joint_sums = jnp.sum(joint_grad.astype(jnp.float32), axis=(0, 1))
    query_bias_local = joint_sums[:model_width]
    value_bias_local = joint_sums[2 * model_width :]
    attention_sums = share_sums(qkv_local, proj_local)
    normed_one_grad = jnp.einsum(
        "fpe,de->fpd", joint_grad, qkv_weight, preferred_element_type=jnp.float32
    )
    unused_one, norm_one_pull = jax.vjp(layer_norm, source, norm1_gain, norm1_shift)
    source_part, gain_one_local, shift_one_local = norm_one_pull(normed_one_grad)
    tokens_grad = middle_grad + source_part
    vectors = lax.psum(
        (
            query_bias_local,
            value_bias_local,
            proj_bias_local,
            up_bias_local,
            down_bias_local,
            gain_one_local,
            shift_one_local,
            gain_two_local,
            shift_two_local,
        ),
        ("wide", "narrow"),
    )
    return (
        output.astype(jnp.bfloat16),
        tokens_grad,
        attention_sums[0],
        vectors[0],
        vectors[1],
        attention_sums[1],
        vectors[2],
        feed_sums[0],
        vectors[3],
        feed_sums[1],
        vectors[4],
        vectors[5],
        vectors[6],
        vectors[7],
        vectors[8],
    )


def solution(mesh):
    wide, narrow = mesh.shape["wide"], mesh.shape["narrow"]
    placed = (
        P(("wide", "narrow"), None, None),
        P(("wide", "narrow"), None),
        P(("wide", "narrow"), None, None),
        P(),
        P(),
        P(),
        P(),
        P(),
        P(),
        P(),
        P(),
        P(),
        P(),
        P(),
        P(),
        P(),
    )
    fused = (wide, narrow) == (16, 2)

    def layer(*args):
        return local_fused(wide, narrow, *args) if fused else local(*args)

    return jax.shard_map(
        layer,
        mesh=mesh,
        in_specs=placed,
        out_specs=(
            P(("wide", "narrow"), None, None),
            P(("wide", "narrow"), None, None),
            P("wide", "narrow"),
            P(),
            P(),
            P("wide", "narrow"),
            P(),
            P("wide", "narrow"),
            P(),
            P("wide", "narrow"),
            P(),
            P(),
            P(),
            P(),
            P(),
        ),
        check_vma=False,
    )
```

```python
import jax
import jax.numpy as jnp
from jax import lax
from jax.experimental import pallas as pl
from jax.experimental.pallas import tpu as pltpu
from jax.sharding import PartitionSpec as P

HEADS = 12
F32 = jnp.float32
BF16 = jnp.bfloat16
SLOTS = 6
LAGS = (0, 2, 4, 6)
LEAD = 3
FIRST = 9


def dot(a, b):
    return lax.dot_general(a, b, (((1,), (0,)), ((), ())), preferred_element_type=F32)


def dot_nt(a, b):
    return lax.dot_general(a, b, (((1,), (1,)), ((), ())), preferred_element_type=F32)


def dot_tn(a, b):
    return lax.dot_general(a, b, (((0,), (0,)), ((), ())), preferred_element_type=F32)


def standardise(rows):
    centred = rows - jnp.mean(rows, -1, keepdims=True)
    scale = lax.rsqrt(jnp.mean(centred * centred, -1, keepdims=True) + 1e-06)
    return centred * scale, scale


def norm_back(unit_rows, scale, pulled):
    return scale * (
        pulled
        - jnp.mean(pulled, -1, keepdims=True)
        - unit_rows * jnp.mean(pulled * unit_rows, -1, keepdims=True)
    )


def column_sums(rows):
    return jnp.sum(rows, axis=0, keepdims=True)


def layer_kernel(wide, narrow, fields, patches, *refs):
    (
        tokens_in, cotangent_in, qkv_in, proj_in, up_in, down_in, land_in,
    ) = refs[:7]
    vectors_in, refs = refs[7:16], refs[16:]
    (
        output_out, tokens_out, qkv_out, proj_out, up_out, down_out, vec_out,
        tok, cot, n1, qkv, att, mid, n2, act_t, acts, hgrs, acc, ngr, left, w_a, w_b, w_p, qkv_bias, flat,
        keep, core_in, up_sums, up_sum, down_sum, proj_sum, qkv_sum, in_0, in_1, in_2, in_3, vec, vec_in,
        load_sem, core_send, core_recv, core_free, stage_send, stage_recv, final_sem,
        vec_send, vec_recv, store_sem, land,
    ) = refs[:-9]
    vectors_held = refs[-9:]
    (
        query_bias, value_bias, proj_bias, up_bias, down_bias,
        gain_one, shift_one, gain_two, shift_two,
    ) = vectors_held
    model = tok.shape[1]
    hidden_width = w_a.shape[1]
    stage_in = (in_0, in_1, in_2, in_3)
    act, hgr = acts.at[0], hgrs.at[0]
    at_wide = lax.axis_index("wide")
    at_narrow = lax.axis_index("narrow")
    width = model // narrow
    block_rows = model // wide
    group_rows = block_rows // 3
    chunk = width
    parts = 36

    def my_bit(axis, level):
        index = at_wide if axis == "wide" else at_narrow
        return lax.rem(lax.div(index, 1 << level), 2)

    def partner(axis, level):
        shift = (1 << level) * (1 - 2 * my_bit(axis, level))
        if axis == "wide":
            return (at_wide + shift, at_narrow)
        return (at_wide, at_narrow + shift)

    wide_bits = [("wide", i) for i in range(1, wide.bit_length() - 1)]
    narrow_bits = [("narrow", i) for i in range(narrow.bit_length() - 1)]
    all_bits = [("wide", 0)] + wide_bits + narrow_bits
    stages = len(wide_bits) + len(narrow_bits)
    blocks = 1 << stages
    core = my_bit("wide", 0)
    mine = {bit: my_bit(*bit) for bit in all_bits}
    to = {bit: partner(*bit) for bit in all_bits}

    def order(part, group):
        if group == 0:
            return narrow_bits + wide_bits
        if group == 1:
            return wide_bits[:1] + narrow_bits + wide_bits[1:]
        if part % 2 == 0:
            return wide_bits[1:2] + narrow_bits + wide_bits[:1] + wide_bits[2:]
        return wide_bits[1:2] + wide_bits[:1] + narrow_bits + wide_bits[2:]

    def place(part, group, row_block, column_block):
        found = 0
        for axis, level in order(part, group):
            index = row_block if axis == "wide" else column_block
            found = 2 * found + ((index >> level) & 1)
        return found

    barrier = pltpu.get_barrier_semaphore()
    for bit in all_bits:
        pl.semaphore_signal(
            barrier, inc=1, device_id=to[bit], device_id_type=pl.DeviceIdType.MESH
        )

    def remote(src, dst, send, recv, bit):
        return pltpu.make_async_remote_copy(
            src_ref=src, dst_ref=dst, send_sem=send, recv_sem=recv,
            device_id=to[bit], device_id_type=pl.DeviceIdType.MESH,
        )

    def kept_slot(part):
        return part % (3 * SLOTS)

    def sent_slot(part):
        return 3 * SLOTS + part % 6

    def core_copy(part):
        slot = part % 6
        return remote(
            keep.at[sent_slot(part)], core_in.at[slot],
            core_send.at[slot], core_recv.at[slot], ("wide", 0),
        )

    def core_start(part):
        if part >= 6:
            pl.semaphore_wait(core_free, 1)
        core_copy(part).start()

    def span(part, group, stage):
        half = blocks >> (stage + 1)
        sequence = order(part, group)
        base = 0
        for earlier in range(stage):
            base = base + mine[sequence[earlier]] * (blocks >> (earlier + 1))
        bit = sequence[stage]
        return half, base + mine[bit] * half, base + (1 - mine[bit]) * half, bit

    gaps = [LEAD] + [LAGS[i] - LAGS[i - 1] for i in range(1, 4)]
    cycle = [2 * (gap + gap % 2) for gap in gaps]

    def stage_copy(part, group, stage):
        half, own, other, bit = span(part, group, stage)
        sent = sum(gaps[:stage]) + part % gaps[stage]
        held = sum(cycle[:stage]) + part % cycle[stage]
        return remote(
            keep.at[kept_slot(part), group, pl.ds(other, half)],
            stage_in[stage].at[part % cycle[stage], group],
            stage_send.at[sent, group],
            stage_recv.at[held, group],
            bit,
        )

    def core_end(part):
        slot = part % 6
        core_copy(part).wait()
        for group in range(3):
            keep[kept_slot(part), group] += core_in[slot, group]
            stage_copy(part, group, 0).start()
        if part + 6 < parts:
            pl.semaphore_signal(
                core_free, inc=1, device_id=to[("wide", 0)],
                device_id_type=pl.DeviceIdType.MESH,
            )

    def result_place(part, group):
        unit, row = part // 3, (part % 3) * group_rows
        if unit < 4:
            return up_sum, row, unit * width + group * 128
        if unit < 8:
            return down_sum, (unit - 4) * block_rows + row, group * 128
        if unit == 8:
            return proj_sum, row, group * 128
        return qkv_sum, row, (unit - 9) * width + group * 128

    def stage_end(part, stage):
        for group in range(3):
            stage_copy(part, group, stage).wait()
            half, own, other, bit = span(part, group, stage)
            slot, came = kept_slot(part), stage_in[stage].at[part % cycle[stage], group]
            if stage + 1 < stages:
                keep[slot, group, pl.ds(own, half)] += came[...]
                stage_copy(part, group, stage + 1).start()
            else:
                ref, row, column = result_place(part, group)
                ref[row : row + group_rows, column : column + 128] = (
                    keep[slot, group, own] + came[0]
                )

    result_copies = [
        pltpu.make_async_copy(src, dst, final_sem.at[number])
        for number, (src, dst) in enumerate(
            ((up_sum, up_out), (down_sum, down_out), (proj_sum, proj_out), (qkv_sum, qkv_out))
        )
    ]
    last_part = {11: 0, 23: 1, 26: 2, 35: 3}

    def tick(number, between=()):
        for stage in reversed(range(stages)):
            if stage == 1:
                for step in between:
                    step()
            part = number - LAGS[stage]
            if 0 <= part < parts:
                stage_end(part, stage)
                if stage + 1 == stages and part in last_part:
                    result_copies[last_part[part]].start()

    def make_unit(unit, lhs_half, rhs):
        half_blocks = wide // 2

        def one(half, carry):
            product = dot(lhs_half(half), rhs())
            for third in range(3):
                part = 3 * unit + third
                kept, sent = kept_slot(part), sent_slot(part)
                index = [kept + core * (sent - kept), sent + core * (kept - sent)]
                for row_block in range(half_blocks):
                    top = row_block * block_rows + third * group_rows
                    for column_block in range(narrow):
                        for group in range(3):
                            first = place(part, group, row_block, column_block)
                            step = place(part, group, half_blocks, 0)
                            side = column_block * width + group * 128
                            keep[index[row_block % 2], group, first + half * step] = product[
                                top : top + group_rows, side : side + 128
                            ]
            return carry

        lax.fori_loop(0, 2, one, 0)
        for third in range(3):
            core_start(3 * unit + third)

    def row_of(vector):
        return vector[...].reshape(1, vector.shape[0])

    def load(src, dst, number):
        copy = pltpu.make_async_copy(src, dst, load_sem.at[number])
        copy.start()
        return copy

    tok_load = load(tokens_in, tok, 0)
    small_loads = [load(land_in, land, 6)] + [
        load(src, dst, 7 + number)
        for number, (src, dst) in enumerate(zip(vectors_in, vectors_held))
    ]
    thirds = [pl.ds(number * model, model) for number in range(3)]
    qkv_loads = [
        load(qkv_in.at[:, columns], w_a.at[:, columns], number)
        for columns, number in zip(thirds, (1, 16, 17))
    ]
    vec[...] = jnp.zeros_like(vec)
    acc[...] = jnp.zeros_like(acc)
    ngr[...] = jnp.zeros_like(ngr)
    for small in small_loads:
        small.wait()
    qkv_bias[:, 0:model] = row_of(query_bias)
    qkv_bias[:, model : 2 * model] = jnp.zeros((1, model), F32)
    qkv_bias[:, 2 * model :] = row_of(value_bias)
    for number, vector in enumerate(
        (proj_bias, down_bias, gain_one, shift_one, gain_two, shift_two)
    ):
        flat[number : number + 1, 0:model] = row_of(vector)
    flat[6:7, :] = row_of(up_bias)

    def field_rows(field):
        return pl.ds(pl.multiple_of(field * patches, patches), patches)

    def each_field(step):
        def body(field, carry):
            step(field)
            return carry

        lax.fori_loop(0, fields, body, 0)

    tok_load.wait()
    at_model = pl.ds(0, model)
    proj_row, down_row, gain_one_row, shift_one_row, gain_two_row, shift_two_row = (
        flat.at[pl.ds(number, 1), at_model] for number in range(6)
    )
    up_row = flat.at[pl.ds(6, 1), :]

    def norm_one(field):
        rows = field_rows(field)
        unit_rows, scale = standardise(tok[rows, :].astype(F32))
        n1[rows, :] = (unit_rows * gain_one_row[...] + shift_one_row[...]).astype(BF16)

    each_field(norm_one)
    later_loads = []
    for number, columns in enumerate(thirds):
        qkv_loads[number].wait()
        if number == 2:
            later_loads += [load(proj_in, w_p, 2), load(cotangent_in, cot, 3), load(down_in, w_b, 4)]
        qkv[:, columns] = (dot(n1[...], w_a[:, columns]) + qkv_bias[:, columns]).astype(BF16)
    proj_load, cot_load, down_load = later_loads
    up_load = load(up_in, w_a, 5)

    lane = lax.broadcasted_iota(jnp.int32, (1, 128), 1)
    head_masks = [(lane < 64).astype(BF16), (lane >= 64).astype(BF16)]
    lane_full = lax.broadcasted_iota(jnp.int32, (patches, 128), 1)
    pairs = model // 128

    def stack_heads(rows, factor=1.0):
        return jnp.concatenate([rows * (mask * BF16(factor)) for mask in head_masks], 0)

    def pick_heads(rows):
        return jnp.where(lane_full < 64, rows[:patches], rows[patches:])

    def soften(stacked, key_rows, visible):
        scores = [dot_nt(one, keys) for one, keys in zip(stacked, key_rows)]
        scores = [jnp.where(visible, one, -1e30) for one in scores]
        tops = [jnp.max(one, -1, keepdims=True) for one in scores]
        exponents = [jnp.exp(one - top) for one, top in zip(scores, tops)]
        shares = [1.0 / jnp.sum(one, -1, keepdims=True) for one in exponents]
        return [one * share for one, share in zip(exponents, shares)]

    def pair_columns(pair):
        return [pl.ds(part * model + pair * 128, 128) for part in range(3)]

    def visible_of(field):
        return jnp.broadcast_to(land[pl.ds(field, 1), :], (2 * patches, patches)) > 0

    def attend(field):
        rows = field_rows(field)
        visible = visible_of(field)
        at = [pair_columns(pair) for pair in range(pairs)]
        stacked = [stack_heads(qkv[rows, at_q], 0.125) for at_q, at_k, at_v in at]
        attention = soften(stacked, [qkv[rows, at_k] for at_q, at_k, at_v in at], visible)
        both = [
            dot(one.astype(BF16), qkv[rows, at_v])
            for one, (at_q, at_k, at_v) in zip(attention, at)
        ]
        for pair in range(pairs):
            att[rows, pl.ds(pair * 128, 128)] = pick_heads(both[pair]).astype(BF16)

    each_field(attend)
    proj_load.wait()

    def residual(tile, carry):
        columns = pl.ds(pl.multiple_of(tile * 256, 256), 256)
        mid[:, columns] = (
            tok[:, columns].astype(F32) + dot(att[...], w_p[:, columns]) + proj_row[:, columns]
        )
        return carry

    lax.fori_loop(0, model // 256, residual, 0)

    def norm_two(field):
        rows = field_rows(field)
        unit_rows, scale = standardise(mid[rows, :])
        normed = (unit_rows * gain_two_row[...] + shift_two_row[...]).astype(BF16)
        n2[rows, :] = normed
        left[:, rows] = normed.T

    each_field(norm_two)

    root = 0.7978845608028654

    def hidden_columns(part, column_block):
        return pl.multiple_of(column_block * (hidden_width // narrow) + part * chunk, chunk)

    def each_block(step):
        def body(column_block, carry):
            step(column_block)
            return carry

        lax.fori_loop(0, narrow, body, 0)

    def feed(part):
        def one(column_block):
            first = hidden_columns(part, column_block)
            columns = pl.ds(first, chunk)
            here = pl.ds(pl.multiple_of(column_block * chunk, chunk), chunk)
            hidden = dot(n2[...], w_a[:, columns]) + up_row[:, columns]
            pulled = dot_nt(cot[...], w_b[columns, :])
            square = hidden * hidden
            bent = jnp.tanh(hidden * (root + (root * 0.044715) * square))
            cdf = 0.5 + 0.5 * bent
            activated = (hidden * cdf).astype(BF16)
            slope = cdf + (hidden * (0.5 - 0.5 * bent * bent)) * (
                root + (3 * root * 0.044715) * square
            )
            grad = (pulled * slope).astype(BF16)
            acts[part, :, here] = activated
            hgrs[part, :, here] = grad
            act_t[columns, :] = activated.T
            up_sums[:, columns] = column_sums(grad.astype(F32))

        each_block(one)

    def feed_sums(part):
        def one(column_block):
            columns = pl.ds(hidden_columns(part, column_block), chunk)
            here = pl.ds(pl.multiple_of(column_block * chunk, chunk), chunk)
            acc[...] += dot(acts[part, :, here], w_b[columns, :])
            ngr[...] += dot_nt(hgrs[part, :, here], w_a[:, columns])

        each_block(one)

    def left_half(half):
        return left[pl.ds(pl.multiple_of(half * (model // 2), model // 2), model // 2), :]

    def up_unit(part):
        make_unit(part, left_half, lambda: hgrs[part])

    def down_unit(part):
        def rows(half):
            first = half * (hidden_width // 2) + part * block_rows
            return jnp.concatenate(
                [
                    act_t[
                        pl.ds(pl.multiple_of(first + block * 4 * block_rows, 16), block_rows), :
                    ]
                    for block in range(wide // 2)
                ],
                0,
            )

        make_unit(4 + part, rows, lambda: cot[...])

    def store_output(field):
        rows = field_rows(field)
        act[rows, :] = (mid[rows, :] + acc[rows, :] + down_row[...]).astype(BF16)

    output_copy = pltpu.make_async_copy(act, output_out, store_sem.at[0])
    tokens_copy = pltpu.make_async_copy(acc, tokens_out, store_sem.at[1])

    def add_sums(row, columns, rows):
        vec[pl.ds(row, 1), columns] += column_sums(rows)

    everything = pl.ds(0, model)

    def middle_back(field):
        rows = field_rows(field)
        unit_rows, scale = standardise(mid[rows, :])
        grads = ngr[rows, :]
        top = cot[rows, :].astype(F32)
        add_sums(7, everything, top)
        add_sums(10, everything, grads * unit_rows)
        add_sums(11, everything, grads)
        total = top + norm_back(unit_rows, scale, grads * gain_two_row[...])
        acc[rows, :] = total
        low = total.astype(BF16)
        hgr[rows, :] = low
        add_sums(2, everything, low.astype(F32))

    def attend_back(field, first_pair, last_pair):
        rows = field_rows(field)
        visible = visible_of(field)

        some = range(first_pair, last_pair)
        at = [pair_columns(pair) for pair in some]
        here = [pl.ds(pair * 128, 128) for pair in some]
        stacked = [stack_heads(qkv[rows, at_q], 0.125) for at_q, at_k, at_v in at]
        pulled = [stack_heads(act[rows, columns]) for columns in here]
        attention = soften(stacked, [qkv[rows, at_k] for at_q, at_k, at_v in at], visible)
        inner = [dot_nt(one, qkv[rows, at_v]) for one, (at_q, at_k, at_v) in zip(pulled, at)]
        inner = [
            one - jnp.sum(share * one, -1, keepdims=True) for share, one in zip(attention, inner)
        ]
        scores_grad = [(share * one).astype(BF16) for share, one in zip(attention, inner)]
        queries_grad = [
            (pick_heads(dot(one, qkv[rows, at_k])) * 0.125).astype(BF16)
            for one, (at_q, at_k, at_v) in zip(scores_grad, at)
        ]
        keys_grad = [dot_tn(one, rest).astype(BF16) for one, rest in zip(scores_grad, stacked)]
        values_grad = [
            dot_tn(one.astype(BF16), rest).astype(BF16) for one, rest in zip(attention, pulled)
        ]
        for number, (at_q, at_k, at_v) in enumerate(at):
            qkv[rows, at_q] = queries_grad[number]
            qkv[rows, at_k] = keys_grad[number]
            qkv[rows, at_v] = values_grad[number]
            add_sums(0, here[number], queries_grad[number].astype(F32))
            add_sums(1, here[number], values_grad[number].astype(F32))

    def turn(source):
        for field in range(fields):
            left[:, field_rows(field)] = source[field_rows(field), :].T

    def proj_unit():
        turn(att)
        make_unit(8, left_half, lambda: hgr[...])

    def qkv_unit(part):
        stride = 3 * model // narrow
        make_unit(
            9 + part,
            left_half,
            lambda: jnp.concatenate(
                [
                    qkv[:, pl.ds(block * stride + part * width, width)]
                    for block in range(narrow)
                ],
                1,
            ),
        )

    def source_back(field):
        rows = field_rows(field)
        unit_rows, scale = standardise(tok[rows, :].astype(F32))
        grads = ngr[rows, :]
        add_sums(8, everything, grads * unit_rows)
        add_sums(9, everything, grads)
        acc[rows, :] += norm_back(unit_rows, scale, grads * gain_one_row[...])

    def vec_copy(number):
        return remote(
            vec, vec_in.at[number], vec_send.at[number], vec_recv.at[number], all_bits[number]
        )

    def vec_end(number):
        vec_copy(number).wait()
        vec[...] += vec_in[number]
        if number + 1 < len(all_bits):
            vec_copy(number + 1).start()

    def make_attended_grad():
        output_copy.wait()
        act[...] = dot_nt(hgr[...], w_p[...]).astype(BF16)

    def finish_output():
        for number in range(hidden_width // model):
            vec[3 + number : 4 + number, :] = up_sums[:, number * model : (number + 1) * model]
        each_field(store_output)
        output_copy.start()

    qkv_again = pltpu.make_async_copy(qkv_in, w_a.at[:, pl.ds(0, 3 * model)], load_sem.at[1])

    def make_normed_grad(half):
        columns = pl.ds(half * (model // 2), model // 2)
        if half == 0:
            qkv_again.wait()
        ngr[:, columns] = dot_nt(qkv[...], w_a[columns, pl.ds(0, 3 * model)])

    def finish_tokens():
        each_field(source_back)
        tokens_copy.start()
        vec_copy(0).start()

    def some(step, *values):
        return lambda: step(*values)

    halves = [(0, pairs // 2), (pairs // 2, pairs)]
    backs = [
        some(attend_back, field, *half) for field in range(fields) for half in halves
    ]
    backs_at = {13: 1, 15: 1, 16: 1, 18: 1, 19: 1, 21: 1, 22: 2}
    work = {
        0: [some(feed, 2)],
        1: [some(feed_sums, 0)],
        2: [some(up_unit, 2)],
        3: [some(feed, 3)],
        5: [some(up_unit, 3)],
        6: [some(feed_sums, 1)],
        7: [some(feed_sums, 2)],
        8: [some(down_unit, 0)],
        9: [some(feed_sums, 3), qkv_again.start],
        10: [finish_output],
        11: [some(down_unit, 1)],
        12: [some(each_field, middle_back), make_attended_grad],
        14: [some(down_unit, 2)],
        17: [some(down_unit, 3)],
        20: [proj_unit],
        23: [some(turn, n1), some(qkv_unit, 0)],
        24: [some(make_normed_grad, 0)],
        25: [some(make_normed_grad, 1)],
        26: [some(qkv_unit, 1)],
        27: [finish_tokens],
        29: [some(qkv_unit, 2)],
    }
    for number, count in backs_at.items():
        work[number] = [backs.pop(0) for _ in range(count)]
    for number in range(len(all_bits)):
        work.setdefault(30 + 2 * number, []).append(some(vec_end, number))

    up_load.wait()
    down_load.wait()
    cot_load.wait()
    feed(0)
    pl.semaphore_wait(barrier, len(all_bits))
    up_unit(0)
    feed(1)
    core_end(0)
    core_end(1)
    core_end(2)
    up_unit(1)
    vec_store = pltpu.make_async_copy(vec, vec_out, store_sem.at[2])
    for number in range(parts + LAGS[-1]):
        steps = work.get(number, [])
        for step in steps[:FIRST]:
            step()
        tick(number, steps[FIRST:])
        if 0 <= number + LEAD < parts:
            core_end(number + LEAD)
        if number == 30 + 2 * (len(all_bits) - 1):
            vec_store.start()
    for copy in result_copies:
        copy.wait()
    tokens_copy.wait()
    vec_store.wait()


def place_results(*refs):
    arrays, vec_in, placed, vectors_out = refs[:6], refs[6], refs[7:13], refs[13:22]
    in_sem, out_sem, vec_sem, vec, *held = refs[22:]
    vectors, held = held[:9], held[9:]

    def pieces(ref):
        count = 4 if ref.shape[0] % 64 == 0 and ref.shape[0] >= 512 else 1
        size = ref.shape[0] // count
        return [pl.ds(number * size, size) for number in range(count)]

    moves = [
        (src.at[rows], mid.at[rows], dst.at[rows])
        for src, mid, dst in zip(arrays, held, placed)
        for rows in pieces(src)
    ]
    vec_copy = pltpu.make_async_copy(vec_in, vec, vec_sem.at[9])
    vec_copy.start()
    inward, outward = [], []
    for number, (src, mid, dst) in enumerate(moves):
        inward.append(pltpu.make_async_copy(src, mid, in_sem.at[number]))
        outward.append(pltpu.make_async_copy(mid, dst, out_sem.at[number]))
        inward[-1].start()
    vec_copy.wait()
    row = 0
    vec_outward = []
    for number, (vector, vector_out) in enumerate(zip(vectors, vectors_out)):
        model = vec.shape[1]
        for part in range(vector.shape[0] // model):
            vector[pl.ds(part * model, model)] = vec[row, :]
            row += 1
        vec_outward.append(pltpu.make_async_copy(vector, vector_out, vec_sem.at[number]))
        vec_outward[-1].start()
    for before, after in zip(inward, outward):
        before.wait()
        after.start()
    for copy in outward + vec_outward:
        copy.wait()


def local_fused(wide, narrow, *args):
    (
        tokens, land_mask, cotangent, qkv_weight, query_bias, value_bias, proj_weight, proj_bias,
        up_weight, up_bias, down_weight, down_bias, norm1_gain, norm1_shift, norm2_gain, norm2_shift,
    ) = args
    fields, patches, model = tokens.shape
    rows = fields * patches
    hidden_width = up_weight.shape[1]
    width, block_rows = model // narrow, model // wide
    bits = (wide * narrow).bit_length() - 1
    blocks = wide * narrow // 2
    group_rows = block_rows // 3
    gaps = [LEAD] + [LAGS[i] - LAGS[i - 1] for i in range(1, 4)]
    cycle = [2 * (gap + gap % 2) for gap in gaps]
    anywhere = pl.BlockSpec(memory_space=pl.ANY)

    def vmem(shape, dtype=F32):
        return pltpu.VMEM(shape, dtype)

    dma = pltpu.SemaphoreType.DMA
    vectors = [model] * 3 + [hidden_width] + [model] * 5
    results = pl.pallas_call(
        lambda *refs: layer_kernel(wide, narrow, fields, patches, *refs),
        out_shape=[
            jax.ShapeDtypeStruct((rows, model), BF16),
            jax.ShapeDtypeStruct((rows, model), F32),
            jax.ShapeDtypeStruct((block_rows, 3 * width), F32),
            jax.ShapeDtypeStruct((block_rows, width), F32),
            jax.ShapeDtypeStruct((block_rows, 4 * width), F32),
            jax.ShapeDtypeStruct((4 * block_rows, width), F32),
            jax.ShapeDtypeStruct((16, model), F32),
        ],
        in_specs=[anywhere] * 16,
        out_specs=[anywhere] * 7,
        scratch_shapes=[
            vmem((rows, model), BF16),
            vmem((rows, model), BF16),
            vmem((rows, model), BF16),
            vmem((rows, 3 * model), BF16),
            vmem((rows, model), BF16),
            vmem((rows, model)),
            vmem((rows, model), BF16),
            vmem((hidden_width, rows), BF16),
            vmem((4, rows, model), BF16),
            vmem((4, rows, model), BF16),
            vmem((rows, model)),
            vmem((rows, model)),
            vmem((model, rows), BF16),
            vmem((model, hidden_width), BF16),
            vmem((hidden_width, model), BF16),
            vmem((model, model), BF16),
            vmem((1, 3 * model)),
            vmem((8, hidden_width)),
            vmem((3 * SLOTS + 6, 3, blocks, group_rows, 128)),
            vmem((6, 3, blocks, group_rows, 128)),
            vmem((1, hidden_width)),
            vmem((block_rows, 4 * width)),
            vmem((4 * block_rows, width)),
            vmem((block_rows, width)),
            vmem((block_rows, 3 * width)),
            *[vmem((cycle[s], 3, blocks >> (s + 1), group_rows, 128)) for s in range(4)],
            vmem((16, model)),
            vmem((bits, 16, model)),
            dma((18,)),
            dma((6,)),
            dma((6,)),
            pltpu.SemaphoreType.REGULAR,
            dma((sum(gaps), 3)),
            dma((sum(cycle), 3)),
            dma((4,)),
            dma((bits,)),
            dma((bits,)),
            dma((3,)),
            vmem((fields, patches), jnp.int32),
            *[vmem((size,)) for size in vectors],
        ],
        compiler_params=pltpu.CompilerParams(
            collective_id=0, has_side_effects=True, vmem_limit_bytes=63 << 20
        ),
        name="encoder_layer",
    )(
        tokens.reshape(rows, model),
        cotangent.reshape(rows, model),
        qkv_weight,
        proj_weight,
        up_weight,
        down_weight,
        land_mask,
        query_bias,
        value_bias,
        proj_bias,
        up_bias,
        down_bias,
        norm1_gain,
        norm1_shift,
        norm2_gain,
        norm2_shift,
    )
    placed = pl.pallas_call(
        place_results,
        out_shape=[jax.ShapeDtypeStruct(array.shape, array.dtype) for array in results[:6]]
        + [jax.ShapeDtypeStruct((size,), F32) for size in vectors],
        in_specs=[anywhere] * 7,
        out_specs=[anywhere] * 15,
        scratch_shapes=[dma((12,)), dma((12,)), dma((10,)), vmem((16, model))]
        + [vmem((size,)) for size in vectors]
        + [vmem(array.shape, array.dtype) for array in results[:6]],
        name="place_results",
    )(*results)
    output, tokens_grad, qkv_grad, proj_grad, up_grad, down_grad = placed[:6]
    (
        query_grad, value_grad, proj_bias_grad, up_bias_grad, down_bias_grad,
        gain_one_grad, shift_one_grad, gain_two_grad, shift_two_grad,
    ) = placed[6:]
    return (
        output.reshape(tokens.shape),
        tokens_grad.reshape(tokens.shape),
        qkv_grad,
        query_grad,
        value_grad,
        proj_grad,
        proj_bias_grad,
        up_grad,
        up_bias_grad,
        down_grad,
        down_bias_grad,
        gain_one_grad,
        shift_one_grad,
        gain_two_grad,
        shift_two_grad,
    )


def layer_norm(inputs, norm_gain, norm_shift):
    average = jnp.mean(inputs, -1, keepdims=True)
    centred = inputs - average
    variance = jnp.mean(centred * centred, -1, keepdims=True)
    return centred * lax.rsqrt(variance + 1e-06) * norm_gain + norm_shift


def attend_scores(queries, key_rows, visible, scaling):
    scores = (
        jnp.einsum("fqhe,fkhe->fhqk", queries, key_rows, preferred_element_type=jnp.float32)
        * scaling
    )
    return jnp.where(visible[:, None, None, :], scores, -1e30)


def share_sums(former, latter):
    row_sums = (
        lax.psum_scatter(former, "wide", scatter_dimension=0, tiled=True),
        lax.psum_scatter(latter, "wide", scatter_dimension=0, tiled=True),
    )
    return (
        lax.psum_scatter(row_sums[0], "narrow", scatter_dimension=1, tiled=True),
        lax.psum_scatter(row_sums[1], "narrow", scatter_dimension=1, tiled=True),
    )


def local(
    tokens,
    land_mask,
    cotangent,
    qkv_weight,
    query_bias,
    value_bias,
    proj_weight,
    proj_bias,
    up_weight,
    up_bias,
    down_weight,
    down_bias,
    norm1_gain,
    norm1_shift,
    norm2_gain,
    norm2_shift,
):
    field_count, length, model_width = tokens.shape
    head_count = HEADS
    head_width = model_width // head_count
    scaling = head_width ** (-0.5)
    visible = land_mask > 0
    split_shape = (field_count, length, head_count, head_width)
    source = tokens.astype(jnp.float32)
    normed_one = layer_norm(source, norm1_gain, norm1_shift).astype(jnp.bfloat16)
    joint = jnp.einsum("fpd,de->fpe", normed_one, qkv_weight, preferred_element_type=jnp.float32)
    queries = (joint[..., :model_width] + query_bias).astype(jnp.bfloat16).reshape(split_shape)
    key_rows = joint[..., model_width : 2 * model_width].astype(jnp.bfloat16).reshape(split_shape)
    values = (joint[..., 2 * model_width :] + value_bias).astype(jnp.bfloat16).reshape(split_shape)
    scores = attend_scores(queries, key_rows, visible, scaling)
    highest = jnp.max(scores, -1, keepdims=True)
    exponent = jnp.exp(scores - highest)
    summed = jnp.sum(exponent, -1, keepdims=True)
    attention = exponent / summed
    log_total = highest + jnp.log(summed)
    attended = jnp.einsum(
        "fhqk,fkhe->fqhe",
        attention.astype(jnp.bfloat16),
        values,
        preferred_element_type=jnp.float32,
    )
    attended = attended.reshape(field_count, length, model_width).astype(jnp.bfloat16)
    middle = (
        source
        + jnp.einsum("fpd,de->fpe", attended, proj_weight, preferred_element_type=jnp.float32)
        + proj_bias
    )
    normed_two = layer_norm(middle, norm2_gain, norm2_shift).astype(jnp.bfloat16)
    hidden = (
        jnp.einsum("fpd,dn->fpn", normed_two, up_weight, preferred_element_type=jnp.float32)
        + up_bias
    )
    activated_full, gelu_pull = jax.vjp(jax.nn.gelu, hidden)
    activated = activated_full.astype(jnp.bfloat16)
    output = (
        middle
        + jnp.einsum("fpn,nd->fpd", activated, down_weight, preferred_element_type=jnp.float32)
        + down_bias
    )
    grad_out = cotangent.astype(jnp.float32)
    down_local = jnp.einsum("fpn,fpd->nd", activated, cotangent, preferred_element_type=jnp.float32)
    down_bias_local = jnp.sum(grad_out, axis=(0, 1))
    activated_grad = jnp.einsum(
        "fpd,nd->fpn", cotangent, down_weight, preferred_element_type=jnp.float32
    )
    hidden_grad = gelu_pull(activated_grad)[0].astype(jnp.bfloat16)
    up_local = jnp.einsum(
        "fpd,fpn->dn", normed_two, hidden_grad, preferred_element_type=jnp.float32
    )
    up_bias_local = jnp.sum(hidden_grad.astype(jnp.float32), axis=(0, 1))
    feed_sums = share_sums(up_local, down_local)
    normed_two_grad = jnp.einsum(
        "fpn,dn->fpd", hidden_grad, up_weight, preferred_element_type=jnp.float32
    )
    unused_two, norm_two_pull = jax.vjp(layer_norm, middle, norm2_gain, norm2_shift)
    middle_part, gain_two_local, shift_two_local = norm_two_pull(normed_two_grad)
    middle_grad = grad_out + middle_part
    middle_low = middle_grad.astype(jnp.bfloat16)
    proj_local = jnp.einsum("fpd,fpe->de", attended, middle_low, preferred_element_type=jnp.float32)
    proj_bias_local = jnp.sum(middle_low.astype(jnp.float32), axis=(0, 1))
    attended_grad = jnp.einsum(
        "fpe,de->fpd", middle_low, proj_weight, preferred_element_type=jnp.float32
    )
    attended_grad = attended_grad.astype(jnp.bfloat16).reshape(split_shape)
    scores = attend_scores(queries, key_rows, visible, scaling)
    attention = jnp.exp(scores - log_total)
    values_grad = jnp.einsum(
        "fhqk,fqhe->fkhe",
        attention.astype(jnp.bfloat16),
        attended_grad,
        preferred_element_type=jnp.float32,
    )
    attention_grad = jnp.einsum(
        "fqhe,fkhe->fhqk", attended_grad, values, preferred_element_type=jnp.float32
    )
    inner_sum = jnp.sum(attention * attention_grad, -1, keepdims=True)
    scores_grad = (attention * (attention_grad - inner_sum)).astype(jnp.bfloat16)
    queries_grad = (
        jnp.einsum("fhqk,fkhe->fqhe", scores_grad, key_rows, preferred_element_type=jnp.float32)
        * scaling
    )
    keys_grad = (
        jnp.einsum("fhqk,fqhe->fkhe", scores_grad, queries, preferred_element_type=jnp.float32)
        * scaling
    )
    flat_shape = (field_count, length, model_width)
    joint_grad = jnp.concatenate(
        [
            queries_grad.reshape(flat_shape),
            keys_grad.reshape(flat_shape),
            values_grad.reshape(flat_shape),
        ],
        -1,
    ).astype(jnp.bfloat16)
    qkv_local = jnp.einsum(
        "fpd,fpe->de", normed_one, joint_grad, preferred_element_type=jnp.float32
    )
    joint_sums = jnp.sum(joint_grad.astype(jnp.float32), axis=(0, 1))
    query_bias_local = joint_sums[:model_width]
    value_bias_local = joint_sums[2 * model_width :]
    attention_sums = share_sums(qkv_local, proj_local)
    normed_one_grad = jnp.einsum(
        "fpe,de->fpd", joint_grad, qkv_weight, preferred_element_type=jnp.float32
    )
    unused_one, norm_one_pull = jax.vjp(layer_norm, source, norm1_gain, norm1_shift)
    source_part, gain_one_local, shift_one_local = norm_one_pull(normed_one_grad)
    tokens_grad = middle_grad + source_part
    vectors = lax.psum(
        (
            query_bias_local,
            value_bias_local,
            proj_bias_local,
            up_bias_local,
            down_bias_local,
            gain_one_local,
            shift_one_local,
            gain_two_local,
            shift_two_local,
        ),
        ("wide", "narrow"),
    )
    return (
        output.astype(jnp.bfloat16),
        tokens_grad,
        attention_sums[0],
        vectors[0],
        vectors[1],
        attention_sums[1],
        vectors[2],
        feed_sums[0],
        vectors[3],
        feed_sums[1],
        vectors[4],
        vectors[5],
        vectors[6],
        vectors[7],
        vectors[8],
    )


def solution(mesh):
    wide, narrow = mesh.shape["wide"], mesh.shape["narrow"]
    placed = (
        P(("wide", "narrow"), None, None),
        P(("wide", "narrow"), None),
        P(("wide", "narrow"), None, None),
        P(),
        P(),
        P(),
        P(),
        P(),
        P(),
        P(),
        P(),
        P(),
        P(),
        P(),
        P(),
        P(),
    )
    fused = (wide, narrow) == (16, 2)

    def layer(*args):
        return local_fused(wide, narrow, *args) if fused else local(*args)

    return jax.shard_map(
        layer,
        mesh=mesh,
        in_specs=placed,
        out_specs=(
            P(("wide", "narrow"), None, None),
            P(("wide", "narrow"), None, None),
            P("wide", "narrow"),
            P(),
            P(),
            P("wide", "narrow"),
            P(),
            P("wide", "narrow"),
            P(),
            P("wide", "narrow"),
            P(),
            P(),
            P(),
            P(),
            P(),
        ),
        check_vma=False,
    )
```

```python
import jax
import jax.numpy as jnp
from jax import lax
from jax.experimental import pallas as pl
from jax.experimental.pallas import tpu as pltpu
from jax.sharding import PartitionSpec as P

HEADS = 12
F32 = jnp.float32
BF16 = jnp.bfloat16
SLOTS = 6
LAGS = (0, 2, 4, 6)
LEAD = 3
FIRST = 9


def dot(a, b):
    return lax.dot_general(a, b, (((1,), (0,)), ((), ())), preferred_element_type=F32)


def dot_nt(a, b):
    return lax.dot_general(a, b, (((1,), (1,)), ((), ())), preferred_element_type=F32)


def dot_tn(a, b):
    return lax.dot_general(a, b, (((0,), (0,)), ((), ())), preferred_element_type=F32)


def standardise(rows):
    centred = rows - jnp.mean(rows, -1, keepdims=True)
    scale = lax.rsqrt(jnp.mean(centred * centred, -1, keepdims=True) + 1e-06)
    return centred * scale, scale


def norm_back(unit_rows, scale, pulled):
    return scale * (
        pulled
        - jnp.mean(pulled, -1, keepdims=True)
        - unit_rows * jnp.mean(pulled * unit_rows, -1, keepdims=True)
    )


def column_sums(rows):
    return jnp.sum(rows, axis=0, keepdims=True)


def layer_kernel(wide, narrow, fields, patches, *refs):
    (
        tokens_in, cotangent_in, qkv_in, proj_in, up_in, down_in, land_in,
    ) = refs[:7]
    vectors_in, refs = refs[7:16], refs[16:]
    (
        output_out, tokens_out, qkv_out, proj_out, up_out, down_out, vec_out,
        tok, cot, n1, qkv, att, mid, n2, act_t, acts, hgrs, acc, ngr, left, w_a, w_b, w_p, qkv_bias, flat,
        keep, core_in, up_sums, up_sum, down_sum, proj_sum, qkv_sum, in_0, in_1, in_2, in_3, vec, vec_in,
        load_sem, core_send, core_recv, core_free, stage_send, stage_recv, final_sem,
        vec_send, vec_recv, store_sem, land,
    ) = refs[:-9]
    vectors_held = refs[-9:]
    (
        query_bias, value_bias, proj_bias, up_bias, down_bias,
        gain_one, shift_one, gain_two, shift_two,
    ) = vectors_held
    model = tok.shape[1]
    hidden_width = w_a.shape[1]
    stage_in = (in_0, in_1, in_2, in_3)
    act, hgr = acts.at[0], hgrs.at[0]
    at_wide = lax.axis_index("wide")
    at_narrow = lax.axis_index("narrow")
    width = model // narrow
    block_rows = model // wide
    group_rows = block_rows // 3
    chunk = width
    parts = 36

    def my_bit(axis, level):
        index = at_wide if axis == "wide" else at_narrow
        return lax.rem(lax.div(index, 1 << level), 2)

    def partner(axis, level):
        shift = (1 << level) * (1 - 2 * my_bit(axis, level))
        if axis == "wide":
            return (at_wide + shift, at_narrow)
        return (at_wide, at_narrow + shift)

    wide_bits = [("wide", i) for i in range(1, wide.bit_length() - 1)]
    narrow_bits = [("narrow", i) for i in range(narrow.bit_length() - 1)]
    all_bits = [("wide", 0)] + wide_bits + narrow_bits
    stages = len(wide_bits) + len(narrow_bits)
    blocks = 1 << stages
    core = my_bit("wide", 0)
    mine = {bit: my_bit(*bit) for bit in all_bits}
    to = {bit: partner(*bit) for bit in all_bits}

    def order(part, group):
        if group == 0:
            return narrow_bits + wide_bits
        if group == 1:
            return wide_bits[:1] + narrow_bits + wide_bits[1:]
        if part % 2 == 0:
            return wide_bits[1:2] + narrow_bits + wide_bits[:1] + wide_bits[2:]
        return wide_bits[1:2] + wide_bits[:1] + narrow_bits + wide_bits[2:]

    def place(part, group, row_block, column_block):
        found = 0
        for axis, level in order(part, group):
            index = row_block if axis == "wide" else column_block
            found = 2 * found + ((index >> level) & 1)
        return found

    barrier = pltpu.get_barrier_semaphore()
    for bit in all_bits:
        pl.semaphore_signal(
            barrier, inc=1, device_id=to[bit], device_id_type=pl.DeviceIdType.MESH
        )

    def remote(src, dst, send, recv, bit):
        return pltpu.make_async_remote_copy(
            src_ref=src, dst_ref=dst, send_sem=send, recv_sem=recv,
            device_id=to[bit], device_id_type=pl.DeviceIdType.MESH,
        )

    def kept_slot(part):
        return part % (3 * SLOTS)

    def sent_slot(part):
        return 3 * SLOTS + part % 6

    def core_copy(part):
        slot = part % 6
        return remote(
            keep.at[sent_slot(part)], core_in.at[slot],
            core_send.at[slot], core_recv.at[slot], ("wide", 0),
        )

    def core_start(part):
        if part >= 6:
            pl.semaphore_wait(core_free, 1)
        core_copy(part).start()

    def span(part, group, stage):
        half = blocks >> (stage + 1)
        sequence = order(part, group)
        base = 0
        for earlier in range(stage):
            base = base + mine[sequence[earlier]] * (blocks >> (earlier + 1))
        bit = sequence[stage]
        return half, base + mine[bit] * half, base + (1 - mine[bit]) * half, bit

    gaps = [LEAD] + [LAGS[i] - LAGS[i - 1] for i in range(1, 4)]
    cycle = [2 * (gap + gap % 2) for gap in gaps]

    def stage_copy(part, group, stage):
        half, own, other, bit = span(part, group, stage)
        sent = sum(gaps[:stage]) + part % gaps[stage]
        held = sum(cycle[:stage]) + part % cycle[stage]
        return remote(
            keep.at[kept_slot(part), group, pl.ds(other, half)],
            stage_in[stage].at[part % cycle[stage], group],
            stage_send.at[sent, group],
            stage_recv.at[held, group],
            bit,
        )

    def core_end(part):
        slot = part % 6
        core_copy(part).wait()
        for group in range(3):
            keep[kept_slot(part), group] += core_in[slot, group]
            stage_copy(part, group, 0).start()
        if part + 6 < parts:
            pl.semaphore_signal(
                core_free, inc=1, device_id=to[("wide", 0)],
                device_id_type=pl.DeviceIdType.MESH,
            )

    def result_place(part, group):
        unit, row = part // 3, (part % 3) * group_rows
        if unit < 4:
            return up_sum, row, unit * width + group * 128
        if unit < 8:
            return down_sum, (unit - 4) * block_rows + row, group * 128
        if unit == 8:
            return proj_sum, row, group * 128
        return qkv_sum, row, (unit - 9) * width + group * 128

    def stage_end(part, stage):
        for group in range(3):
            stage_copy(part, group, stage).wait()
            half, own, other, bit = span(part, group, stage)
            slot, came = kept_slot(part), stage_in[stage].at[part % cycle[stage], group]
            if stage + 1 < stages:
                keep[slot, group, pl.ds(own, half)] += came[...]
                stage_copy(part, group, stage + 1).start()
            else:
                ref, row, column = result_place(part, group)
                ref[row : row + group_rows, column : column + 128] = (
                    keep[slot, group, own] + came[0]
                )

    result_copies = [
        pltpu.make_async_copy(src, dst, final_sem.at[number])
        for number, (src, dst) in enumerate(
            ((up_sum, up_out), (down_sum, down_out), (proj_sum, proj_out), (qkv_sum, qkv_out))
        )
    ]
    last_part = {11: 0, 23: 1, 26: 2, 35: 3}

    def tick(number, between=()):
        for stage in reversed(range(stages)):
            if stage == 1:
                for step in between:
                    step()
            part = number - LAGS[stage]
            if 0 <= part < parts:
                stage_end(part, stage)
                if stage + 1 == stages and part in last_part:
                    result_copies[last_part[part]].start()

    def make_unit(unit, lhs_half, rhs):
        half_blocks = wide // 2

        def one(half, carry):
            product = dot(lhs_half(half), rhs())
            for third in range(3):
                part = 3 * unit + third
                kept, sent = kept_slot(part), sent_slot(part)
                index = [kept + core * (sent - kept), sent + core * (kept - sent)]
                for row_block in range(half_blocks):
                    top = row_block * block_rows + third * group_rows
                    for column_block in range(narrow):
                        for group in range(3):
                            first = place(part, group, row_block, column_block)
                            step = place(part, group, half_blocks, 0)
                            side = column_block * width + group * 128
                            keep[index[row_block % 2], group, first + half * step] = product[
                                top : top + group_rows, side : side + 128
                            ]
            return carry

        lax.fori_loop(0, 2, one, 0)
        for third in range(3):
            core_start(3 * unit + third)

    def make_first_unit(rhs):
        for part in range(3):
            lhs = jnp.concatenate(
                [
                    left[pl.ds(row_block * block_rows + part * group_rows, group_rows), :]
                    for row_block in range(wide)
                ],
                0,
            )
            product = dot(lhs, rhs())
            kept, sent = kept_slot(part), sent_slot(part)
            index = [kept + core * (sent - kept), sent + core * (kept - sent)]
            for row_block in range(wide):
                top = row_block * group_rows
                for column_block in range(narrow):
                    for group in range(3):
                        where = place(part, group, row_block, column_block)
                        side = column_block * width + group * 128
                        keep[index[row_block % 2], group, where] = product[
                            top : top + group_rows, side : side + 128
                        ]
            core_start(part)

    def row_of(vector):
        return vector[...].reshape(1, vector.shape[0])

    def load(src, dst, number):
        copy = pltpu.make_async_copy(src, dst, load_sem.at[number])
        copy.start()
        return copy

    tok_load = load(tokens_in, tok, 0)
    small_loads = [load(land_in, land, 6)] + [
        load(src, dst, 7 + number)
        for number, (src, dst) in enumerate(zip(vectors_in, vectors_held))
    ]
    thirds = [pl.ds(number * model, model) for number in range(3)]
    qkv_loads = [
        load(qkv_in.at[:, columns], w_a.at[:, columns], number)
        for columns, number in zip(thirds, (1, 16, 17))
    ]
    vec[...] = jnp.zeros_like(vec)
    acc[...] = jnp.zeros_like(acc)
    ngr[...] = jnp.zeros_like(ngr)
    for small in small_loads:
        small.wait()
    qkv_bias[:, 0:model] = row_of(query_bias)
    qkv_bias[:, model : 2 * model] = jnp.zeros((1, model), F32)
    qkv_bias[:, 2 * model :] = row_of(value_bias)
    for number, vector in enumerate(
        (proj_bias, down_bias, gain_one, shift_one, gain_two, shift_two)
    ):
        flat[number : number + 1, 0:model] = row_of(vector)
    flat[6:7, :] = row_of(up_bias)

    def field_rows(field):
        return pl.ds(pl.multiple_of(field * patches, patches), patches)

    def each_field(step):
        def body(field, carry):
            step(field)
            return carry

        lax.fori_loop(0, fields, body, 0)

    tok_load.wait()
    at_model = pl.ds(0, model)
    proj_row, down_row, gain_one_row, shift_one_row, gain_two_row, shift_two_row = (
        flat.at[pl.ds(number, 1), at_model] for number in range(6)
    )
    up_row = flat.at[pl.ds(6, 1), :]

    def norm_one(field):
        rows = field_rows(field)
        unit_rows, scale = standardise(tok[rows, :].astype(F32))
        n1[rows, :] = (unit_rows * gain_one_row[...] + shift_one_row[...]).astype(BF16)

    each_field(norm_one)
    later_loads = []
    for number, columns in enumerate(thirds):
        qkv_loads[number].wait()
        if number == 2:
            later_loads += [load(proj_in, w_p, 2), load(cotangent_in, cot, 3), load(down_in, w_b, 4)]
        qkv[:, columns] = (dot(n1[...], w_a[:, columns]) + qkv_bias[:, columns]).astype(BF16)
    proj_load, cot_load, down_load = later_loads
    up_load = load(up_in, w_a, 5)

    lane = lax.broadcasted_iota(jnp.int32, (1, 128), 1)
    head_masks = [(lane < 64).astype(BF16), (lane >= 64).astype(BF16)]
    lane_full = lax.broadcasted_iota(jnp.int32, (patches, 128), 1)
    pairs = model // 128

    def stack_heads(rows, factor=1.0):
        return jnp.concatenate([rows * (mask * BF16(factor)) for mask in head_masks], 0)

    def pick_heads(rows):
        return jnp.where(lane_full < 64, rows[:patches], rows[patches:])

    def soften(stacked, key_rows, visible):
        scores = [dot_nt(one, keys) for one, keys in zip(stacked, key_rows)]
        scores = [jnp.where(visible, one, -1e30) for one in scores]
        tops = [jnp.max(one, -1, keepdims=True) for one in scores]
        exponents = [jnp.exp(one - top) for one, top in zip(scores, tops)]
        shares = [1.0 / jnp.sum(one, -1, keepdims=True) for one in exponents]
        return [one * share for one, share in zip(exponents, shares)]

    def pair_columns(pair):
        return [pl.ds(part * model + pair * 128, 128) for part in range(3)]

    def visible_of(field):
        return jnp.broadcast_to(land[pl.ds(field, 1), :], (2 * patches, patches)) > 0

    def attend(field):
        rows = field_rows(field)
        visible = visible_of(field)
        at = [pair_columns(pair) for pair in range(pairs)]
        stacked = [stack_heads(qkv[rows, at_q], 0.125) for at_q, at_k, at_v in at]
        attention = soften(stacked, [qkv[rows, at_k] for at_q, at_k, at_v in at], visible)
        both = [
            dot(one.astype(BF16), qkv[rows, at_v])
            for one, (at_q, at_k, at_v) in zip(attention, at)
        ]
        for pair in range(pairs):
            att[rows, pl.ds(pair * 128, 128)] = pick_heads(both[pair]).astype(BF16)

    each_field(attend)
    proj_load.wait()

    def residual(tile, carry):
        columns = pl.ds(pl.multiple_of(tile * 256, 256), 256)
        mid[:, columns] = (
            tok[:, columns].astype(F32) + dot(att[...], w_p[:, columns]) + proj_row[:, columns]
        )
        return carry

    lax.fori_loop(0, model // 256, residual, 0)

    def norm_two(field):
        rows = field_rows(field)
        unit_rows, scale = standardise(mid[rows, :])
        normed = (unit_rows * gain_two_row[...] + shift_two_row[...]).astype(BF16)
        n2[rows, :] = normed
        left[:, rows] = normed.T

    each_field(norm_two)

    root = 0.7978845608028654

    def hidden_columns(part, column_block):
        first = column_block * (hidden_width // narrow) + part * chunk
        return first if isinstance(first, int) else pl.multiple_of(first, chunk)

    def block_start(column_block):
        first = column_block * chunk
        return first if isinstance(first, int) else pl.multiple_of(first, chunk)

    def each_block(step):
        def body(column_block, carry):
            step(column_block)
            return carry

        lax.fori_loop(0, narrow, body, 0)

    def feed(part, step=each_block):
        def one(column_block):
            first = hidden_columns(part, column_block)
            columns = pl.ds(first, chunk)
            here = pl.ds(block_start(column_block), chunk)
            hidden = dot(n2[...], w_a[:, columns]) + up_row[:, columns]
            pulled = dot_nt(cot[...], w_b[columns, :])
            square = hidden * hidden
            bent = jnp.tanh(hidden * (root + (root * 0.044715) * square))
            cdf = 0.5 + 0.5 * bent
            activated = (hidden * cdf).astype(BF16)
            slope = cdf + (hidden * (0.5 - 0.5 * bent * bent)) * (
                root + (3 * root * 0.044715) * square
            )
            grad = (pulled * slope).astype(BF16)
            acts[part, :, here] = activated
            hgrs[part, :, here] = grad
            act_t[columns, :] = activated.T
            up_sums[:, columns] = column_sums(grad.astype(F32))

        step(one)

    def feed_sums(part):
        def one(column_block):
            columns = pl.ds(hidden_columns(part, column_block), chunk)
            here = pl.ds(pl.multiple_of(column_block * chunk, chunk), chunk)
            acc[...] += dot(acts[part, :, here], w_b[columns, :])
            ngr[...] += dot_nt(hgrs[part, :, here], w_a[:, columns])

        each_block(one)

    def left_half(half):
        return left[pl.ds(pl.multiple_of(half * (model // 2), model // 2), model // 2), :]

    def up_unit(part):
        make_unit(part, left_half, lambda: hgrs[part])

    def down_unit(part):
        def rows(half):
            first = half * (hidden_width // 2) + part * block_rows
            return jnp.concatenate(
                [
                    act_t[
                        pl.ds(pl.multiple_of(first + block * 4 * block_rows, 16), block_rows), :
                    ]
                    for block in range(wide // 2)
                ],
                0,
            )

        make_unit(4 + part, rows, lambda: cot[...])

    def store_output(field):
        rows = field_rows(field)
        act[rows, :] = (mid[rows, :] + acc[rows, :] + down_row[...]).astype(BF16)

    output_copy = pltpu.make_async_copy(act, output_out, store_sem.at[0])
    tokens_copy = pltpu.make_async_copy(acc, tokens_out, store_sem.at[1])

    def add_sums(row, columns, rows):
        vec[pl.ds(row, 1), columns] += column_sums(rows)

    everything = pl.ds(0, model)

    def middle_back(field):
        rows = field_rows(field)
        unit_rows, scale = standardise(mid[rows, :])
        grads = ngr[rows, :]
        top = cot[rows, :].astype(F32)
        add_sums(7, everything, top)
        add_sums(10, everything, grads * unit_rows)
        add_sums(11, everything, grads)
        total = top + norm_back(unit_rows, scale, grads * gain_two_row[...])
        acc[rows, :] = total
        low = total.astype(BF16)
        hgr[rows, :] = low
        add_sums(2, everything, low.astype(F32))

    def attend_back(field, first_pair, last_pair):
        rows = field_rows(field)
        visible = visible_of(field)

        some = range(first_pair, last_pair)
        at = [pair_columns(pair) for pair in some]
        here = [pl.ds(pair * 128, 128) for pair in some]
        stacked = [stack_heads(qkv[rows, at_q], 0.125) for at_q, at_k, at_v in at]
        pulled = [stack_heads(act[rows, columns]) for columns in here]
        attention = soften(stacked, [qkv[rows, at_k] for at_q, at_k, at_v in at], visible)
        inner = [dot_nt(one, qkv[rows, at_v]) for one, (at_q, at_k, at_v) in zip(pulled, at)]
        inner = [
            one - jnp.sum(share * one, -1, keepdims=True) for share, one in zip(attention, inner)
        ]
        scores_grad = [(share * one).astype(BF16) for share, one in zip(attention, inner)]
        queries_grad = [
            (pick_heads(dot(one, qkv[rows, at_k])) * 0.125).astype(BF16)
            for one, (at_q, at_k, at_v) in zip(scores_grad, at)
        ]
        keys_grad = [dot_tn(one, rest).astype(BF16) for one, rest in zip(scores_grad, stacked)]
        values_grad = [
            dot_tn(one.astype(BF16), rest).astype(BF16) for one, rest in zip(attention, pulled)
        ]
        for number, (at_q, at_k, at_v) in enumerate(at):
            qkv[rows, at_q] = queries_grad[number]
            qkv[rows, at_k] = keys_grad[number]
            qkv[rows, at_v] = values_grad[number]
            add_sums(0, here[number], queries_grad[number].astype(F32))
            add_sums(1, here[number], values_grad[number].astype(F32))

    def turn(source):
        for field in range(fields):
            left[:, field_rows(field)] = source[field_rows(field), :].T

    def proj_unit():
        turn(att)
        make_unit(8, left_half, lambda: hgr[...])

    def qkv_unit(part):
        stride = 3 * model // narrow
        make_unit(
            9 + part,
            left_half,
            lambda: jnp.concatenate(
                [
                    qkv[:, pl.ds(block * stride + part * width, width)]
                    for block in range(narrow)
                ],
                1,
            ),
        )

    def source_back(field):
        rows = field_rows(field)
        unit_rows, scale = standardise(tok[rows, :].astype(F32))
        grads = ngr[rows, :]
        add_sums(8, everything, grads * unit_rows)
        add_sums(9, everything, grads)
        acc[rows, :] += norm_back(unit_rows, scale, grads * gain_one_row[...])

    def vec_copy(number):
        return remote(
            vec, vec_in.at[number], vec_send.at[number], vec_recv.at[number], all_bits[number]
        )

    def vec_end(number):
        vec_copy(number).wait()
        vec[...] += vec_in[number]
        if number + 1 < len(all_bits):
            vec_copy(number + 1).start()

    def make_attended_grad():
        output_copy.wait()
        act[...] = dot_nt(hgr[...], w_p[...]).astype(BF16)

    def finish_output():
        for number in range(hidden_width // model):
            vec[3 + number : 4 + number, :] = up_sums[:, number * model : (number + 1) * model]
        each_field(store_output)
        output_copy.start()

    qkv_again = pltpu.make_async_copy(qkv_in, w_a.at[:, pl.ds(0, 3 * model)], load_sem.at[1])

    def make_normed_grad(half):
        columns = pl.ds(half * (model // 2), model // 2)
        if half == 0:
            qkv_again.wait()
        ngr[:, columns] = dot_nt(qkv[...], w_a[columns, pl.ds(0, 3 * model)])

    def finish_tokens():
        each_field(source_back)
        tokens_copy.start()
        vec_copy(0).start()

    def some(step, *values):
        return lambda: step(*values)

    halves = [(0, pairs // 2), (pairs // 2, pairs)]
    backs = [
        some(attend_back, field, *half) for field in range(fields) for half in halves
    ]
    backs_at = {13: 1, 15: 1, 16: 1, 18: 1, 19: 1, 21: 1, 22: 2}
    work = {
        0: [some(feed, 2)],
        1: [some(feed_sums, 0)],
        2: [some(up_unit, 2)],
        3: [some(feed, 3)],
        5: [some(up_unit, 3)],
        6: [some(feed_sums, 1)],
        7: [some(feed_sums, 2)],
        8: [some(down_unit, 0)],
        9: [some(feed_sums, 3), qkv_again.start],
        10: [finish_output],
        11: [some(down_unit, 1)],
        12: [some(each_field, middle_back), make_attended_grad],
        14: [some(down_unit, 2)],
        17: [some(down_unit, 3)],
        20: [proj_unit],
        23: [some(turn, n1), some(qkv_unit, 0)],
        24: [some(make_normed_grad, 0)],
        25: [some(make_normed_grad, 1)],
        26: [some(qkv_unit, 1)],
        27: [finish_tokens],
        29: [some(qkv_unit, 2)],
    }
    for number, count in backs_at.items():
        work[number] = [backs.pop(0) for _ in range(count)]
    for number in range(len(all_bits)):
        work.setdefault(30 + 2 * number, []).append(some(vec_end, number))

    up_load.wait()
    down_load.wait()
    cot_load.wait()
    feed(0, lambda one: [one(column_block) for column_block in range(narrow)])
    pl.semaphore_wait(barrier, len(all_bits))
    make_first_unit(lambda: hgrs[0])
    feed(1, lambda one: one(0))
    core_end(0)
    core_end(1)
    for column_block in range(1, narrow):
        feed(1, lambda one: one(column_block))
    core_end(2)
    up_unit(1)
    vec_store = pltpu.make_async_copy(vec, vec_out, store_sem.at[2])
    for number in range(parts + LAGS[-1]):
        steps = work.get(number, [])
        for step in steps[:FIRST]:
            step()
        tick(number, steps[FIRST:])
        if 0 <= number + LEAD < parts:
            core_end(number + LEAD)
        if number == 30 + 2 * (len(all_bits) - 1):
            vec_store.start()
    for copy in result_copies:
        copy.wait()
    tokens_copy.wait()
    vec_store.wait()


def place_results(*refs):
    arrays, vec_in, placed, vectors_out = refs[:6], refs[6], refs[7:13], refs[13:22]
    in_sem, out_sem, vec_sem, vec, *held = refs[22:]
    vectors, held = held[:9], held[9:]

    def pieces(ref):
        count = 4 if ref.shape[0] % 64 == 0 and ref.shape[0] >= 512 else 1
        size = ref.shape[0] // count
        return [pl.ds(number * size, size) for number in range(count)]

    moves = [
        (src.at[rows], mid.at[rows], dst.at[rows])
        for src, mid, dst in zip(arrays, held, placed)
        for rows in pieces(src)
    ]
    vec_copy = pltpu.make_async_copy(vec_in, vec, vec_sem.at[9])
    vec_copy.start()
    inward, outward = [], []
    for number, (src, mid, dst) in enumerate(moves):
        inward.append(pltpu.make_async_copy(src, mid, in_sem.at[number]))
        outward.append(pltpu.make_async_copy(mid, dst, out_sem.at[number]))
        inward[-1].start()
    vec_copy.wait()
    row = 0
    vec_outward = []
    for number, (vector, vector_out) in enumerate(zip(vectors, vectors_out)):
        model = vec.shape[1]
        for part in range(vector.shape[0] // model):
            vector[pl.ds(part * model, model)] = vec[row, :]
            row += 1
        vec_outward.append(pltpu.make_async_copy(vector, vector_out, vec_sem.at[number]))
        vec_outward[-1].start()
    for before, after in zip(inward, outward):
        before.wait()
        after.start()
    for copy in outward + vec_outward:
        copy.wait()


def local_fused(wide, narrow, *args):
    (
        tokens, land_mask, cotangent, qkv_weight, query_bias, value_bias, proj_weight, proj_bias,
        up_weight, up_bias, down_weight, down_bias, norm1_gain, norm1_shift, norm2_gain, norm2_shift,
    ) = args
    fields, patches, model = tokens.shape
    rows = fields * patches
    hidden_width = up_weight.shape[1]
    width, block_rows = model // narrow, model // wide
    bits = (wide * narrow).bit_length() - 1
    blocks = wide * narrow // 2
    group_rows = block_rows // 3
    gaps = [LEAD] + [LAGS[i] - LAGS[i - 1] for i in range(1, 4)]
    cycle = [2 * (gap + gap % 2) for gap in gaps]
    anywhere = pl.BlockSpec(memory_space=pl.ANY)

    def vmem(shape, dtype=F32):
        return pltpu.VMEM(shape, dtype)

    dma = pltpu.SemaphoreType.DMA
    vectors = [model] * 3 + [hidden_width] + [model] * 5
    results = pl.pallas_call(
        lambda *refs: layer_kernel(wide, narrow, fields, patches, *refs),
        out_shape=[
            jax.ShapeDtypeStruct((rows, model), BF16),
            jax.ShapeDtypeStruct((rows, model), F32),
            jax.ShapeDtypeStruct((block_rows, 3 * width), F32),
            jax.ShapeDtypeStruct((block_rows, width), F32),
            jax.ShapeDtypeStruct((block_rows, 4 * width), F32),
            jax.ShapeDtypeStruct((4 * block_rows, width), F32),
            jax.ShapeDtypeStruct((16, model), F32),
        ],
        in_specs=[anywhere] * 16,
        out_specs=[anywhere] * 7,
        scratch_shapes=[
            vmem((rows, model), BF16),
            vmem((rows, model), BF16),
            vmem((rows, model), BF16),
            vmem((rows, 3 * model), BF16),
            vmem((rows, model), BF16),
            vmem((rows, model)),
            vmem((rows, model), BF16),
            vmem((hidden_width, rows), BF16),
            vmem((4, rows, model), BF16),
            vmem((4, rows, model), BF16),
            vmem((rows, model)),
            vmem((rows, model)),
            vmem((model, rows), BF16),
            vmem((model, hidden_width), BF16),
            vmem((hidden_width, model), BF16),
            vmem((model, model), BF16),
            vmem((1, 3 * model)),
            vmem((8, hidden_width)),
            vmem((3 * SLOTS + 6, 3, blocks, group_rows, 128)),
            vmem((6, 3, blocks, group_rows, 128)),
            vmem((1, hidden_width)),
            vmem((block_rows, 4 * width)),
            vmem((4 * block_rows, width)),
            vmem((block_rows, width)),
            vmem((block_rows, 3 * width)),
            *[vmem((cycle[s], 3, blocks >> (s + 1), group_rows, 128)) for s in range(4)],
            vmem((16, model)),
            vmem((bits, 16, model)),
            dma((18,)),
            dma((6,)),
            dma((6,)),
            pltpu.SemaphoreType.REGULAR,
            dma((sum(gaps), 3)),
            dma((sum(cycle), 3)),
            dma((4,)),
            dma((bits,)),
            dma((bits,)),
            dma((3,)),
            vmem((fields, patches), jnp.int32),
            *[vmem((size,)) for size in vectors],
        ],
        compiler_params=pltpu.CompilerParams(
            collective_id=0, has_side_effects=True, vmem_limit_bytes=63 << 20
        ),
        name="encoder_layer",
    )(
        tokens.reshape(rows, model),
        cotangent.reshape(rows, model),
        qkv_weight,
        proj_weight,
        up_weight,
        down_weight,
        land_mask,
        query_bias,
        value_bias,
        proj_bias,
        up_bias,
        down_bias,
        norm1_gain,
        norm1_shift,
        norm2_gain,
        norm2_shift,
    )
    placed = pl.pallas_call(
        place_results,
        out_shape=[jax.ShapeDtypeStruct(array.shape, array.dtype) for array in results[:6]]
        + [jax.ShapeDtypeStruct((size,), F32) for size in vectors],
        in_specs=[anywhere] * 7,
        out_specs=[anywhere] * 15,
        scratch_shapes=[dma((12,)), dma((12,)), dma((10,)), vmem((16, model))]
        + [vmem((size,)) for size in vectors]
        + [vmem(array.shape, array.dtype) for array in results[:6]],
        name="place_results",
    )(*results)
    output, tokens_grad, qkv_grad, proj_grad, up_grad, down_grad = placed[:6]
    (
        query_grad, value_grad, proj_bias_grad, up_bias_grad, down_bias_grad,
        gain_one_grad, shift_one_grad, gain_two_grad, shift_two_grad,
    ) = placed[6:]
    return (
        output.reshape(tokens.shape),
        tokens_grad.reshape(tokens.shape),
        qkv_grad,
        query_grad,
        value_grad,
        proj_grad,
        proj_bias_grad,
        up_grad,
        up_bias_grad,
        down_grad,
        down_bias_grad,
        gain_one_grad,
        shift_one_grad,
        gain_two_grad,
        shift_two_grad,
    )


def layer_norm(inputs, norm_gain, norm_shift):
    average = jnp.mean(inputs, -1, keepdims=True)
    centred = inputs - average
    variance = jnp.mean(centred * centred, -1, keepdims=True)
    return centred * lax.rsqrt(variance + 1e-06) * norm_gain + norm_shift


def attend_scores(queries, key_rows, visible, scaling):
    scores = (
        jnp.einsum("fqhe,fkhe->fhqk", queries, key_rows, preferred_element_type=jnp.float32)
        * scaling
    )
    return jnp.where(visible[:, None, None, :], scores, -1e30)


def share_sums(former, latter):
    row_sums = (
        lax.psum_scatter(former, "wide", scatter_dimension=0, tiled=True),
        lax.psum_scatter(latter, "wide", scatter_dimension=0, tiled=True),
    )
    return (
        lax.psum_scatter(row_sums[0], "narrow", scatter_dimension=1, tiled=True),
        lax.psum_scatter(row_sums[1], "narrow", scatter_dimension=1, tiled=True),
    )


def local(
    tokens,
    land_mask,
    cotangent,
    qkv_weight,
    query_bias,
    value_bias,
    proj_weight,
    proj_bias,
    up_weight,
    up_bias,
    down_weight,
    down_bias,
    norm1_gain,
    norm1_shift,
    norm2_gain,
    norm2_shift,
):
    field_count, length, model_width = tokens.shape
    head_count = HEADS
    head_width = model_width // head_count
    scaling = head_width ** (-0.5)
    visible = land_mask > 0
    split_shape = (field_count, length, head_count, head_width)
    source = tokens.astype(jnp.float32)
    normed_one = layer_norm(source, norm1_gain, norm1_shift).astype(jnp.bfloat16)
    joint = jnp.einsum("fpd,de->fpe", normed_one, qkv_weight, preferred_element_type=jnp.float32)
    queries = (joint[..., :model_width] + query_bias).astype(jnp.bfloat16).reshape(split_shape)
    key_rows = joint[..., model_width : 2 * model_width].astype(jnp.bfloat16).reshape(split_shape)
    values = (joint[..., 2 * model_width :] + value_bias).astype(jnp.bfloat16).reshape(split_shape)
    scores = attend_scores(queries, key_rows, visible, scaling)
    highest = jnp.max(scores, -1, keepdims=True)
    exponent = jnp.exp(scores - highest)
    summed = jnp.sum(exponent, -1, keepdims=True)
    attention = exponent / summed
    log_total = highest + jnp.log(summed)
    attended = jnp.einsum(
        "fhqk,fkhe->fqhe",
        attention.astype(jnp.bfloat16),
        values,
        preferred_element_type=jnp.float32,
    )
    attended = attended.reshape(field_count, length, model_width).astype(jnp.bfloat16)
    middle = (
        source
        + jnp.einsum("fpd,de->fpe", attended, proj_weight, preferred_element_type=jnp.float32)
        + proj_bias
    )
    normed_two = layer_norm(middle, norm2_gain, norm2_shift).astype(jnp.bfloat16)
    hidden = (
        jnp.einsum("fpd,dn->fpn", normed_two, up_weight, preferred_element_type=jnp.float32)
        + up_bias
    )
    activated_full, gelu_pull = jax.vjp(jax.nn.gelu, hidden)
    activated = activated_full.astype(jnp.bfloat16)
    output = (
        middle
        + jnp.einsum("fpn,nd->fpd", activated, down_weight, preferred_element_type=jnp.float32)
        + down_bias
    )
    grad_out = cotangent.astype(jnp.float32)
    down_local = jnp.einsum("fpn,fpd->nd", activated, cotangent, preferred_element_type=jnp.float32)
    down_bias_local = jnp.sum(grad_out, axis=(0, 1))
    activated_grad = jnp.einsum(
        "fpd,nd->fpn", cotangent, down_weight, preferred_element_type=jnp.float32
    )
    hidden_grad = gelu_pull(activated_grad)[0].astype(jnp.bfloat16)
    up_local = jnp.einsum(
        "fpd,fpn->dn", normed_two, hidden_grad, preferred_element_type=jnp.float32
    )
    up_bias_local = jnp.sum(hidden_grad.astype(jnp.float32), axis=(0, 1))
    feed_sums = share_sums(up_local, down_local)
    normed_two_grad = jnp.einsum(
        "fpn,dn->fpd", hidden_grad, up_weight, preferred_element_type=jnp.float32
    )
    unused_two, norm_two_pull = jax.vjp(layer_norm, middle, norm2_gain, norm2_shift)
    middle_part, gain_two_local, shift_two_local = norm_two_pull(normed_two_grad)
    middle_grad = grad_out + middle_part
    middle_low = middle_grad.astype(jnp.bfloat16)
    proj_local = jnp.einsum("fpd,fpe->de", attended, middle_low, preferred_element_type=jnp.float32)
    proj_bias_local = jnp.sum(middle_low.astype(jnp.float32), axis=(0, 1))
    attended_grad = jnp.einsum(
        "fpe,de->fpd", middle_low, proj_weight, preferred_element_type=jnp.float32
    )
    attended_grad = attended_grad.astype(jnp.bfloat16).reshape(split_shape)
    scores = attend_scores(queries, key_rows, visible, scaling)
    attention = jnp.exp(scores - log_total)
    values_grad = jnp.einsum(
        "fhqk,fqhe->fkhe",
        attention.astype(jnp.bfloat16),
        attended_grad,
        preferred_element_type=jnp.float32,
    )
    attention_grad = jnp.einsum(
        "fqhe,fkhe->fhqk", attended_grad, values, preferred_element_type=jnp.float32
    )
    inner_sum = jnp.sum(attention * attention_grad, -1, keepdims=True)
    scores_grad = (attention * (attention_grad - inner_sum)).astype(jnp.bfloat16)
    queries_grad = (
        jnp.einsum("fhqk,fkhe->fqhe", scores_grad, key_rows, preferred_element_type=jnp.float32)
        * scaling
    )
    keys_grad = (
        jnp.einsum("fhqk,fqhe->fkhe", scores_grad, queries, preferred_element_type=jnp.float32)
        * scaling
    )
    flat_shape = (field_count, length, model_width)
    joint_grad = jnp.concatenate(
        [
            queries_grad.reshape(flat_shape),
            keys_grad.reshape(flat_shape),
            values_grad.reshape(flat_shape),
        ],
        -1,
    ).astype(jnp.bfloat16)
    qkv_local = jnp.einsum(
        "fpd,fpe->de", normed_one, joint_grad, preferred_element_type=jnp.float32
    )
    joint_sums = jnp.sum(joint_grad.astype(jnp.float32), axis=(0, 1))
    query_bias_local = joint_sums[:model_width]
    value_bias_local = joint_sums[2 * model_width :]
    attention_sums = share_sums(qkv_local, proj_local)
    normed_one_grad = jnp.einsum(
        "fpe,de->fpd", joint_grad, qkv_weight, preferred_element_type=jnp.float32
    )
    unused_one, norm_one_pull = jax.vjp(layer_norm, source, norm1_gain, norm1_shift)
    source_part, gain_one_local, shift_one_local = norm_one_pull(normed_one_grad)
    tokens_grad = middle_grad + source_part
    vectors = lax.psum(
        (
            query_bias_local,
            value_bias_local,
            proj_bias_local,
            up_bias_local,
            down_bias_local,
            gain_one_local,
            shift_one_local,
            gain_two_local,
            shift_two_local,
        ),
        ("wide", "narrow"),
    )
    return (
        output.astype(jnp.bfloat16),
        tokens_grad,
        attention_sums[0],
        vectors[0],
        vectors[1],
        attention_sums[1],
        vectors[2],
        feed_sums[0],
        vectors[3],
        feed_sums[1],
        vectors[4],
        vectors[5],
        vectors[6],
        vectors[7],
        vectors[8],
    )


def solution(mesh):
    wide, narrow = mesh.shape["wide"], mesh.shape["narrow"]
    placed = (
        P(("wide", "narrow"), None, None),
        P(("wide", "narrow"), None),
        P(("wide", "narrow"), None, None),
        P(),
        P(),
        P(),
        P(),
        P(),
        P(),
        P(),
        P(),
        P(),
        P(),
        P(),
        P(),
        P(),
    )
    fused = (wide, narrow) == (16, 2)

    def layer(*args):
        return local_fused(wide, narrow, *args) if fused else local(*args)

    return jax.shard_map(
        layer,
        mesh=mesh,
        in_specs=placed,
        out_specs=(
            P(("wide", "narrow"), None, None),
            P(("wide", "narrow"), None, None),
            P("wide", "narrow"),
            P(),
            P(),
            P("wide", "narrow"),
            P(),
            P("wide", "narrow"),
            P(),
            P("wide", "narrow"),
            P(),
            P(),
            P(),
            P(),
            P(),
        ),
        check_vma=False,
    )
```
